128 devices in a mesh: tm: 4 (over z), col: 32 (over x, y, core).
Axes of the slice: x: 4, y: 4, z: 4, core: 2. Of those that a mesh axis runs over, the one named last changes fastest.
Arguments:
- forcing_state: float32 [4, 5, 64, 4, 8192], P('tm', None, None, None, 'col'), may hold values from -6 to 6
- model_error: float32 [4, 5, 64, 4, 8192], P('tm', None, None, None, 'col'), may hold values from 0.3 to 3
- courant: float32 [4, 4, 64, 4, 8192], P('tm', None, None, None, 'col'), may hold values from 0.2 to 0.9
- vertical_mix: float32 [5, 64, 64], replicated, may hold values from -0.75 to 0.75
- radiance_jacobian: float32 [320, 128], replicated, may hold values from -0.3125 to 0.3125
- innovation: float32 [4, 16384, 128], P('tm', 'col'), may hold values from -6 to 6
- report_error: float32 [4, 16384, 128], P('tm', 'col'), may hold values from 0.3 to 3
- report_column: int32 [4, 16384], P('tm', 'col'), may hold values from 0 to 32767, as said below
- report_slot: int32 [4, 16384], P('tm', 'col'), may hold values from 0 to 3
- report_count: int32 [4, 32, 4], P('tm', 'col'), may hold values from 32 to 128
Outputs:
- model_dual: float32 [4, 5, 64, 4, 8192], P('tm', None, None, None, 'col')
- report_dual: float32 [4, 16384, 128], P('tm', 'col')
- increment: float32 [4, 5, 64, 4, 8192], P('tm', None, None, None, 'col')
- model_residual: float32 [4, 5, 64, 4, 8192], P('tm', None, None, None, 'col')
- report_residual: float32 [4, 16384, 128], P('tm', 'col')
- increment_residual: float32 [4, 5, 64, 4, 8192], P('tm', None, None, None, 'col')
The draws below stay inside these ranges and needn't reach their ends.
Inputs may be any that keep to these rules, and one draw needn't show every extreme that they name: `report_column`: on each device and in each section, the rows name grid columns in at most 32 of one block of 256 columns (the block that one index of col holds); in every section one block receives exactly 32 rows from every device.
All inputs are finite; a program needn't handle non-finite values.
Results may differ from the reference program's by a relative error of at most 0.00013.
Values sent between devices are 32-bit elements; how exact they have to be, the bound alone decides.
A program may use at most 128 MiB of HBM per device.

```python
import math
import jax
import jax.numpy as jnp
from jax import lax

FIELDS = 5
LEVELS = 64
CHANNELS = 128
LAT_ROWS = 4
COL_DEV = 256
REPORTS_DEV = 512
INSTRUMENTS = 4
MODEL_STEPS = 4
ITERATIONS = 2
SECTIONS = 4
GRID_COLUMNS = 8192
INST_ROWS = 128
CAPACITY = 32
N_COL = 32


def draw_report_column(key, part):
    key = jax.random.fold_in(key, 11)
    owners = GRID_COLUMNS // COL_DEV
    pool = jnp.arange(owners * CAPACITY, dtype=jnp.int32)
    pool_owner = pool // CAPACITY
    hot_block = jax.random.randint(jax.random.fold_in(key, 1), (SECTIONS,), 0, owners)
    hot_block = hot_block.at[SECTIONS - 1].set(0)
    hot_block = hot_block.at[0].set(owners - 1)
    heaviness = jax.random.randint(jax.random.fold_in(key, 2), (SECTIONS, owners), 1, 5)

    def one_device(section, device):
        device_key = jax.random.fold_in(jax.random.fold_in(key, 3 + section), device)
        noise = jax.random.randint(jax.random.fold_in(device_key, 1), (owners * CAPACITY,), 0, 4096)
        score = noise // heaviness[section][pool_owner] + jnp.where(pool_owner == hot_block[section], 1 << 20, 0)
        order = jnp.argsort(score, stable=True)
        others = pool_owner[order[:REPORTS_DEV - CAPACITY]]
        chosen = jnp.concatenate([jnp.full((CAPACITY,), hot_block[section], jnp.int32), others])
        chosen = jax.random.permutation(jax.random.fold_in(device_key, 2), chosen)
        east = chosen * COL_DEV + jax.random.randint(jax.random.fold_in(device_key, 3), (REPORTS_DEV,), 0, COL_DEV)
        north = jax.random.randint(jax.random.fold_in(device_key, 4), (REPORTS_DEV,), 0, LAT_ROWS)
        cell = north * GRID_COLUMNS + east
        position = jnp.arange(REPORTS_DEV, dtype=jnp.int32)
        first_hot = jnp.argmax((chosen == hot_block[section]).astype(jnp.int32)).astype(jnp.int32)
        top_cell = jnp.int32(LAT_ROWS * GRID_COLUMNS - 1)
        cell = jnp.where((position == first_hot) & (section == 0), top_cell, cell)
        cell = jnp.where((position == first_hot) & (section == SECTIONS - 1) & (section != 0), jnp.int32(0), cell)
        return cell
    sections = jnp.arange(SECTIONS, dtype=jnp.int32)
    devices = jnp.arange(owners, dtype=jnp.int32)

    def one_section(section):

        def per_device(device):
            return one_device(section, device)
        return jax.vmap(per_device)(devices)
    layout = jax.vmap(one_section)(sections)
    return layout.reshape(SECTIONS, owners * REPORTS_DEV).astype(jnp.int32)


def draw_report_count(key, part):
    key = jax.random.fold_in(key, 12)
    owners = GRID_COLUMNS // COL_DEV
    total = SECTIONS * owners * INSTRUMENTS
    counts = jax.random.randint(jax.random.fold_in(key, 1), (total,), INST_ROWS // 4, INST_ROWS + 1)
    fullest = jax.random.randint(jax.random.fold_in(key, 2), (), 0, total)
    offset = jax.random.randint(jax.random.fold_in(key, 3), (), 1, total)
    emptiest = (fullest + offset) % total
    position = jnp.arange(total, dtype=jnp.int32)
    counts = jnp.where(position == fullest, INST_ROWS, counts)
    counts = jnp.where(position == emptiest, INST_ROWS // 4, counts)
    return counts.reshape(SECTIONS, owners, INSTRUMENTS).astype(jnp.int32)


def touch_ends(array, own_key, low, top_value):
    index_at = [jax.random.randint(jax.random.fold_in(own_key, axis), (), 0, length) for axis, length in enumerate(array.shape)]
    main_axis = array.shape.index(max(array.shape))
    next_to = index_at[:main_axis] + [(index_at[main_axis] + 1) % array.shape[main_axis]] + index_at[main_axis + 1:]
    return array.at[tuple(index_at)].set(low).at[tuple(next_to)].set(top_value)


def shard_levels(key, extent, split, low, high):
    loudness, own = 1.0, jax.random.fold_in(key, 6)
    for axis_at, shards_of in split:
        steps = jnp.exp(jax.random.uniform(jax.random.fold_in(own, axis_at), (shards_of,), jnp.float32, low / len(split), high / len(split)))
        loudness = loudness * jnp.repeat(steps, extent[axis_at] // shards_of).reshape([-1 if axis == axis_at else 1 for axis in range(len(extent))])
    return loudness


def centred(key, dims, width, reach, cuts=(), kind=jnp.bfloat16):
    level = shard_levels(key, dims, cuts, -0.22, 0.18) if cuts else 1.0
    result = jax.random.normal(key, dims, jnp.float32) * width * level
    return jnp.minimum(jnp.maximum(result, -reach), reach).astype(kind)


def setup_inputs(seed: int = 0) -> dict:
    key_of = jax.random.split(jax.random.key(seed), 11)
    forcing_state = centred(key_of[0], (SECTIONS, FIELDS, LEVELS, LAT_ROWS, GRID_COLUMNS), 1.0, 6.0, ((0, 4), (4, 32)), jnp.float32)
    model_error = jnp.clip(jnp.exp(math.log(3.0) - 2.3025851 * jax.random.uniform(key_of[1], (SECTIONS, FIELDS, LEVELS, LAT_ROWS, GRID_COLUMNS), jnp.float32) ** shard_levels(key_of[1], (SECTIONS, FIELDS, LEVELS, LAT_ROWS, GRID_COLUMNS), ((0, 4), (4, 32)), -0.2, 0.2)), 0.3, 3.0)
    courant = jnp.clip(jnp.exp(math.log(0.9) - 1.50407736 * jax.random.uniform(key_of[2], (SECTIONS, MODEL_STEPS, LEVELS, LAT_ROWS, GRID_COLUMNS), jnp.float32) ** shard_levels(key_of[2], (SECTIONS, MODEL_STEPS, LEVELS, LAT_ROWS, GRID_COLUMNS), ((0, 4), (4, 32)), -0.2, 0.2)), 0.2, 0.9)
    vertical_mix = centred(key_of[3], (FIELDS, LEVELS, LEVELS), LEVELS ** -0.5, 0.75, (), jnp.float32)
    radiance_jacobian = centred(key_of[4], (FIELDS * LEVELS, CHANNELS), (FIELDS * LEVELS) ** -0.5, 0.3125, (), jnp.float32)
    innovation = centred(key_of[5], (SECTIONS, N_COL * REPORTS_DEV, CHANNELS), 1.0, 6.0, ((0, 4), (1, 32)), jnp.float32)
    report_error = jnp.clip(jnp.exp(math.log(3.0) - 2.3025851 * jax.random.uniform(key_of[6], (SECTIONS, N_COL * REPORTS_DEV, CHANNELS), jnp.float32) ** shard_levels(key_of[6], (SECTIONS, N_COL * REPORTS_DEV, CHANNELS), ((0, 4), (1, 32)), -0.2, 0.2)), 0.3, 3.0)
    report_column = draw_report_column(jax.random.fold_in(key_of[10], 71), 0)
    report_slot = touch_ends(jax.random.randint(key_of[8], (SECTIONS, N_COL * REPORTS_DEV), 0, MODEL_STEPS), jax.random.fold_in(key_of[8], 1), 0, MODEL_STEPS - 1).astype(jnp.int32)
    report_count = draw_report_count(jax.random.fold_in(key_of[10], 71), 0)
    return dict(forcing_state=forcing_state, model_error=model_error, courant=courant, vertical_mix=vertical_mix, radiance_jacobian=radiance_jacobian, innovation=innovation, report_error=report_error, report_column=report_column, report_slot=report_slot, report_count=report_count)


def mixing(vertical_mix):
    return 0.6 * jnp.eye(LEVELS, dtype=jnp.float32)[None] + 0.4 * vertical_mix


def advance(values, courant_now, mixer):
    before = jnp.roll(values, 1, axis=3)
    upwind = values - courant_now * (values - before)
    return jnp.einsum("fkl,flyx->fkyx", mixer, upwind, precision=lax.Precision.HIGHEST)


def retreat(values, courant_now, mixer):
    mixed_back = jnp.einsum("flk,flyx->fkyx", mixer, values, precision=lax.Precision.HIGHEST)
    carried = courant_now * mixed_back
    return mixed_back - carried + jnp.roll(carried, -1, axis=3)


def validity(report_count):
    row_index = jnp.arange(INST_ROWS, dtype=jnp.int32)
    inside = row_index[None, None, None, :] < report_count[:, :, :, None]
    return inside.reshape(SECTIONS, N_COL * REPORTS_DEV).astype(jnp.float32)


def apply_system(model_dual, report_dual, increment, model_error, report_error, courant, mixer, jacobian, report_column, report_slot, weights):
    north_index = report_column // GRID_COLUMNS
    east_index = report_column % GRID_COLUMNS
    upper_list, middle_list, lower_list = [], [], []
    arriving = jnp.zeros_like(increment[0])
    for section in range(SECTIONS):
        values = increment[section]
        history = []
        for moment in range(MODEL_STEPS):
            history.append(values)
            values = advance(values, courant[section, moment], mixer)
        history = jnp.stack(history)
        upper_list.append(model_error[section] * model_dual[section] + increment[section] - arriving)
        arriving = values
        picked = history[report_slot[section], :, :, north_index[section], east_index[section]]
        picked = picked.reshape(N_COL * REPORTS_DEV, FIELDS * LEVELS)
        observed = jnp.dot(picked, jacobian, precision=lax.Precision.HIGHEST)
        row_weight = weights[section][:, None]
        middle_list.append(row_weight * (report_error[section] * report_dual[section] + observed))
        spread = jnp.dot(row_weight * report_dual[section], jacobian.T, precision=lax.Precision.HIGHEST)
        inject = jnp.zeros((MODEL_STEPS, LAT_ROWS, GRID_COLUMNS, FIELDS * LEVELS), jnp.float32)
        inject = inject.at[report_slot[section], north_index[section], east_index[section]].add(spread)
        inject = jnp.transpose(inject.reshape(MODEL_STEPS, LAT_ROWS, GRID_COLUMNS, FIELDS, LEVELS), (0, 3, 4, 1, 2))
        if section + 1 < SECTIONS:
            later_dual = model_dual[section + 1]
        else:
            later_dual = jnp.zeros_like(model_dual[section])
        adjoint = -later_dual
        for moment in reversed(range(MODEL_STEPS)):
            adjoint = retreat(adjoint, courant[section, moment], mixer) + inject[moment]
        lower_list.append(model_dual[section] + adjoint)
    return jnp.stack(upper_list), jnp.stack(middle_list), jnp.stack(lower_list)


def reference(forcing_state, model_error, courant, vertical_mix, radiance_jacobian, innovation, report_error, report_column, report_slot, report_count):
    mixer = mixing(vertical_mix)
    weights = validity(report_count)
    model_res = forcing_state
    report_res = weights[:, :, None] * innovation
    incr_res = jnp.zeros_like(forcing_state)
    model_sol = jnp.zeros_like(forcing_state)
    report_sol = jnp.zeros_like(innovation)
    incr_sol = jnp.zeros_like(forcing_state)
    for iteration in range(ITERATIONS):
        upper, middle, lower = apply_system(model_res, report_res, incr_res, model_error, report_error, courant, mixer, radiance_jacobian, report_column, report_slot, weights)
        projection = jnp.sum(model_res * upper) + jnp.sum(report_res * middle) + jnp.sum(incr_res * lower)
        energy = jnp.sum(upper * upper) + jnp.sum(middle * middle) + jnp.sum(lower * lower)
        step_size = projection / energy
        model_sol = model_sol + step_size * model_res
        report_sol = report_sol + step_size * report_res
        incr_sol = incr_sol + step_size * incr_res
        model_res = model_res - step_size * upper
        report_res = report_res - step_size * middle
        incr_res = incr_res - step_size * lower
    return (model_sol, report_sol, incr_sol, model_res, report_res, incr_res)
```

```python
import functools

import jax
import jax.numpy as jnp
from jax import lax
from jax.experimental import pallas as pl
from jax.experimental.pallas import tpu as pltpu
from jax.sharding import PartitionSpec as P

F32, BF16, I32 = jnp.float32, jnp.bfloat16, jnp.int32
MESH = pl.DeviceIdType.MESH
LEVELS, LAT, WIDTH, STEPS, CHANNELS = 64, 4, 256, 4, 128
ROWS, INST = 512, 4
INST_ROWS = ROWS // INST
SLOTS = 2 * ROWS
CELLS = LAT * WIDTH
HALO = 16
GROUPS = ((0, 4), (4, 4), (8, 2))


def split2(x):
    hi = x.astype(BF16)
    return hi, (x - hi.astype(F32)).astype(BF16)


def pack(w):
    row = jnp.concatenate(split2(w), axis=1)
    return jnp.concatenate([row, row], axis=0)


def halves(o):
    return o[:, :128] + o[:, 128:]


def mm(u, w):
    left = jnp.concatenate(split2(u), axis=1)
    return halves(jnp.dot(left, w, preferred_element_type=F32))


def native_rows(block, y, xt, count):
    return pl.ds(block * LEVELS * 2 * LAT + xt * LAT + y, count, stride=2 * LAT)


def load_pair(ref, g, y, xt):
    return ref[native_rows(2 * g, y, xt, 128), :]


def load_last(ref, y, xt):
    top = ref[native_rows(4, y, xt, 64), :]
    low = ref[native_rows(4, y + 2, xt, 64), :]
    return jnp.concatenate([top, low], axis=0)


def folded(x):
    return jnp.sum(x.reshape(x.shape[0] // 8, 8, 128), axis=0)


def system_kernel(
    n, nt,
    f_in, d_in, c_in, vm, jac, inn, rvar, col, slot, cnt,
    v1n, v2n, pun, pm_out, sc_out,
    f_t, df_t, rf, rd, c_t, v1, closing, arr, z, yacc, ysplit, rowsplit, keyrow,
    wa, wf, jf, jt, p_mat, pt_mat,
    send_m, send_1, send_2, recv_m, recv_1, recv_2, obs_s, obs_r,
    acc, red, redbuf, zred, zbuf,
    a2a_ss, a2a_rs, z_ss, z_rs, h_ss, h_rs, vh_ss, vh_rs, zz_ss, zz_rs,
):
    cap = SLOTS // n
    s, c = lax.axis_index("tm"), lax.axis_index("col")
    prev_s, next_s = lax.rem(s + nt - 1, nt), lax.rem(s + 1, nt)
    west, east = lax.rem(c + n - 1, n), lax.rem(c + 1, n)

    def rcopy(src, dst, ss, rs, to):
        return pltpu.make_async_remote_copy(
            src_ref=src, dst_ref=dst, send_sem=ss, recv_sem=rs, device_id=to, device_id_type=MESH
        )

    barrier = pltpu.get_barrier_semaphore()

    def greet(to):
        pl.semaphore_signal(barrier, inc=1, device_id=to, device_id_type=MESH)

    greet((prev_s, west))
    greet((next_s, east))

    @pl.loop(1, nt)
    def _(d):
        greet((lax.rem(s + d, nt), c))

    @pl.loop(1, n)
    def _(d):
        greet((s, lax.rem(c + d, n)))

    @pl.loop(0, 8)
    def _(k):
        for xt in range(2):
            f_t[k, pl.ds(xt * 128, 128), :] = load_pair(f_in, k // 4, k % 4, xt).T

    @pl.loop(0, 2)
    def _(y):
        for xt in range(2):
            f_t[8 + y, pl.ds(xt * 128, 128), :] = load_last(f_in, y, xt).T

    pl.semaphore_wait(barrier, n + nt)

    def z_send(src, dst, base, to):
        rest = []
        for i, (k0, kn) in enumerate(GROUPS):
            rest.append(
                rcopy(
                    src.at[pl.ds(k0, kn)], dst.at[pl.ds(k0, kn), pl.ds(0, WIDTH)],
                    z_ss.at[base + i], z_rs.at[base + i], to,
                )
            )
        return rest

    def z_halo(src, dst, i):
        return rcopy(
            src.at[:, pl.ds(0, HALO)], dst.at[:, pl.ds(WIDTH, HALO)],
            h_ss.at[i], h_rs.at[i], (prev_s, west),
        )

    f_halo = z_halo(f_t, rf, 0)
    f_halo.start()
    f_send = z_send(f_t, rf, 0, (prev_s, c))
    for copy in f_send:
        copy.start()

    rows_iota = lax.broadcasted_iota(I32, (ROWS, ROWS), 0)
    lane_iota = lax.broadcasted_iota(I32, (ROWS, ROWS), 1)
    upper_ones = jnp.where(rows_iota <= lane_iota, 1.0, 0.0).astype(BF16)
    column = col[...]
    shift_w, mask_n = WIDTH.bit_length() - 1, n - 1
    owner = (column >> shift_w) & mask_n
    cell = (column >> (shift_w + n.bit_length() - 1)) * WIDTH + (column & (WIDTH - 1))
    key = (slot[...] * CELLS + cell).astype(F32)
    owners = lax.broadcasted_iota(I32, (n, ROWS), 0)
    owned = jnp.where(owners == owner, 1.0, 0.0)
    ranks = jnp.dot(owned.astype(BF16), upper_ones, preferred_element_type=F32)
    landing = jnp.sum(owned * ((owners * cap).astype(F32) + ranks - 1.0), axis=0, keepdims=True)

    def as_column(row, b):
        return jnp.broadcast_to(row[:, b * 128:(b + 1) * 128], (128, 128)).T

    key_col = jnp.concatenate([as_column(key, b) for b in range(4)], axis=0)
    for b in range(SLOTS // 128):
        spots = (lax.broadcasted_iota(I32, (128, ROWS), 0) + b * 128).astype(F32)
        p_mat[b * 128:(b + 1) * 128, :] = jnp.where(spots == landing, 1.0, 0.0).astype(BF16)
    spots = lax.broadcasted_iota(I32, (128, SLOTS), 1).astype(F32)
    for b in range(ROWS // 128):
        land_col = jnp.concatenate([as_column(landing, b)] * (SLOTS // 128), axis=1)
        pt_mat[b * 128:(b + 1) * 128, :] = jnp.where(spots == land_col, 1.0, 0.0).astype(BF16)

    def placed(parts, out):
        right = jnp.concatenate(parts, axis=1)
        for b in range(4):
            o = jnp.dot(p_mat[b * 256:(b + 1) * 256, :], right, preferred_element_type=F32)
            total = o[:, :128]
            for i in range(1, len(parts)):
                total = total + o[:, i * 128:(i + 1) * 128]
            out[b * 256:(b + 1) * 256, :] = total

    def split3(x):
        hi, rest = x.astype(BF16), x - x.astype(BF16).astype(F32)
        return (hi,) + split2(rest)

    def exchange(i, src, dst, d):
        peer = lax.rem(c + d, n)
        return rcopy(
            src.at[pl.ds(pl.multiple_of(peer * cap, cap), cap)],
            dst.at[pl.ds(pl.multiple_of(c * cap, cap), cap)],
            a2a_ss.at[i, d], a2a_rs.at[i, d], (s, peer),
        )

    def exchange_start(i, src, dst):
        @pl.loop(1, n)
        def _(d):
            exchange(i, src, dst, d).start()

        mine = pl.ds(pl.multiple_of(c * cap, cap), cap)
        dst[mine, :] = src[mine, :]

    def exchange_wait(i, src, dst):
        @pl.loop(1, n)
        def _(d):
            peer = lax.rem(c + n - d, n)
            rcopy(
                src.at[pl.ds(0, cap)],
                dst.at[pl.ds(pl.multiple_of(peer * cap, cap), cap)],
                a2a_ss.at[i, d], a2a_rs.at[i, d], (s, peer),
            ).wait_recv()

    def exchange_sent(i, src, dst):
        @pl.loop(1, n)
        def _(d):
            exchange(i, src, dst, d).wait_send()

    placed(split2(key_col), send_m)
    exchange_start(0, send_m, recv_m)
    inst_iota = lax.broadcasted_iota(I32, (INST_ROWS, CHANNELS), 0)
    weight = jnp.concatenate(
        [jnp.where(inst_iota < cnt[0, i], 1.0, 0.0) for i in range(INST)], axis=0
    )
    wd = weight * inn[...]
    placed(split3(wd), send_1)
    exchange_start(1, send_1, recv_1)

    acc[...] = jnp.zeros_like(acc)

    def wind(m, y, xt):
        return c_in[native_rows(m, y, xt, 64), :]

    @pl.loop(0, STEPS * LAT)
    def _(i):
        m, y = i // LAT, i % LAT
        for xt in range(2):
            one = wind(m, y, xt)
            c_t[m * 6 + y, pl.ds(HALO + xt * 128, 128), :] = jnp.concatenate([one, one], axis=0).T

    @pl.loop(0, STEPS * 2)
    def _(i):
        m, y = i // 2, i % 2
        for xt in range(2):
            both = jnp.concatenate([wind(m, y, xt), wind(m, y + 2, xt)], axis=0)
            c_t[m * 6 + 4 + y, pl.ds(HALO + xt * 128, 128), :] = both.T

    c_west = rcopy(
        c_t.at[:, pl.ds(HALO, HALO)], c_t.at[:, pl.ds(HALO + WIDTH, HALO)],
        h_ss.at[2], h_rs.at[2], (s, west),
    )
    c_east = rcopy(
        c_t.at[:, pl.ds(WIDTH, HALO)], c_t.at[:, pl.ds(0, HALO)],
        h_ss.at[3], h_rs.at[3], (s, east),
    )
    c_west.start()
    c_east.start()

    eye = jnp.where(
        lax.broadcasted_iota(I32, (64, 64), 0) == lax.broadcasted_iota(I32, (64, 64), 1), 1.0, 0.0
    )
    nothing = jnp.zeros((64, 64), F32)
    for g, (fa, fb) in enumerate(((0, 1), (2, 3), (4, 4))):
        ma, mb = 0.6 * eye + 0.4 * vm[fa], 0.6 * eye + 0.4 * vm[fb]
        block = jnp.concatenate(
            [jnp.concatenate([ma, nothing], axis=1), jnp.concatenate([nothing, mb], axis=1)],
            axis=0,
        )
        wa[g] = pack(block)
        wf[g] = pack(block.T)
    none = jnp.zeros((64, CHANNELS), F32)
    last = jac[256:320, :]
    for g, block in enumerate(
        (
            jac[0:128, :], jac[128:256, :],
            jnp.concatenate([last, none], axis=0), jnp.concatenate([none, last], axis=0),
        )
    ):
        jf[g] = pack(block)
        jt[g] = pack(block.T)

    @pl.loop(0, 8)
    def _(k):
        for xt in range(2):
            g, y = k // 4, k % 4
            df_t[k, pl.ds(xt * 128, 128), :] = (
                load_pair(f_in, g, y, xt) * load_pair(d_in, g, y, xt)
            ).T

    @pl.loop(0, 2)
    def _(y):
        for xt in range(2):
            df_t[8 + y, pl.ds(xt * 128, 128), :] = (
                load_last(f_in, y, xt) * load_last(d_in, y, xt)
            ).T

    d_halo = z_halo(df_t, rd, 1)
    d_halo.start()
    d_send = z_send(df_t, rd, 3, (prev_s, c))
    for copy in d_send:
        copy.start()

    wrd = weight * (rvar[...] * wd)
    placed(split3(wrd), send_2)
    exchange_start(2, send_2, recv_2)

    def scatter(r, rows):
        rowsplit[...] = jnp.concatenate(split2(rows[...]), axis=1)

        @pl.loop(0, STEPS * LAT)
        def _(i):
            spot = (lax.broadcasted_iota(I32, (WIDTH, SLOTS), 0) + i * WIDTH).astype(F32)
            hit = jnp.where(spot == keyrow[0:1, :], 1.0, 0.0).astype(BF16)
            o = jnp.dot(hit, rowsplit[...], preferred_element_type=F32)
            z[r, i, pl.ds(0, WIDTH), :] = halves(o)

        edge = rcopy(
            z.at[r, :, pl.ds(0, HALO)], z.at[r, :, pl.ds(WIDTH, HALO)],
            h_ss.at[4 + r], h_rs.at[4 + r], (s, west),
        )
        edge.start()
        return edge

    exchange_wait(0, send_m, recv_m)
    for b in range(SLOTS // 128):
        keyrow[:, b * 128:(b + 1) * 128] = recv_m[b * 128:(b + 1) * 128, :].T[0:8, :]
    exchange_wait(1, send_1, recv_1)
    z_edge1 = scatter(0, recv_1)

    later = jnp.where(s < nt - 1, -1.0, 0.0).astype(F32)
    span = WIDTH + HALO

    def adjoint(r, k, g, wind_at, inject, received, own):
        a = received[k] * later
        for m in reversed(range(STEPS)):
            w = mm(a, wa[g])
            p = c_t[m * 6 + wind_at, pl.ds(HALO, span), :] * w
            a = w - p + pltpu.roll(p, span - 1, 0) + inject(m)
        return own[k] + a[0:WIDTH, :]

    def adjoint_pair(r, k, received, own):
        g, y = k // 4, k % 4
        return adjoint(r, k, g, y, lambda m: mm(z[r, m * LAT + y], jt[g]), received, own)

    def adjoint_last(r, y, received, own):
        def inject(m):
            return mm(z[r, m * LAT + y], jt[2]) + mm(z[r, m * LAT + y + 2], jt[3])

        return adjoint(r, 8 + y, 2, 4 + y, inject, received, own)

    def forward(k, g, wind_at, observe):
        v = v1[k]
        for m in range(STEPS):
            observe(m, v[HALO:, :])
            wind_now = c_t[m * 6 + wind_at, pl.ds(0, span), :]
            v = mm(v - wind_now * (v - pltpu.roll(v, 1, 0)), wf[g])
        closing[k] = v[HALO:, :]

    def put_pair(ref, g, y, value):
        for xt in range(2):
            ref[native_rows(2 * g, y, xt, 128), :] = value[xt * 128:(xt + 1) * 128, :].T

    def put_last(ref, y, value):
        for xt in range(2):
            turned = value[xt * 128:(xt + 1) * 128, :].T
            ref[native_rows(4, y, xt, 64), :] = turned[:64, :]
            ref[native_rows(4, y + 2, xt, 64), :] = turned[64:, :]

    yacc[...] = jnp.zeros_like(yacc)
    c_west.wait_recv()
    c_east.wait_recv()
    f_halo.wait_recv()
    z_edge1.wait_recv()

    def edge_v1(i):
        k0, kn = GROUPS[i]
        return rcopy(
            v1.at[pl.ds(k0, kn), pl.ds(WIDTH, HALO)], v1.at[pl.ds(k0, kn), pl.ds(0, HALO)],
            vh_ss.at[i], vh_rs.at[i], (s, east),
        )

    def send_closing(i):
        k0, kn = GROUPS[i]
        return rcopy(
            closing.at[pl.ds(k0, kn)], arr.at[pl.ds(k0, kn)],
            zz_ss.at[i], zz_rs.at[i], (next_s, c),
        )

    edges = [edge_v1(i) for i in range(3)]
    closings = [send_closing(i) for i in range(3)]

    def first_adjoint(i):
        f_send[i].wait_recv()
        if i < 2:
            @pl.loop(4 * i, 4 * i + 4)
            def _(k):
                value = adjoint_pair(0, k, rf, f_t)
                v1[k, pl.ds(HALO, WIDTH), :] = value
                acc[1] += folded(value * value)
                put_pair(v1n, k // 4, k % 4, value)
        else:
            @pl.loop(0, 2)
            def _(y):
                value = adjoint_last(0, y, rf, f_t)
                v1[8 + y, pl.ds(HALO, WIDTH), :] = value
                acc[1] += folded(value * value)
                put_last(v1n, y, value)
        edges[i].start()

    def first_forward(i):
        edges[i].wait_recv()
        if i < 2:
            @pl.loop(4 * i, 4 * i + 4)
            def _(k):
                g, y = k // 4, k % 4

                def observe(m, v):
                    yacc[m * LAT + y] += mm(v, jf[g])

                forward(k, g, y, observe)
        else:
            @pl.loop(0, 2)
            def _(y):
                def observe(m, v):
                    yacc[m * LAT + y] += mm(v, jf[2])
                    yacc[m * LAT + y + 2] += mm(v, jf[3])

                forward(8 + y, 2, 4 + y, observe)
        closings[i].start()

    first_adjoint(0)
    exchange_wait(2, send_2, recv_2)
    z_edge2 = scatter(1, recv_2)
    first_forward(0)
    first_adjoint(1)
    first_forward(1)
    first_adjoint(2)
    first_forward(2)

    @pl.loop(0, STEPS * LAT)
    def _(i):
        ysplit[pl.ds(pl.multiple_of(i * WIDTH, WIDTH), WIDTH), :] = jnp.concatenate(
            split2(yacc[i]), axis=1
        )

    @pl.loop(0, 4)
    def _(b):
        rows = pl.ds(pl.multiple_of(b * 256, 256), 256)
        at = jnp.concatenate([recv_m[rows, :]] * (CELLS // 128), axis=1)
        total = jnp.zeros((256, 256), F32)
        for m in range(STEPS):
            spot = (lax.broadcasted_iota(I32, (256, CELLS), 1) + m * CELLS).astype(F32)
            hit = jnp.where(spot == at, 1.0, 0.0).astype(BF16)
            total = total + jnp.dot(
                hit, ysplit[m * CELLS:(m + 1) * CELLS, :], preferred_element_type=F32
            )
        obs_s[rows, :] = halves(total)

    exchange_start(3, obs_s, obs_r)

    @pl.loop(0, 10)
    def _(i):
        rows = pl.ds(pl.multiple_of(i * 256, 256), 256)
        f = f_in[rows, :]
        df = f * d_in[rows, :]
        acc[0] += folded(f * df)
        acc[1] += folded(df * df)

    acc[0] += folded(wd * wrd)
    acc[1] += folded(wrd * wrd)

    d_halo.wait_recv()
    z_edge2.wait_recv()

    def second_adjoint(i):
        d_send[i].wait_recv()

        def take(k, value):
            own = v1[k, pl.ds(HALO, WIDTH), :]
            acc[3] += folded(own * value)
            acc[4] += folded(value * value)

        if i < 2:
            @pl.loop(4 * i, 4 * i + 4)
            def _(k):
                value = adjoint_pair(1, k, rd, df_t)
                take(k, value)
                put_pair(v2n, k // 4, k % 4, value)
        else:
            @pl.loop(0, 2)
            def _(y):
                value = adjoint_last(1, y, rd, df_t)
                take(8 + y, value)
                put_last(v2n, y, value)

    has_before = jnp.where(s > 0, 1.0, 0.0).astype(F32)

    def arrive(i):
        closings[i].wait_recv()
        if i < 2:
            @pl.loop(4 * i, 4 * i + 4)
            def _(k):
                value = v1[k, pl.ds(HALO, WIDTH), :] - has_before * arr[k]
                put_pair(pun, k // 4, k % 4, value)
        else:
            @pl.loop(0, 2)
            def _(y):
                value = v1[8 + y, pl.ds(HALO, WIDTH), :] - has_before * arr[8 + y]
                put_last(pun, y, value)

    second_adjoint(0)
    second_adjoint(1)
    for i in range(3):
        arrive(i)

    @pl.loop(0, 10)
    def _(i):
        rows = pl.ds(pl.multiple_of(i * 256, 256), 256)
        f, d = f_in[rows, :], d_in[rows, :]
        df = f * d
        pu = d * df + pun[rows, :]
        pun[rows, :] = pu
        acc[2] += folded(f * pu)
        acc[3] += folded(df * pu)
        acc[4] += folded(pu * pu)

    exchange_wait(3, obs_s, obs_r)
    right = jnp.concatenate(split2(obs_r[...]), axis=1)
    seen = halves(jnp.dot(pt_mat[...], right, preferred_element_type=F32))
    pm = weight * (rvar[...] * wrd + seen)
    pm_out[...] = pm
    acc[2] += folded(wd * pm)
    acc[3] += folded(wrd * pm)
    acc[4] += folded(pm * pm)

    second_adjoint(2)

    lines = [jnp.sum(acc[i], axis=0, keepdims=True) for i in range(5)]
    red[...] = jnp.concatenate(lines + [jnp.zeros((3, 128), F32)], axis=0)

    def share(d):
        return rcopy(
            red, redbuf.at[c], a2a_ss.at[4, d], a2a_rs.at[4, d], (s, lax.rem(c + d, n))
        )

    @pl.loop(1, n)
    def _(d):
        share(d).start()

    redbuf[c] = red[...]

    @pl.loop(1, n)
    def _(d):
        peer = lax.rem(c + n - d, n)
        rcopy(red, redbuf.at[peer], a2a_ss.at[4, d], a2a_rs.at[4, d], (s, peer)).wait_recv()

    zred[...] = jnp.sum(redbuf[...], axis=0)

    def share_z(d):
        return rcopy(
            zred, zbuf.at[s], z_ss.at[6 + d], z_rs.at[6 + d], (lax.rem(s + d, nt), c)
        )

    for d in range(1, nt):
        share_z(d).start()
    zbuf[s] = zred[...]
    for d in range(1, nt):
        peer = lax.rem(s + nt - d, nt)
        rcopy(zred, zbuf.at[peer], z_ss.at[6 + d], z_rs.at[6 + d], (peer, c)).wait_recv()

    total = jnp.sum(jnp.sum(zbuf[...], axis=0), axis=1, keepdims=True)
    total = jnp.broadcast_to(total, (8, 128))
    rq, qq, rp, qp, pp = (total[i:i + 1, :] for i in range(5))
    step1 = rq / qq
    step2 = step1 * (step1 * qp - rp) / (qq - 2.0 * step1 * qp + step1 * step1 * pp)
    sc_out[...] = jnp.concatenate(
        [step1 + step2, step1 * step2, jnp.zeros((6, 128), F32)], axis=0
    )

    for i, (src, dst) in enumerate(
        ((send_m, recv_m), (send_1, recv_1), (send_2, recv_2), (obs_s, obs_r))
    ):
        exchange_sent(i, src, dst)

    @pl.loop(1, n)
    def _(d):
        share(d).wait_send()

    for d in range(1, nt):
        share_z(d).wait_send()
    for copy in [f_halo, d_halo, c_west, c_east, z_edge1, z_edge2] + f_send + d_send:
        copy.wait_send()
    for copy in edges + closings:
        copy.wait_send()


def finish_kernel(sc, f_in, d_in, v1, v2, pu, inn, rvar, cnt, pm, ms, rs, xs, mr, rr, xr):
    t, q = sc[0:1, :], sc[1:2, :]
    f, d = f_in[...], d_in[...]
    df = f * d
    ms[...] = t * f - q * df
    mr[...] = f - t * df + q * pu[...]
    v = v1[...]
    xs[...] = -(q * v)
    xr[...] = q * v2[...] - t * v
    inside = lax.broadcasted_iota(I32, (INST_ROWS, CHANNELS), 0) < cnt[0, pl.program_id(0)]
    weight = jnp.where(inside, 1.0, 0.0)
    wd = weight * inn[...]
    wrd = weight * (rvar[...] * wd)
    rs[...] = t * wd - q * wrd
    rr[...] = wd - t * wrd + q * pm[...]


def to_rows(x):
    a, b, y, w = x.shape
    return x.reshape(a, b, y, w // 128, 128).transpose(0, 1, 3, 2, 4).reshape(-1, 128)


def from_rows(x, shape):
    a, b, y, w = shape
    return x.reshape(a, b, w // 128, y, 128).transpose(0, 1, 3, 2, 4).reshape(shape)


def body(n, nt, forcing_state, model_error, courant, vertical_mix, radiance_jacobian,
         innovation, report_error, report_column, report_slot, report_count):
    f, d, wind = (to_rows(x[0]) for x in (forcing_state, model_error, courant))
    inn, rvar, cnt = innovation[0], report_error[0], report_count[0]
    size = f.shape[0]
    vmem = pl.BlockSpec(memory_space=pltpu.VMEM)
    smem = pl.BlockSpec(memory_space=pltpu.SMEM)
    V = pltpu.VMEM
    state = jax.ShapeDtypeStruct((size, 128), F32)
    reports = jax.ShapeDtypeStruct((ROWS, CHANNELS), F32)
    span = WIDTH + HALO
    slots = V((SLOTS, 128), F32)
    dma = pltpu.SemaphoreType.DMA
    v1, v2, pu, pm, sc = pl.pallas_call(
        functools.partial(system_kernel, n, nt),
        out_shape=(state, state, state, reports, jax.ShapeDtypeStruct((8, 128), F32)),
        in_specs=[vmem] * 9 + [smem],
        out_specs=(vmem,) * 5,
        scratch_shapes=[
            V((10, WIDTH, 128), F32), V((10, WIDTH, 128), F32),
            V((10, span, 128), F32), V((10, span, 128), F32),
            V((6 * STEPS, span + HALO, 128), F32),
            V((10, span, 128), F32), V((10, WIDTH, 128), F32), V((10, WIDTH, 128), F32),
            V((2, STEPS * LAT, span, 128), F32), V((STEPS * LAT, WIDTH, 128), F32),
            V((STEPS * CELLS, 256), BF16), V((SLOTS, 256), BF16), V((8, SLOTS), F32),
            V((3, 256, 256), BF16), V((3, 256, 256), BF16),
            V((4, 256, 256), BF16), V((4, 256, 256), BF16),
            V((SLOTS, ROWS), BF16), V((ROWS, SLOTS), BF16),
            slots, slots, slots, slots, slots, slots, slots, slots,
            V((5, 8, 128), F32), V((8, 128), F32), V((n, 8, 128), F32),
            V((8, 128), F32), V((nt, 8, 128), F32),
            dma((5, n)), dma((5, n)), dma((6 + nt,)), dma((6 + nt,)),
            dma((6,)), dma((6,)), dma((3,)), dma((3,)), dma((3,)), dma((3,)),
        ],
        compiler_params=pltpu.CompilerParams(
            collective_id=0, has_side_effects=True, vmem_limit_bytes=56 * 1024 * 1024
        ),
        cost_estimate=pl.CostEstimate(flops=40 * 10**9, bytes_accessed=10**7, transcendentals=0),
    )(f, d, wind, vertical_mix, radiance_jacobian, inn, rvar, report_column, report_slot, cnt)
    part = pl.BlockSpec((size // INST, 128), lambda i: (i, 0))
    rpart = pl.BlockSpec((INST_ROWS, CHANNELS), lambda i: (i, 0))
    ms, rs, xs, mr, rr, xr = pl.pallas_call(
        finish_kernel,
        grid=(INST,),
        out_shape=(state, reports, state, state, reports, state),
        in_specs=[
            pl.BlockSpec((8, 128), lambda i: (0, 0)), part, part, part, part, part,
            rpart, rpart, smem, rpart,
        ],
        out_specs=(part, rpart, part, part, rpart, part),
        compiler_params=pltpu.CompilerParams(vmem_limit_bytes=32 * 1024 * 1024),
    )(sc, f, d, v1, v2, pu, inn, rvar, cnt, pm)
    shape = forcing_state.shape[1:]
    ms, xs, mr, xr = (from_rows(x, shape)[None] for x in (ms, xs, mr, xr))
    return ms, rs[None], xs, mr, rr[None], xr


def solution(mesh):
    grid = P("tm", None, None, None, "col")
    reports = P("tm", "col", None)
    in_specs = (
        grid, grid, grid, P(), P(), reports, reports, P("tm", "col"), P("tm", "col"), reports,
    )
    out_specs = (grid, reports, grid, grid, reports, grid)
    run = functools.partial(body, mesh.shape["col"], mesh.shape["tm"])
    return jax.shard_map(run, mesh=mesh, in_specs=in_specs, out_specs=out_specs, check_vma=False)
```

```python
import functools

import jax
import jax.numpy as jnp
from jax import lax
from jax.experimental import pallas as pl
from jax.experimental.pallas import tpu as pltpu
from jax.sharding import PartitionSpec as P

F32, BF16, I32 = jnp.float32, jnp.bfloat16, jnp.int32
MESH = pl.DeviceIdType.MESH
LEVELS, LAT, WIDTH, STEPS, CHANNELS = 64, 4, 256, 4, 128
ROWS, INST = 512, 4
INST_ROWS = ROWS // INST
SLOTS = 2 * ROWS
CELLS = LAT * WIDTH
HALO, EDGE = 16, 8
LAST = 8
GROUPS = ((0, 4), (4, 4), (8, 2))


def split2(x):
    hi = x.astype(BF16)
    return hi, (x - hi.astype(F32)).astype(BF16)


def pack(w):
    row = jnp.concatenate(split2(w), axis=1)
    return jnp.concatenate([row, row], axis=0)


def halves(o):
    return o[:, :128] + o[:, 128:]


def mm(u, w):
    left = jnp.concatenate(split2(u), axis=1)
    return halves(jnp.dot(left, w, preferred_element_type=F32))


def native_rows(block, y, xt, count):
    return pl.ds(block * LEVELS * 2 * LAT + xt * LAT + y, count, stride=2 * LAT)


def load_pair(ref, g, y, xt):
    return ref[native_rows(2 * g, y, xt, 128), :]


def load_last(ref, y, xt):
    top = ref[native_rows(4, y, xt, 64), :]
    low = ref[native_rows(4, y + 2, xt, 64), :]
    return jnp.concatenate([top, low], axis=0)


def folded(x):
    return jnp.sum(x.reshape(x.shape[0] // 8, 8, 128), axis=0)


def system_kernel(
    n, nt,
    f_hbm, d_hbm, c_hbm, vm_hbm, jac_hbm, inn_hbm, rvar_hbm, col_hbm, slot_hbm, cnt_hbm,
    f_in, d_in, v1n, v2n, pun, wd_out, wrd_out, pm_out, sc_out,
    c_in, vm, jac, inn, rvar, col, slot, cnt,
    f_t, df_t, rf, rd, c_t, v1, closing, arr, z, yacc, ysplit, rowsplit, keyrow,
    wa, wf, jf, jt, p_mat, pt_mat, send_a, recv_a, obs_s, obs_r,
    acc, red, redbuf, zred, zbuf,
    in_s, a2a_ss, a2a_rs, z_ss, z_rs, h_ss, h_rs, vh_ss, vh_rs, zz_ss, zz_rs,
):
    cap = SLOTS // n
    s, c = lax.axis_index("tm"), lax.axis_index("col")
    prev_s, next_s = lax.rem(s + nt - 1, nt), lax.rem(s + 1, nt)
    west, east = lax.rem(c + n - 1, n), lax.rem(c + 1, n)

    def rcopy(src, dst, ss, rs, to):
        return pltpu.make_async_remote_copy(
            src_ref=src, dst_ref=dst, send_sem=ss, recv_sem=rs, device_id=to, device_id_type=MESH
        )

    pairs = (
        (f_hbm, f_in), (col_hbm, col), (slot_hbm, slot), (cnt_hbm, cnt), (inn_hbm, inn),
        (rvar_hbm, rvar), (c_hbm, c_in), (vm_hbm, vm), (jac_hbm, jac), (d_hbm, d_in),
    )
    loads = [pltpu.make_async_copy(a, b, in_s.at[i]) for i, (a, b) in enumerate(pairs)]
    for load in loads:
        load.start()

    barrier = pltpu.get_barrier_semaphore()

    def greet(to):
        pl.semaphore_signal(barrier, inc=1, device_id=to, device_id_type=MESH)

    greet((prev_s, west))
    greet((next_s, east))

    @pl.loop(1, nt)
    def _(d):
        greet((lax.rem(s + d, nt), c))

    @pl.loop(1, n)
    def _(d):
        greet((s, lax.rem(c + d, n)))

    loads[0].wait()

    @pl.loop(0, 8)
    def _(k):
        for xt in range(2):
            f_t[k, pl.ds(xt * 128, 128), :] = load_pair(f_in, k // 4, k % 4, xt).T

    @pl.loop(0, 2)
    def _(y):
        for xt in range(2):
            f_t[8 + y, pl.ds(xt * 128, 128), :] = load_last(f_in, y, xt).T

    pl.semaphore_wait(barrier, n + nt)

    def z_send(src, dst, base, to):
        rest = []
        for i, (k0, kn) in enumerate(GROUPS):
            rest.append(
                rcopy(
                    src.at[pl.ds(k0, kn)], dst.at[pl.ds(k0, kn), pl.ds(0, WIDTH)],
                    z_ss.at[base + i], z_rs.at[base + i], to,
                )
            )
        return rest

    def z_halo(src, dst, i):
        return rcopy(
            src.at[:, pl.ds(0, EDGE)], dst.at[:, pl.ds(WIDTH, EDGE)],
            h_ss.at[i], h_rs.at[i], (prev_s, west),
        )

    f_halo = z_halo(f_t, rf, 0)
    f_halo.start()
    f_send = z_send(f_t, rf, 0, (prev_s, c))
    for copy in f_send:
        copy.start()

    rows_iota = lax.broadcasted_iota(I32, (ROWS, ROWS), 0)
    lane_iota = lax.broadcasted_iota(I32, (ROWS, ROWS), 1)
    upper_ones = jnp.where(rows_iota <= lane_iota, 1.0, 0.0).astype(BF16)
    for load in loads[1:4]:
        load.wait()
    column = col[...]
    shift_w, mask_n = WIDTH.bit_length() - 1, n - 1
    owner = (column >> shift_w) & mask_n
    cell = (column >> (shift_w + n.bit_length() - 1)) * WIDTH + (column & (WIDTH - 1))
    key = (slot[...] * CELLS + cell).astype(F32)
    owners = lax.broadcasted_iota(I32, (n, ROWS), 0)
    owned = jnp.where(owners == owner, 1.0, 0.0)
    ranks = jnp.dot(owned.astype(BF16), upper_ones, preferred_element_type=F32)
    landing = jnp.sum(owned * ((owners * cap).astype(F32) + ranks - 1.0), axis=0, keepdims=True)

    def as_column(row, b):
        return jnp.broadcast_to(row[:, b * 128:(b + 1) * 128], (128, 128)).T

    key_col = jnp.concatenate([as_column(key, b) for b in range(4)], axis=0)
    for b in range(SLOTS // 128):
        spots = (lax.broadcasted_iota(I32, (128, ROWS), 0) + b * 128).astype(F32)
        p_mat[b * 128:(b + 1) * 128, :] = jnp.where(spots == landing, 1.0, 0.0).astype(BF16)
    spots = lax.broadcasted_iota(I32, (128, SLOTS), 1).astype(F32)
    for b in range(ROWS // 128):
        land_col = jnp.concatenate([as_column(landing, b)] * (SLOTS // 128), axis=1)
        pt_mat[b * 128:(b + 1) * 128, :] = jnp.where(spots == land_col, 1.0, 0.0).astype(BF16)

    def split3(x):
        hi, rest = x.astype(BF16), x - x.astype(BF16).astype(F32)
        return (hi,) + split2(rest)

    def exchange(i, src, dst, d):
        peer = lax.rem(c + d, n)
        return rcopy(
            src.at[peer], dst.at[c], a2a_ss.at[i, d], a2a_rs.at[i, d], (s, peer)
        )

    def exchange_start(i, src, dst):
        @pl.loop(1, n)
        def _(d):
            exchange(i, src, dst, d).start()

        dst[c] = src[c]

    def exchange_wait(i, src, dst):
        @pl.loop(1, n)
        def _(d):
            peer = lax.rem(c + n - d, n)
            rcopy(
                src.at[peer], dst.at[peer], a2a_ss.at[i, d], a2a_rs.at[i, d], (s, peer)
            ).wait_recv()

    def exchange_sent(i, src, dst):
        @pl.loop(1, n)
        def _(d):
            exchange(i, src, dst, d).wait_send()

    loads[4].wait()
    loads[5].wait()
    inst_iota = lax.broadcasted_iota(I32, (INST_ROWS, CHANNELS), 0)
    weight = jnp.concatenate(
        [jnp.where(inst_iota < cnt[0:1, i:i + 1], 1.0, 0.0) for i in range(INST)], axis=0
    )
    wd = weight * inn[...]
    wrd = weight * (rvar[...] * wd)
    wd_out[...] = wd
    wrd_out[...] = wrd
    parts = split3(wd) + split3(wrd) + split2(key_col)
    right = jnp.concatenate(parts, axis=1)
    per = 256 // cap
    for b in range(4):
        o = jnp.dot(p_mat[b * 256:(b + 1) * 256, :], right, preferred_element_type=F32)
        o = [o[:, i * 128:(i + 1) * 128] for i in range(8)]
        for i, total in enumerate((o[0] + o[1] + o[2], o[3] + o[4] + o[5], o[6] + o[7])):
            send_a[b * per:(b + 1) * per, i * cap:(i + 1) * cap, :] = total.reshape(per, cap, 128)
    exchange_start(0, send_a, recv_a)

    acc[...] = jnp.zeros_like(acc)

    loads[6].wait()

    def wind(m, y, xt):
        return c_in[native_rows(m, y, xt, 64), :]

    @pl.loop(0, STEPS * LAT)
    def _(i):
        m, y = i // LAT, i % LAT
        for xt in range(2):
            one = wind(m, y, xt)
            c_t[m * 6 + y, pl.ds(HALO + xt * 128, 128), :] = jnp.concatenate([one, one], axis=0).T

    @pl.loop(0, STEPS * 2)
    def _(i):
        m, y = i // 2, i % 2
        for xt in range(2):
            both = jnp.concatenate([wind(m, y, xt), wind(m, y + 2, xt)], axis=0)
            c_t[m * 6 + 4 + y, pl.ds(HALO + xt * 128, 128), :] = both.T

    c_west = rcopy(
        c_t.at[:, pl.ds(HALO, EDGE)], c_t.at[:, pl.ds(HALO + WIDTH, EDGE)],
        h_ss.at[2], h_rs.at[2], (s, west),
    )
    c_east = rcopy(
        c_t.at[:, pl.ds(WIDTH + HALO - EDGE, EDGE)], c_t.at[:, pl.ds(HALO - EDGE, EDGE)],
        h_ss.at[3], h_rs.at[3], (s, east),
    )
    c_west.start()
    c_east.start()

    loads[7].wait()
    loads[8].wait()

    eye = jnp.where(
        lax.broadcasted_iota(I32, (64, 64), 0) == lax.broadcasted_iota(I32, (64, 64), 1), 1.0, 0.0
    )
    nothing = jnp.zeros((64, 64), F32)
    for g, (fa, fb) in enumerate(((0, 1), (2, 3), (4, 4))):
        ma, mb = 0.6 * eye + 0.4 * vm[fa], 0.6 * eye + 0.4 * vm[fb]
        block = jnp.concatenate(
            [jnp.concatenate([ma, nothing], axis=1), jnp.concatenate([nothing, mb], axis=1)],
            axis=0,
        )
        wa[g] = pack(block)
        wf[g] = pack(block.T)
    none = jnp.zeros((64, CHANNELS), F32)
    last = jac[256:320, :]
    for g, block in enumerate(
        (
            jac[0:128, :], jac[128:256, :],
            jnp.concatenate([last, none], axis=0), jnp.concatenate([none, last], axis=0),
        )
    ):
        jf[g] = pack(block)
        jt[g] = pack(block.T)

    loads[9].wait()

    @pl.loop(0, 8)
    def _(k):
        for xt in range(2):
            g, y = k // 4, k % 4
            df_t[k, pl.ds(xt * 128, 128), :] = (
                load_pair(f_in, g, y, xt) * load_pair(d_in, g, y, xt)
            ).T

    @pl.loop(0, 2)
    def _(y):
        for xt in range(2):
            df_t[8 + y, pl.ds(xt * 128, 128), :] = (
                load_last(f_in, y, xt) * load_last(d_in, y, xt)
            ).T

    d_halo = z_halo(df_t, rd, 1)
    d_halo.start()
    d_send = z_send(df_t, rd, 3, (prev_s, c))
    for copy in d_send:
        copy.start()

    exchange_wait(0, send_a, recv_a)

    def received_rows(i):
        return recv_a[:, i * cap:(i + 1) * cap, :].reshape(SLOTS, 128)

    keys = received_rows(2)
    for b in range(SLOTS // 128):
        keyrow[:, b * 128:(b + 1) * 128] = keys[b * 128:(b + 1) * 128, :].T[0:8, :]
    rowsplit[...] = jnp.concatenate(split2(received_rows(0)) + split2(received_rows(1)), axis=1)

    @pl.loop(0, STEPS * LAT)
    def _(i):
        spot = (lax.broadcasted_iota(I32, (WIDTH, SLOTS), 0) + i * WIDTH).astype(F32)
        hit = jnp.where(spot == keyrow[0:1, :], 1.0, 0.0).astype(BF16)
        o = jnp.dot(hit, rowsplit[...], preferred_element_type=F32)
        z[0, i, pl.ds(0, WIDTH), :] = halves(o[:, :256])
        z[1, i, pl.ds(0, WIDTH), :] = halves(o[:, 256:])

    z_edge = rcopy(
        z.at[:, pl.ds(LAT, 3 * LAT), pl.ds(0, EDGE)],
        z.at[:, pl.ds(LAT, 3 * LAT), pl.ds(WIDTH, EDGE)],
        h_ss.at[4], h_rs.at[4], (s, west),
    )
    z_edge.start()

    later = jnp.where(s < nt - 1, -1.0, 0.0).astype(F32)
    span = WIDTH + HALO

    def block(x, first, rows, count):
        return x[pl.ds(first, 2), pl.ds(rows, count), :].reshape(2 * count, 128)

    def adjoint(r, k, g, y, received, own):
        a = block(received, k, 0, span) * later
        wind_at = 4 if k is LAST else y
        for m in reversed(range(STEPS)):
            w = mm(a, wa[g])
            p = block(c_t, m * 6 + wind_at, HALO, span) * w
            if k is LAST:
                inject = mm(block(z.at[r], m * LAT, 0, span), jt[2])
                inject = inject + mm(block(z.at[r], m * LAT + 2, 0, span), jt[3])
            else:
                inject = mm(block(z.at[r], m * LAT + y, 0, span), jt[g])
            a = w - p + pltpu.roll(p, 2 * span - 1, 0) + inject
        a = a.reshape(2, span, 128)
        return [own[k + i] + a[i, 0:WIDTH, :] for i in range(2)]

    def forward(k, g, y):
        v = block(v1, k, 0, span)
        wind_at = 4 if k is LAST else y
        for m in range(STEPS):
            inner = v.reshape(2, span, 128)[:, HALO:, :].reshape(2 * WIDTH, 128)
            if k is LAST:
                yacc[pl.ds(m * LAT, 2)] += mm(inner, jf[2]).reshape(2, WIDTH, 128)
                yacc[pl.ds(m * LAT + 2, 2)] += mm(inner, jf[3]).reshape(2, WIDTH, 128)
            else:
                yacc[pl.ds(m * LAT + y, 2)] += mm(inner, jf[g]).reshape(2, WIDTH, 128)
            wind_now = block(c_t, m * 6 + wind_at, 0, span)
            v = mm(v - wind_now * (v - pltpu.roll(v, 1, 0)), wf[g])
        closing[pl.ds(k, 2)] = v.reshape(2, span, 128)[:, HALO:, :]

    def each_pair(i, run):
        if i < 2:
            @pl.loop(0, 2)
            def _(j):
                run(4 * i + 2 * j, i, 2 * j)
        else:
            run(LAST, 2, 0)

    def put_pair(ref, g, y, value):
        for xt in range(2):
            ref[native_rows(2 * g, y, xt, 128), :] = value[xt * 128:(xt + 1) * 128, :].T

    def put(ref, k, g, y, value):
        if g == 2:
            put_last(ref, y, value)
        else:
            put_pair(ref, g, y, value)

    def put_last(ref, y, value):
        for xt in range(2):
            turned = value[xt * 128:(xt + 1) * 128, :].T
            ref[native_rows(4, y, xt, 64), :] = turned[:64, :]
            ref[native_rows(4, y + 2, xt, 64), :] = turned[64:, :]

    yacc[...] = jnp.zeros_like(yacc)
    c_west.wait_recv()
    c_east.wait_recv()
    f_halo.wait_recv()
    z_edge.wait_recv()

    def edge_v1(i):
        k0, kn = GROUPS[i]
        return rcopy(
            v1.at[pl.ds(k0, kn), pl.ds(WIDTH + HALO - EDGE, EDGE)],
            v1.at[pl.ds(k0, kn), pl.ds(HALO - EDGE, EDGE)],
            vh_ss.at[i], vh_rs.at[i], (s, east),
        )

    def send_closing(i):
        k0, kn = GROUPS[i]
        return rcopy(
            closing.at[pl.ds(k0, kn)], arr.at[pl.ds(k0, kn)],
            zz_ss.at[i], zz_rs.at[i], (next_s, c),
        )

    edges = [edge_v1(i) for i in range(3)]
    closings = [send_closing(i) for i in range(3)]

    def first_adjoint(i):
        f_send[i].wait_recv()

        def run(k, g, y):
            for j, value in enumerate(adjoint(0, k, g, y, rf, f_t)):
                v1[k + j, pl.ds(HALO, WIDTH), :] = value
                acc[1] += folded(value * value)
                put(v1n, k + j, g, y + j, value)

        each_pair(i, run)
        edges[i].start()

    def first_forward(i):
        edges[i].wait_recv()
        each_pair(i, forward)
        closings[i].start()

    first_adjoint(0)
    first_adjoint(1)
    first_forward(0)
    first_adjoint(2)
    first_forward(1)
    first_forward(2)

    @pl.loop(0, STEPS * LAT)
    def _(i):
        ysplit[pl.ds(pl.multiple_of(i * WIDTH, WIDTH), WIDTH), :] = jnp.concatenate(
            split2(yacc[i]), axis=1
        )

    @pl.loop(0, 4)
    def _(b):
        took = recv_a[pl.ds(pl.multiple_of(b * per, per), per), 2 * cap:3 * cap, :]
        at = jnp.concatenate([took.reshape(256, 128)] * (CELLS // 128), axis=1)
        total = jnp.zeros((256, 256), F32)
        for m in range(STEPS):
            spot = (lax.broadcasted_iota(I32, (256, CELLS), 1) + m * CELLS).astype(F32)
            hit = jnp.where(spot == at, 1.0, 0.0).astype(BF16)
            total = total + jnp.dot(
                hit, ysplit[m * CELLS:(m + 1) * CELLS, :], preferred_element_type=F32
            )
        obs_s[pl.ds(pl.multiple_of(b * per, per), per)] = halves(total).reshape(per, cap, 128)

    exchange_start(1, obs_s, obs_r)

    @pl.loop(0, 10)
    def _(i):
        rows = pl.ds(pl.multiple_of(i * 256, 256), 256)
        f = f_in[rows, :]
        df = f * d_in[rows, :]
        acc[0] += folded(f * df)
        acc[1] += folded(df * df)

    acc[0] += folded(wd * wrd)
    acc[1] += folded(wrd * wrd)

    d_halo.wait_recv()

    def second_adjoint(i):
        d_send[i].wait_recv()

        def run(k, g, y):
            for j, value in enumerate(adjoint(1, k, g, y, rd, df_t)):
                own = v1[k + j, pl.ds(HALO, WIDTH), :]
                acc[3] += folded(own * value)
                acc[4] += folded(value * value)
                put(v2n, k + j, g, y + j, value)

        each_pair(i, run)

    has_before = jnp.where(s > 0, 1.0, 0.0).astype(F32)

    def arrive(i):
        closings[i].wait_recv()
        def run(k, g, y):
            for j in range(2):
                value = v1[k + j, pl.ds(HALO, WIDTH), :] - has_before * arr[k + j]
                put(pun, k + j, g, y + j, value)

        each_pair(i, run)

    second_adjoint(0)
    second_adjoint(1)
    for i in range(3):
        arrive(i)

    @pl.loop(0, 10)
    def _(i):
        rows = pl.ds(pl.multiple_of(i * 256, 256), 256)
        f, d = f_in[rows, :], d_in[rows, :]
        df = f * d
        pu = d * df + pun[rows, :]
        pun[rows, :] = pu
        acc[2] += folded(f * pu)
        acc[3] += folded(df * pu)
        acc[4] += folded(pu * pu)

    exchange_wait(1, obs_s, obs_r)
    right = jnp.concatenate(split2(obs_r[...].reshape(SLOTS, 128)), axis=1)
    seen = halves(jnp.dot(pt_mat[...], right, preferred_element_type=F32))
    pm = weight * (rvar[...] * wrd + seen)
    pm_out[...] = pm
    acc[2] += folded(wd * pm)
    acc[3] += folded(wrd * pm)
    acc[4] += folded(pm * pm)

    second_adjoint(2)

    lines = [jnp.sum(acc[i], axis=0, keepdims=True) for i in range(5)]
    red[...] = jnp.concatenate(lines + [jnp.zeros((3, 128), F32)], axis=0)

    def share(d):
        return rcopy(
            red, redbuf.at[c], a2a_ss.at[2, d], a2a_rs.at[2, d], (s, lax.rem(c + d, n))
        )

    @pl.loop(1, n)
    def _(d):
        share(d).start()

    redbuf[c] = red[...]

    @pl.loop(1, n)
    def _(d):
        peer = lax.rem(c + n - d, n)
        rcopy(red, redbuf.at[peer], a2a_ss.at[2, d], a2a_rs.at[2, d], (s, peer)).wait_recv()

    zred[...] = jnp.sum(redbuf[...], axis=0)

    def share_z(d):
        return rcopy(
            zred, zbuf.at[s], z_ss.at[6 + d], z_rs.at[6 + d], (lax.rem(s + d, nt), c)
        )

    for d in range(1, nt):
        share_z(d).start()
    zbuf[s] = zred[...]
    for d in range(1, nt):
        peer = lax.rem(s + nt - d, nt)
        rcopy(zred, zbuf.at[peer], z_ss.at[6 + d], z_rs.at[6 + d], (peer, c)).wait_recv()

    total = jnp.sum(jnp.sum(zbuf[...], axis=0), axis=1, keepdims=True)
    total = jnp.broadcast_to(total, (8, 128))
    rq, qq, rp, qp, pp = (total[i:i + 1, :] for i in range(5))
    step1 = rq / qq
    step2 = step1 * (step1 * qp - rp) / (qq - 2.0 * step1 * qp + step1 * step1 * pp)
    sc_out[...] = jnp.concatenate(
        [step1 + step2, step1 * step2, jnp.zeros((6, 128), F32)], axis=0
    )

    for i, (src, dst) in enumerate(((send_a, recv_a), (obs_s, obs_r))):
        exchange_sent(i, src, dst)

    @pl.loop(1, n)
    def _(d):
        share(d).wait_send()

    for d in range(1, nt):
        share_z(d).wait_send()
    for copy in [f_halo, d_halo, c_west, c_east, z_edge] + f_send + d_send:
        copy.wait_send()
    for copy in edges + closings:
        copy.wait_send()


def finish_kernel(sc, f_in, d_in, v1, v2, pu, wd_in, wrd_in, pm, ms, rs, xs, mr, rr, xr):
    t, q = sc[0:1, :], sc[1:2, :]
    f, d = f_in[...], d_in[...]
    df = f * d
    ms[...] = t * f - q * df
    mr[...] = f - t * df + q * pu[...]
    v = v1[...]
    xs[...] = -(q * v)
    xr[...] = q * v2[...] - t * v
    wd, wrd = wd_in[...], wrd_in[...]
    rs[...] = t * wd - q * wrd
    rr[...] = wd - t * wrd + q * pm[...]


def to_rows(x):
    a, b, y, w = x.shape
    return x.reshape(a, b, y, w // 128, 128).transpose(0, 1, 3, 2, 4).reshape(-1, 128)


def from_rows(x, shape):
    a, b, y, w = shape
    return x.reshape(a, b, w // 128, y, 128).transpose(0, 1, 3, 2, 4).reshape(shape)


def body(n, nt, forcing_state, model_error, courant, vertical_mix, radiance_jacobian,
         innovation, report_error, report_column, report_slot, report_count):
    f, d, wind = (to_rows(x[0]) for x in (forcing_state, model_error, courant))
    inn, rvar, cnt = innovation[0], report_error[0], report_count[0]
    size = f.shape[0]
    vmem = pl.BlockSpec(memory_space=pltpu.VMEM)
    hbm = pl.BlockSpec(memory_space=pltpu.HBM)
    V = pltpu.VMEM
    state = jax.ShapeDtypeStruct((size, 128), F32)
    reports = jax.ShapeDtypeStruct((ROWS, CHANNELS), F32)
    span, cap = WIDTH + HALO, SLOTS // n
    dma = pltpu.SemaphoreType.DMA
    inputs = (
        f, d, wind, vertical_mix, radiance_jacobian, inn, rvar, report_column, report_slot, cnt,
    )
    inputs = tuple(pltpu.with_memory_space_constraint(x, pltpu.HBM) for x in inputs)
    results = pl.pallas_call(
        functools.partial(system_kernel, n, nt),
        out_shape=(state,) * 5 + (reports,) * 3 + (jax.ShapeDtypeStruct((8, 128), F32),),
        in_specs=[hbm] * 10,
        out_specs=(vmem,) * 9,
        scratch_shapes=[V(x.shape, x.dtype) for x in inputs[2:]] + [
            V((10, WIDTH, 128), F32), V((10, WIDTH, 128), F32),
            V((10, span, 128), F32), V((10, span, 128), F32),
            V((6 * STEPS, span + HALO, 128), F32),
            V((10, span, 128), F32), V((10, WIDTH, 128), F32), V((10, WIDTH, 128), F32),
            V((2, STEPS * LAT, span, 128), F32), V((STEPS * LAT, WIDTH, 128), F32),
            V((STEPS * CELLS, 256), BF16), V((SLOTS, 512), BF16), V((8, SLOTS), F32),
            V((3, 256, 256), BF16), V((3, 256, 256), BF16),
            V((4, 256, 256), BF16), V((4, 256, 256), BF16),
            V((SLOTS, ROWS), BF16), V((ROWS, SLOTS), BF16),
            V((n, 3 * cap, 128), F32), V((n, 3 * cap, 128), F32),
            V((n, cap, 128), F32), V((n, cap, 128), F32),
            V((5, 8, 128), F32), V((8, 128), F32), V((n, 8, 128), F32),
            V((8, 128), F32), V((nt, 8, 128), F32),
            dma((10,)), dma((3, n)), dma((3, n)), dma((6 + nt,)), dma((6 + nt,)),
            dma((5,)), dma((5,)), dma((3,)), dma((3,)), dma((3,)), dma((3,)),
        ],
        compiler_params=pltpu.CompilerParams(
            collective_id=0, has_side_effects=True, vmem_limit_bytes=42 * 1024 * 1024
        ),
        cost_estimate=pl.CostEstimate(flops=40 * 10**9, bytes_accessed=10**7, transcendentals=0),
    )(*inputs)
    fv, dv, v1, v2, pu, wd, wrd, pm, sc = results
    steps = 8
    part = pl.BlockSpec((size // steps, 128), lambda i: (i, 0))
    rpart = pl.BlockSpec((ROWS // steps, CHANNELS), lambda i: (i, 0))
    ms, rs, xs, mr, rr, xr = pl.pallas_call(
        finish_kernel,
        grid=(steps,),
        out_shape=(state, reports, state, state, reports, state),
        in_specs=[pl.BlockSpec((8, 128), lambda i: (0, 0))] + [part] * 5 + [rpart] * 3,
        out_specs=(part, rpart, part, part, rpart, part),
        compiler_params=pltpu.CompilerParams(vmem_limit_bytes=32 * 1024 * 1024),
    )(sc, fv, dv, v1, v2, pu, wd, wrd, pm)
    shape = forcing_state.shape[1:]
    ms, xs, mr, xr = (from_rows(x, shape)[None] for x in (ms, xs, mr, xr))
    return ms, rs[None], xs, mr, rr[None], xr


def solution(mesh):
    grid = P("tm", None, None, None, "col")
    reports = P("tm", "col", None)
    in_specs = (
        grid, grid, grid, P(), P(), reports, reports, P("tm", "col"), P("tm", "col"), reports,
    )
    out_specs = (grid, reports, grid, grid, reports, grid)
    run = functools.partial(body, mesh.shape["col"], mesh.shape["tm"])
    return jax.shard_map(run, mesh=mesh, in_specs=in_specs, out_specs=out_specs, check_vma=False)
```

```python
import functools

import jax
import jax.numpy as jnp
from jax import lax
from jax.experimental import pallas as pl
from jax.experimental.pallas import tpu as pltpu
from jax.sharding import PartitionSpec as P

F32, BF16, I32 = jnp.float32, jnp.bfloat16, jnp.int32
MESH = pl.DeviceIdType.MESH
LEVELS, LAT, WIDTH, STEPS, CHANNELS = 64, 4, 256, 4, 128
ROWS, INST = 512, 4
INST_ROWS = ROWS // INST
SLOTS = 2 * ROWS
CELLS = LAT * WIDTH
HALO, EDGE = 16, 8
LAST = 8
GROUPS = ((0, 4), (4, 4), (8, 2))


def split2(x):
    hi = x.astype(BF16)
    return hi, (x - hi.astype(F32)).astype(BF16)


def pack(w):
    row = jnp.concatenate(split2(w), axis=1)
    return jnp.concatenate([row, row], axis=0)


def halves(o):
    return o[:, :128] + o[:, 128:]


def mm(u, w):
    left = jnp.concatenate(split2(u), axis=1)
    return halves(jnp.dot(left, w, preferred_element_type=F32))


def native_rows(block, y, xt, count):
    return pl.ds(block * LEVELS * 2 * LAT + xt * LAT + y, count, stride=2 * LAT)


def load_pair(ref, g, y, xt):
    return ref[native_rows(2 * g, y, xt, 128), :]


def load_last(ref, y, xt):
    top = ref[native_rows(4, y, xt, 64), :]
    low = ref[native_rows(4, y + 2, xt, 64), :]
    return jnp.concatenate([top, low], axis=0)


def folded(x):
    return jnp.sum(x.reshape(x.shape[0] // 8, 8, 128), axis=0)


def system_kernel(
    n, nt,
    f_hbm, d_hbm, c_hbm, vm_hbm, jac_hbm, inn_hbm, rvar_hbm, col_hbm, slot_hbm, cnt_hbm,
    f_in, d_in, v1n, v2n, pun, wd_out, wrd_out, pm_out, sc_out,
    c_in, vm, jac, inn, rvar, col, slot, cnt,
    f_t, df_t, rf, rd, c_t, v1, closing, arr, z, yacc, ysplit, rowsplit, keyrow, keycol,
    wa, wf, jf, jt, p_mat, pt_mat, send_a, recv_a, send_b, recv_b, obs_s, obs_r,
    acc, red, redbuf, zred, zbuf,
    in_s, a2a_ss, a2a_rs, z_ss, z_rs, h_ss, h_rs, vh_ss, vh_rs, zz_ss, zz_rs,
):
    cap = SLOTS // n
    s, c = lax.axis_index("tm"), lax.axis_index("col")
    prev_s, next_s = lax.rem(s + nt - 1, nt), lax.rem(s + 1, nt)
    west, east = lax.rem(c + n - 1, n), lax.rem(c + 1, n)

    def rcopy(src, dst, ss, rs, to):
        return pltpu.make_async_remote_copy(
            src_ref=src, dst_ref=dst, send_sem=ss, recv_sem=rs, device_id=to, device_id_type=MESH
        )

    def z_send(src, dst, base, to):
        rest = []
        for i, (k0, kn) in enumerate(GROUPS):
            rest.append(
                rcopy(
                    src.at[pl.ds(k0, kn)], dst.at[pl.ds(k0, kn), pl.ds(0, WIDTH)],
                    z_ss.at[base + i], z_rs.at[base + i], to,
                )
            )
        return rest

    def z_halo(src, dst, i):
        return rcopy(
            src.at[:, pl.ds(0, EDGE)], dst.at[:, pl.ds(WIDTH, EDGE)],
            h_ss.at[i], h_rs.at[i], (prev_s, west),
        )

    def exchange(i, src, dst, d):
        peer = lax.rem(c + d, n)
        return rcopy(
            src.at[peer], dst.at[c], a2a_ss.at[i, d], a2a_rs.at[i, d], (s, peer)
        )

    def exchange_start(i, src, dst):
        @pl.loop(1, n)
        def _(d):
            exchange(i, src, dst, d).start()

        dst[c] = src[c]

    def exchange_wait(i, src, dst):
        @pl.loop(1, n)
        def _(d):
            peer = lax.rem(c + n - d, n)
            rcopy(
                src.at[peer], dst.at[peer], a2a_ss.at[i, d], a2a_rs.at[i, d], (s, peer)
            ).wait_recv()

    def exchange_sent(i, src, dst):
        @pl.loop(1, n)
        def _(d):
            exchange(i, src, dst, d).wait_send()

    pairs = (
        (f_hbm, f_in), (col_hbm, col), (slot_hbm, slot), (cnt_hbm, cnt), (inn_hbm, inn),
        (rvar_hbm, rvar), (c_hbm, c_in), (vm_hbm, vm), (jac_hbm, jac), (d_hbm, d_in),
    )
    loads = [pltpu.make_async_copy(a, b, in_s.at[i]) for i, (a, b) in enumerate(pairs)]
    for load in loads:
        load.start()

    barrier = pltpu.get_barrier_semaphore()

    def greet(to):
        pl.semaphore_signal(barrier, inc=1, device_id=to, device_id_type=MESH)

    greet((prev_s, west))
    greet((next_s, east))

    @pl.loop(1, nt)
    def _(d):
        greet((lax.rem(s + d, nt), c))

    @pl.loop(1, n)
    def _(d):
        greet((s, lax.rem(c + d, n)))

    loads[0].wait()

    @pl.loop(0, 8)
    def _(k):
        for xt in range(2):
            f_t[k, pl.ds(xt * 128, 128), :] = load_pair(f_in, k // 4, k % 4, xt).T

    @pl.loop(0, 2)
    def _(y):
        for xt in range(2):
            f_t[8 + y, pl.ds(xt * 128, 128), :] = load_last(f_in, y, xt).T

    rows_iota = lax.broadcasted_iota(I32, (ROWS, ROWS), 0)
    lane_iota = lax.broadcasted_iota(I32, (ROWS, ROWS), 1)
    upper_ones = jnp.where(rows_iota <= lane_iota, 1.0, 0.0).astype(BF16)
    for load in loads[1:4]:
        load.wait()
    column = col[...]
    shift_w, mask_n = WIDTH.bit_length() - 1, n - 1
    owner = (column >> shift_w) & mask_n
    cell = (column >> (shift_w + n.bit_length() - 1)) * WIDTH + (column & (WIDTH - 1))
    key = (slot[...] * CELLS + cell).astype(F32)
    owners = lax.broadcasted_iota(I32, (n, ROWS), 0)
    owned = jnp.where(owners == owner, 1.0, 0.0)
    ranks = jnp.dot(owned.astype(BF16), upper_ones, preferred_element_type=F32)
    landing = jnp.sum(owned * ((owners * cap).astype(F32) + ranks - 1.0), axis=0, keepdims=True)

    def as_column(row, b):
        return jnp.broadcast_to(row[:, b * 128:(b + 1) * 128], (128, 128)).T

    for b in range(SLOTS // 128):
        spots = (lax.broadcasted_iota(I32, (128, ROWS), 0) + b * 128).astype(F32)
        p_mat[b * 128:(b + 1) * 128, :] = jnp.where(spots == landing, 1.0, 0.0).astype(BF16)
    spots = lax.broadcasted_iota(I32, (128, SLOTS), 1).astype(F32)
    for b in range(ROWS // 128):
        land_col = jnp.concatenate([as_column(landing, b)] * (SLOTS // 128), axis=1)
        pt_mat[b * 128:(b + 1) * 128, :] = jnp.where(spots == land_col, 1.0, 0.0).astype(BF16)

    def split3(x):
        hi, rest = x.astype(BF16), x - x.astype(BF16).astype(F32)
        return (hi,) + split2(rest)

    loads[4].wait()
    loads[5].wait()
    inst_iota = lax.broadcasted_iota(I32, (INST_ROWS, CHANNELS), 0)
    weight = jnp.concatenate(
        [jnp.where(inst_iota < cnt[0:1, i:i + 1], 1.0, 0.0) for i in range(INST)], axis=0
    )
    wd = weight * inn[...]
    wrd = weight * (rvar[...] * wd)
    wd_out[...] = wd
    wrd_out[...] = wrd
    right = jnp.concatenate(split3(wd) + split3(wrd), axis=1)
    per, lots = 256 // cap, 128 // cap
    for b in range(4):
        o = jnp.dot(p_mat[b * 256:(b + 1) * 256, :], right, preferred_element_type=F32)
        o = [o[:, i * 128:(i + 1) * 128] for i in range(6)]
        owners_here = slice(b * per, (b + 1) * per)
        send_a[owners_here, 8:, :] = (o[0] + o[1] + o[2]).reshape(per, cap, 128)
        send_b[owners_here, :, :] = (o[3] + o[4] + o[5]).reshape(per, cap, 128)
    keys = 0.0
    for part in split2(jnp.broadcast_to(key, (16, ROWS))):
        keys = keys + lax.dot_general(
            part, p_mat[...], (((1,), (1,)), ((), ())), preferred_element_type=F32
        )
    for o in range(n):
        b = o // lots
        send_a[o, 0:8, :] = keys[0:8, b * 128:(b + 1) * 128]

    pl.semaphore_wait(barrier, n + nt)
    f_halo = z_halo(f_t, rf, 0)
    f_halo.start()
    f_send = z_send(f_t, rf, 0, (prev_s, c))
    for copy in f_send:
        copy.start()
    exchange_start(0, send_a, recv_a)

    acc[...] = jnp.zeros_like(acc)

    loads[6].wait()

    def wind(m, y, xt):
        return c_in[native_rows(m, y, xt, 64), :]

    @pl.loop(0, STEPS * LAT)
    def _(i):
        m, y = i // LAT, i % LAT
        for xt in range(2):
            one = wind(m, y, xt)
            c_t[m * 6 + y, pl.ds(HALO + xt * 128, 128), :] = jnp.concatenate([one, one], axis=0).T

    @pl.loop(0, STEPS * 2)
    def _(i):
        m, y = i // 2, i % 2
        for xt in range(2):
            both = jnp.concatenate([wind(m, y, xt), wind(m, y + 2, xt)], axis=0)
            c_t[m * 6 + 4 + y, pl.ds(HALO + xt * 128, 128), :] = both.T

    c_west = rcopy(
        c_t.at[:, pl.ds(HALO, EDGE)], c_t.at[:, pl.ds(HALO + WIDTH, EDGE)],
        h_ss.at[2], h_rs.at[2], (s, west),
    )
    c_east = rcopy(
        c_t.at[:, pl.ds(WIDTH + HALO - EDGE, EDGE)], c_t.at[:, pl.ds(HALO - EDGE, EDGE)],
        h_ss.at[3], h_rs.at[3], (s, east),
    )
    c_west.start()
    c_east.start()
    exchange_start(3, send_b, recv_b)
    loads[9].wait()

    @pl.loop(0, 8)
    def _(k):
        for xt in range(2):
            g, y = k // 4, k % 4
            df_t[k, pl.ds(xt * 128, 128), :] = (
                load_pair(f_in, g, y, xt) * load_pair(d_in, g, y, xt)
            ).T

    @pl.loop(0, 2)
    def _(y):
        for xt in range(2):
            df_t[8 + y, pl.ds(xt * 128, 128), :] = (
                load_last(f_in, y, xt) * load_last(d_in, y, xt)
            ).T

    d_halo = z_halo(df_t, rd, 1)
    d_halo.start()
    d_send = z_send(df_t, rd, 3, (prev_s, c))
    for copy in d_send:
        copy.start()

    loads[7].wait()
    loads[8].wait()

    eye = jnp.where(
        lax.broadcasted_iota(I32, (64, 64), 0) == lax.broadcasted_iota(I32, (64, 64), 1), 1.0, 0.0
    )
    nothing = jnp.zeros((64, 64), F32)
    for g, (fa, fb) in enumerate(((0, 1), (2, 3), (4, 4))):
        ma, mb = 0.6 * eye + 0.4 * vm[fa], 0.6 * eye + 0.4 * vm[fb]
        block = jnp.concatenate(
            [jnp.concatenate([ma, nothing], axis=1), jnp.concatenate([nothing, mb], axis=1)],
            axis=0,
        )
        wa[g] = pack(block)
        wf[g] = pack(block.T)
    none = jnp.zeros((64, CHANNELS), F32)
    last = jac[256:320, :]
    for g, block in enumerate(
        (
            jac[0:128, :], jac[128:256, :],
            jnp.concatenate([last, none], axis=0), jnp.concatenate([none, last], axis=0),
        )
    ):
        jf[g] = pack(block)
        jt[g] = pack(block.T)

    exchange_wait(0, send_a, recv_a)
    meta = pltpu.roll(recv_a[:, 0, :], lax.rem(128 - cap * lax.rem(c, lots), 128), 1)
    lane = lax.broadcasted_iota(I32, (n, 128), 1)
    meta = jnp.where(lane < cap, meta, 0.0)
    tiled = meta
    for i in range(1, lots):
        tiled = tiled + pltpu.roll(meta, cap * i, 1)
    tiled = jnp.concatenate([tiled] * (SLOTS // 128), axis=1)
    sender = lax.broadcasted_iota(I32, (n, SLOTS), 0)
    place = lax.broadcasted_iota(I32, (n, SLOTS), 1)
    mine = (place >= sender * cap) & (place < sender * cap + cap)
    keyrow[...] = jnp.broadcast_to(
        jnp.sum(jnp.where(mine, tiled, 0.0), axis=0, keepdims=True), (8, SLOTS)
    )

    def scatter(r, rows):
        rowsplit[...] = jnp.concatenate(split2(rows.reshape(SLOTS, 128)), axis=1)

        @pl.loop(0, STEPS * LAT)
        def _(i):
            spot = (lax.broadcasted_iota(I32, (WIDTH, SLOTS), 0) + i * WIDTH).astype(F32)
            hit = jnp.where(spot == keyrow[0:1, :], 1.0, 0.0).astype(BF16)
            o = jnp.dot(hit, rowsplit[...], preferred_element_type=F32)
            z[r, i, pl.ds(0, WIDTH), :] = halves(o)

        edge = rcopy(
            z.at[r, pl.ds(LAT, 3 * LAT), pl.ds(0, EDGE)],
            z.at[r, pl.ds(LAT, 3 * LAT), pl.ds(WIDTH, EDGE)],
            h_ss.at[4 + r], h_rs.at[4 + r], (s, west),
        )
        edge.start()
        return edge

    z_edge1 = scatter(0, recv_a[:, 8:, :])

    @pl.loop(0, SLOTS // 128)
    def _(b):
        lanes = pl.ds(pl.multiple_of(b * 128, 128), 128)
        keycol[lanes, :] = jnp.broadcast_to(keyrow[0:1, lanes], (128, 128)).T

    later = jnp.where(s < nt - 1, -1.0, 0.0).astype(F32)
    span = WIDTH + HALO

    def block(x, first, rows, count):
        return x[pl.ds(first, 2), pl.ds(rows, count), :].reshape(2 * count, 128)

    def adjoint(r, k, g, y, received, own):
        a = block(received, k, 0, span) * later
        wind_at = 4 if k is LAST else y
        for m in reversed(range(STEPS)):
            w = mm(a, wa[g])
            p = block(c_t, m * 6 + wind_at, HALO, span) * w
            if k is LAST:
                inject = mm(block(z.at[r], m * LAT, 0, span), jt[2])
                inject = inject + mm(block(z.at[r], m * LAT + 2, 0, span), jt[3])
            else:
                inject = mm(block(z.at[r], m * LAT + y, 0, span), jt[g])
            a = w - p + pltpu.roll(p, 2 * span - 1, 0) + inject
        a = a.reshape(2, span, 128)
        return [own[k + i] + a[i, 0:WIDTH, :] for i in range(2)]

    def forward(k, g, y):
        v = block(v1, k, 0, span)
        wind_at = 4 if k is LAST else y
        for m in range(STEPS):
            inner = v.reshape(2, span, 128)[:, HALO:, :].reshape(2 * WIDTH, 128)
            if k is LAST:
                yacc[pl.ds(m * LAT, 2)] += mm(inner, jf[2]).reshape(2, WIDTH, 128)
                yacc[pl.ds(m * LAT + 2, 2)] += mm(inner, jf[3]).reshape(2, WIDTH, 128)
            else:
                yacc[pl.ds(m * LAT + y, 2)] += mm(inner, jf[g]).reshape(2, WIDTH, 128)
            wind_now = block(c_t, m * 6 + wind_at, 0, span)
            v = mm(v - wind_now * (v - pltpu.roll(v, 1, 0)), wf[g])
        closing[pl.ds(k, 2)] = v.reshape(2, span, 128)[:, HALO:, :]

    def each_pair(i, run):
        if i < 2:
            @pl.loop(0, 2)
            def _(j):
                run(4 * i + 2 * j, i, 2 * j)
        else:
            run(LAST, 2, 0)

    def put_pair(ref, g, y, value):
        for xt in range(2):
            ref[native_rows(2 * g, y, xt, 128), :] = value[xt * 128:(xt + 1) * 128, :].T

    def put(ref, k, g, y, value):
        if g == 2:
            put_last(ref, y, value)
        else:
            put_pair(ref, g, y, value)

    def put_last(ref, y, value):
        for xt in range(2):
            turned = value[xt * 128:(xt + 1) * 128, :].T
            ref[native_rows(4, y, xt, 64), :] = turned[:64, :]
            ref[native_rows(4, y + 2, xt, 64), :] = turned[64:, :]

    yacc[...] = jnp.zeros_like(yacc)
    c_west.wait_recv()
    c_east.wait_recv()
    f_halo.wait_recv()
    z_edge1.wait_recv()

    def edge_v1(i):
        k0, kn = GROUPS[i]
        return rcopy(
            v1.at[pl.ds(k0, kn), pl.ds(WIDTH + HALO - EDGE, EDGE)],
            v1.at[pl.ds(k0, kn), pl.ds(HALO - EDGE, EDGE)],
            vh_ss.at[i], vh_rs.at[i], (s, east),
        )

    def send_closing(i):
        k0, kn = GROUPS[i]
        return rcopy(
            closing.at[pl.ds(k0, kn)], arr.at[pl.ds(k0, kn)],
            zz_ss.at[i], zz_rs.at[i], (next_s, c),
        )

    edges = [edge_v1(i) for i in range(3)]
    closings = [send_closing(i) for i in range(3)]

    def first_adjoint(i):
        f_send[i].wait_recv()

        def run(k, g, y):
            for j, value in enumerate(adjoint(0, k, g, y, rf, f_t)):
                v1[k + j, pl.ds(HALO, WIDTH), :] = value
                acc[1] += folded(value * value)
                put(v1n, k + j, g, y + j, value)

        each_pair(i, run)
        edges[i].start()

    def first_forward(i):
        edges[i].wait_recv()
        each_pair(i, forward)
        closings[i].start()

    first_adjoint(0)
    exchange_wait(3, send_b, recv_b)
    z_edge2 = scatter(1, recv_b[...])
    first_forward(0)
    first_adjoint(1)

    @pl.loop(0, 10)
    def _(i):
        rows = pl.ds(pl.multiple_of(i * 256, 256), 256)
        f = f_in[rows, :]
        df = f * d_in[rows, :]
        acc[0] += folded(f * df)
        acc[1] += folded(df * df)

    acc[0] += folded(wd * wrd)
    acc[1] += folded(wrd * wrd)

    first_forward(1)
    first_adjoint(2)
    first_forward(2)

    @pl.loop(0, STEPS * LAT)
    def _(i):
        ysplit[pl.ds(pl.multiple_of(i * WIDTH, WIDTH), WIDTH), :] = jnp.concatenate(
            split2(yacc[i]), axis=1
        )

    @pl.loop(0, 4)
    def _(b):
        took = keycol[pl.ds(pl.multiple_of(b * 256, 256), 256), :]
        at = jnp.concatenate([took] * (CELLS // 128), axis=1)
        total = jnp.zeros((256, 256), F32)
        for m in range(STEPS):
            spot = (lax.broadcasted_iota(I32, (256, CELLS), 1) + m * CELLS).astype(F32)
            hit = jnp.where(spot == at, 1.0, 0.0).astype(BF16)
            total = total + jnp.dot(
                hit, ysplit[m * CELLS:(m + 1) * CELLS, :], preferred_element_type=F32
            )
        obs_s[pl.ds(pl.multiple_of(b * per, per), per)] = halves(total).reshape(per, cap, 128)

    exchange_start(1, obs_s, obs_r)

    d_halo.wait_recv()
    z_edge2.wait_recv()

    def second_adjoint(i):
        d_send[i].wait_recv()

        def run(k, g, y):
            for j, value in enumerate(adjoint(1, k, g, y, rd, df_t)):
                own = v1[k + j, pl.ds(HALO, WIDTH), :]
                acc[3] += folded(own * value)
                acc[4] += folded(value * value)
                put(v2n, k + j, g, y + j, value)

        each_pair(i, run)

    has_before = jnp.where(s > 0, 1.0, 0.0).astype(F32)

    def arrive(i):
        closings[i].wait_recv()
        def run(k, g, y):
            for j in range(2):
                value = v1[k + j, pl.ds(HALO, WIDTH), :] - has_before * arr[k + j]
                put(pun, k + j, g, y + j, value)

        each_pair(i, run)

    def upper(i):
        first, count = ((0, 4), (4, 4), (8, 2))[i]

        @pl.loop(first, first + count)
        def _(b):
            rows = pl.ds(pl.multiple_of(b * 256, 256), 256)
            f, d = f_in[rows, :], d_in[rows, :]
            df = f * d
            pu = d * df + pun[rows, :]
            pun[rows, :] = pu
            acc[2] += folded(f * pu)
            acc[3] += folded(df * pu)
            acc[4] += folded(pu * pu)

    arrive(0)
    upper(0)
    second_adjoint(0)
    arrive(1)
    upper(1)
    second_adjoint(1)
    exchange_wait(1, obs_s, obs_r)
    right = jnp.concatenate(split2(obs_r[...].reshape(SLOTS, 128)), axis=1)
    seen = halves(jnp.dot(pt_mat[...], right, preferred_element_type=F32))
    pm = weight * (rvar[...] * wrd + seen)
    pm_out[...] = pm
    acc[2] += folded(wd * pm)
    acc[3] += folded(wrd * pm)
    acc[4] += folded(pm * pm)

    arrive(2)
    upper(2)
    second_adjoint(2)

    lines = [jnp.sum(acc[i], axis=0, keepdims=True) for i in range(5)]
    red[...] = jnp.concatenate(lines + [jnp.zeros((3, 128), F32)], axis=0)

    def share(d):
        return rcopy(
            red, redbuf.at[c], a2a_ss.at[2, d], a2a_rs.at[2, d], (s, lax.rem(c + d, n))
        )

    @pl.loop(1, n)
    def _(d):
        share(d).start()

    redbuf[c] = red[...]

    @pl.loop(1, n)
    def _(d):
        peer = lax.rem(c + n - d, n)
        rcopy(red, redbuf.at[peer], a2a_ss.at[2, d], a2a_rs.at[2, d], (s, peer)).wait_recv()

    zred[...] = jnp.sum(redbuf[...], axis=0)

    def share_z(d):
        return rcopy(
            zred, zbuf.at[s], z_ss.at[6 + d], z_rs.at[6 + d], (lax.rem(s + d, nt), c)
        )

    for d in range(1, nt):
        share_z(d).start()
    zbuf[s] = zred[...]
    for d in range(1, nt):
        peer = lax.rem(s + nt - d, nt)
        rcopy(zred, zbuf.at[peer], z_ss.at[6 + d], z_rs.at[6 + d], (peer, c)).wait_recv()

    total = jnp.sum(jnp.sum(zbuf[...], axis=0), axis=1, keepdims=True)
    total = jnp.broadcast_to(total, (8, 128))
    rq, qq, rp, qp, pp = (total[i:i + 1, :] for i in range(5))
    step1 = rq / qq
    step2 = step1 * (step1 * qp - rp) / (qq - 2.0 * step1 * qp + step1 * step1 * pp)
    sc_out[...] = jnp.concatenate(
        [step1 + step2, step1 * step2, jnp.zeros((6, 128), F32)], axis=0
    )

    for i, src, dst in ((0, send_a, recv_a), (1, obs_s, obs_r), (3, send_b, recv_b)):
        exchange_sent(i, src, dst)

    @pl.loop(1, n)
    def _(d):
        share(d).wait_send()

    for d in range(1, nt):
        share_z(d).wait_send()
    for copy in [f_halo, d_halo, c_west, c_east, z_edge1, z_edge2] + f_send + d_send:
        copy.wait_send()
    for copy in edges + closings:
        copy.wait_send()


def finish_kernel(sc, f_in, d_in, v1, v2, pu, wd_in, wrd_in, pm, ms, rs, xs, mr, rr, xr):
    t, q = sc[0:1, :], sc[1:2, :]
    f, d = f_in[...], d_in[...]
    df = f * d
    ms[...] = t * f - q * df
    mr[...] = f - t * df + q * pu[...]
    v = v1[...]
    xs[...] = -(q * v)
    xr[...] = q * v2[...] - t * v
    wd, wrd = wd_in[...], wrd_in[...]
    rs[...] = t * wd - q * wrd
    rr[...] = wd - t * wrd + q * pm[...]


def to_rows(x):
    a, b, y, w = x.shape
    return x.reshape(a, b, y, w // 128, 128).transpose(0, 1, 3, 2, 4).reshape(-1, 128)


def from_rows(x, shape):
    a, b, y, w = shape
    return x.reshape(a, b, w // 128, y, 128).transpose(0, 1, 3, 2, 4).reshape(shape)


def body(n, nt, forcing_state, model_error, courant, vertical_mix, radiance_jacobian,
         innovation, report_error, report_column, report_slot, report_count):
    f, d, wind = (to_rows(x[0]) for x in (forcing_state, model_error, courant))
    inn, rvar, cnt = innovation[0], report_error[0], report_count[0]
    size = f.shape[0]
    vmem = pl.BlockSpec(memory_space=pltpu.VMEM)
    hbm = pl.BlockSpec(memory_space=pltpu.HBM)
    V = pltpu.VMEM
    state = jax.ShapeDtypeStruct((size, 128), F32)
    reports = jax.ShapeDtypeStruct((ROWS, CHANNELS), F32)
    span, cap = WIDTH + HALO, SLOTS // n
    dma = pltpu.SemaphoreType.DMA
    inputs = (
        f, d, wind, vertical_mix, radiance_jacobian, inn, rvar, report_column, report_slot, cnt,
    )
    inputs = tuple(pltpu.with_memory_space_constraint(x, pltpu.HBM) for x in inputs)
    results = pl.pallas_call(
        functools.partial(system_kernel, n, nt),
        out_shape=(state,) * 5 + (reports,) * 3 + (jax.ShapeDtypeStruct((8, 128), F32),),
        in_specs=[hbm] * 10,
        out_specs=(vmem,) * 9,
        scratch_shapes=[V(x.shape, x.dtype) for x in inputs[2:]] + [
            V((10, WIDTH, 128), F32), V((10, WIDTH, 128), F32),
            V((10, span, 128), F32), V((10, span, 128), F32),
            V((6 * STEPS, span + HALO, 128), F32),
            V((10, span, 128), F32), V((10, WIDTH, 128), F32), V((10, WIDTH, 128), F32),
            V((2, STEPS * LAT, span, 128), F32), V((STEPS * LAT, WIDTH, 128), F32),
            V((STEPS * CELLS, 256), BF16), V((SLOTS, 256), BF16), V((8, SLOTS), F32), V((SLOTS, 128), F32),
            V((3, 256, 256), BF16), V((3, 256, 256), BF16),
            V((4, 256, 256), BF16), V((4, 256, 256), BF16),
            V((SLOTS, ROWS), BF16), V((ROWS, SLOTS), BF16),
            V((n, 8 + cap, 128), F32), V((n, 8 + cap, 128), F32),
            V((n, cap, 128), F32), V((n, cap, 128), F32),
            V((n, cap, 128), F32), V((n, cap, 128), F32),
            V((5, 8, 128), F32), V((8, 128), F32), V((n, 8, 128), F32),
            V((8, 128), F32), V((nt, 8, 128), F32),
            dma((10,)), dma((4, n)), dma((4, n)), dma((6 + nt,)), dma((6 + nt,)),
            dma((6,)), dma((6,)), dma((3,)), dma((3,)), dma((3,)), dma((3,)),
        ],
        compiler_params=pltpu.CompilerParams(
            collective_id=0, has_side_effects=True, vmem_limit_bytes=42 * 1024 * 1024
        ),
        cost_estimate=pl.CostEstimate(flops=40 * 10**9, bytes_accessed=10**7, transcendentals=0),
    )(*inputs)
    fv, dv, v1, v2, pu, wd, wrd, pm, sc = results
    steps = 8
    part = pl.BlockSpec((size // steps, 128), lambda i: (i, 0))
    rpart = pl.BlockSpec((ROWS // steps, CHANNELS), lambda i: (i, 0))
    ms, rs, xs, mr, rr, xr = pl.pallas_call(
        finish_kernel,
        grid=(steps,),
        out_shape=(state, reports, state, state, reports, state),
        in_specs=[pl.BlockSpec((8, 128), lambda i: (0, 0))] + [part] * 5 + [rpart] * 3,
        out_specs=(part, rpart, part, part, rpart, part),
        compiler_params=pltpu.CompilerParams(vmem_limit_bytes=32 * 1024 * 1024),
    )(sc, fv, dv, v1, v2, pu, wd, wrd, pm)
    shape = forcing_state.shape[1:]
    ms, xs, mr, xr = (from_rows(x, shape)[None] for x in (ms, xs, mr, xr))
    return ms, rs[None], xs, mr, rr[None], xr


def solution(mesh):
    grid = P("tm", None, None, None, "col")
    reports = P("tm", "col", None)
    in_specs = (
        grid, grid, grid, P(), P(), reports, reports, P("tm", "col"), P("tm", "col"), reports,
    )
    out_specs = (grid, reports, grid, grid, reports, grid)
    run = functools.partial(body, mesh.shape["col"], mesh.shape["tm"])
    return jax.shard_map(run, mesh=mesh, in_specs=in_specs, out_specs=out_specs, check_vma=False)
```

```python
import functools

import jax
import jax.numpy as jnp
from jax import lax
from jax.experimental import pallas as pl
from jax.experimental.pallas import tpu as pltpu
from jax.sharding import PartitionSpec as P

F32, BF16, I32 = jnp.float32, jnp.bfloat16, jnp.int32
MESH = pl.DeviceIdType.MESH
LEVELS, LAT, WIDTH, STEPS, CHANNELS = 64, 4, 256, 4, 128
ROWS, INST = 512, 4
INST_ROWS = ROWS // INST
SLOTS = 2 * ROWS
CELLS = LAT * WIDTH
HALO, EDGE = 16, 8
INNER = 8
LAST = 8
GROUPS = ((0, 4), (4, 4), (8, 2))


def split2(x):
    hi = x.astype(BF16)
    return hi, (x - hi.astype(F32)).astype(BF16)


def pack(w):
    row = jnp.concatenate(split2(w), axis=1)
    return jnp.concatenate([row, row], axis=0)


def halves(o):
    return o[:, :128] + o[:, 128:]


def mm(u, w):
    left = jnp.concatenate(split2(u), axis=1)
    return halves(jnp.dot(left, w, preferred_element_type=F32))


def native_rows(block, y, xt, count):
    return pl.ds(block * LEVELS * 2 * LAT + xt * LAT + y, count, stride=2 * LAT)


def load_pair(ref, g, y, xt):
    return ref[native_rows(2 * g, y, xt, 128), :]


def load_last(ref, y, xt):
    top = ref[native_rows(4, y, xt, 64), :]
    low = ref[native_rows(4, y + 2, xt, 64), :]
    return jnp.concatenate([top, low], axis=0)


def folded(x):
    return jnp.sum(x.reshape(x.shape[0] // 8, 8, 128), axis=0)


def system_kernel(
    n, nt,
    f_hbm, d_hbm, c_hbm, vm_hbm, jac_hbm, inn_hbm, rvar_hbm, col_hbm, slot_hbm, cnt_hbm,
    f_in, d_in, v1n, v2n, pun, wd_out, wrd_out, pm_out, sc_out,
    c_in, vm, jac, inn, rvar, col, slot, cnt,
    f_t, df_t, rf, rd, c_t, v1, closing, arr, z, yacc, ysplit, rowsplit, keyrow, keycol,
    wa, wf, jf, jt, p_mat, pt_mat, send_a, recv_a, send_b, recv_b, obs_s, obs_r,
    acc, red, redbuf, zred, zbuf,
    in_s, a2a_ss, a2a_rs, z_ss, z_rs, h_ss, h_rs, vh_ss, vh_rs, zz_ss, zz_rs, r_ss, r_rs,
):
    cap = SLOTS // n
    s, c = lax.axis_index("tm"), lax.axis_index("col")
    prev_s, next_s = lax.rem(s + nt - 1, nt), lax.rem(s + 1, nt)
    west, east = lax.rem(c + n - 1, n), lax.rem(c + 1, n)

    def rcopy(src, dst, ss, rs, to):
        return pltpu.make_async_remote_copy(
            src_ref=src, dst_ref=dst, send_sem=ss, recv_sem=rs, device_id=to, device_id_type=MESH
        )

    def z_send(src, dst, base, to):
        rest = []
        for i, (k0, kn) in enumerate(GROUPS):
            rest.append(
                rcopy(
                    src.at[pl.ds(k0, kn)], dst.at[pl.ds(k0, kn), pl.ds(0, WIDTH)],
                    z_ss.at[base + i], z_rs.at[base + i], to,
                )
            )
        return rest

    def z_halo(src, dst, i):
        return rcopy(
            src.at[:, pl.ds(0, EDGE)], dst.at[:, pl.ds(WIDTH, EDGE)],
            h_ss.at[i], h_rs.at[i], (prev_s, west),
        )

    def exchange(i, src, dst, d):
        peer = lax.rem(c + d, n)
        return rcopy(
            src.at[peer], dst.at[c], a2a_ss.at[i, d], a2a_rs.at[i, d], (s, peer)
        )

    def exchange_start(i, src, dst):
        @pl.loop(1, n)
        def _(d):
            exchange(i, src, dst, d).start()

        dst[c] = src[c]

    def exchange_wait(i, src, dst):
        @pl.loop(1, n)
        def _(d):
            peer = lax.rem(c + n - d, n)
            rcopy(
                src.at[peer], dst.at[peer], a2a_ss.at[i, d], a2a_rs.at[i, d], (s, peer)
            ).wait_recv()

    def exchange_sent(i, src, dst):
        @pl.loop(1, n)
        def _(d):
            exchange(i, src, dst, d).wait_send()

    pairs = (
        (f_hbm, f_in), (col_hbm, col), (slot_hbm, slot), (cnt_hbm, cnt), (inn_hbm, inn),
        (rvar_hbm, rvar), (c_hbm, c_in), (vm_hbm, vm), (jac_hbm, jac), (d_hbm, d_in),
    )
    loads = [pltpu.make_async_copy(a, b, in_s.at[i]) for i, (a, b) in enumerate(pairs)]
    for load in loads:
        load.start()

    barrier = pltpu.get_barrier_semaphore()

    def greet(to):
        pl.semaphore_signal(barrier, inc=1, device_id=to, device_id_type=MESH)

    greet((prev_s, west))
    greet((next_s, east))

    @pl.loop(1, nt)
    def _(d):
        greet((lax.rem(s + d, nt), c))

        @pl.loop(1, n // INNER)
        def _(e):
            greet((lax.rem(s + d, nt), lax.rem(c + e * INNER, n)))

    @pl.loop(1, n)
    def _(d):
        greet((s, lax.rem(c + d, n)))

    loads[0].wait()

    @pl.loop(0, 8)
    def _(k):
        for xt in range(2):
            f_t[k, pl.ds(xt * 128, 128), :] = load_pair(f_in, k // 4, k % 4, xt).T

    @pl.loop(0, 2)
    def _(y):
        for xt in range(2):
            f_t[8 + y, pl.ds(xt * 128, 128), :] = load_last(f_in, y, xt).T

    pl.semaphore_wait(barrier, n + nt + (nt - 1) * (n // INNER - 1))
    f_halo = z_halo(f_t, rf, 0)
    f_halo.start()
    f_send = z_send(f_t, rf, 0, (prev_s, c))
    for i in (2, 0, 1):
        f_send[i].start()

    rows_iota = lax.broadcasted_iota(I32, (ROWS, ROWS), 0)
    lane_iota = lax.broadcasted_iota(I32, (ROWS, ROWS), 1)
    upper_ones = jnp.where(rows_iota <= lane_iota, 1.0, 0.0).astype(BF16)
    for load in loads[1:4]:
        load.wait()
    column = col[...]
    shift_w, mask_n = WIDTH.bit_length() - 1, n - 1
    owner = (column >> shift_w) & mask_n
    cell = (column >> (shift_w + n.bit_length() - 1)) * WIDTH + (column & (WIDTH - 1))
    key = (slot[...] * CELLS + cell).astype(F32)
    owners = lax.broadcasted_iota(I32, (n, ROWS), 0)
    owned = jnp.where(owners == owner, 1.0, 0.0)
    ranks = jnp.dot(owned.astype(BF16), upper_ones, preferred_element_type=F32)
    landing = jnp.sum(owned * ((owners * cap).astype(F32) + ranks - 1.0), axis=0, keepdims=True)

    def as_column(row, b):
        return jnp.broadcast_to(row[:, b * 128:(b + 1) * 128], (128, 128)).T

    for b in range(SLOTS // 128):
        spots = (lax.broadcasted_iota(I32, (128, ROWS), 0) + b * 128).astype(F32)
        p_mat[b * 128:(b + 1) * 128, :] = jnp.where(spots == landing, 1.0, 0.0).astype(BF16)
    spots = lax.broadcasted_iota(I32, (128, SLOTS), 1).astype(F32)
    for b in range(ROWS // 128):
        land_col = jnp.concatenate([as_column(landing, b)] * (SLOTS // 128), axis=1)
        pt_mat[b * 128:(b + 1) * 128, :] = jnp.where(spots == land_col, 1.0, 0.0).astype(BF16)

    def split3(x):
        hi, rest = x.astype(BF16), x - x.astype(BF16).astype(F32)
        return (hi,) + split2(rest)

    loads[4].wait()
    loads[5].wait()
    inst_iota = lax.broadcasted_iota(I32, (INST_ROWS, CHANNELS), 0)
    weight = jnp.concatenate(
        [jnp.where(inst_iota < cnt[0:1, i:i + 1], 1.0, 0.0) for i in range(INST)], axis=0
    )
    wd = weight * inn[...]
    wrd = weight * (rvar[...] * wd)
    wd_out[...] = wd
    wrd_out[...] = wrd
    right = jnp.concatenate(split3(wd) + split3(wrd), axis=1)
    per, lots = 256 // cap, 128 // cap
    for b in range(4):
        o = jnp.dot(p_mat[b * 256:(b + 1) * 256, :], right, preferred_element_type=F32)
        o = [o[:, i * 128:(i + 1) * 128] for i in range(6)]
        owners_here = slice(b * per, (b + 1) * per)
        send_a[owners_here, 8:, :] = (o[0] + o[1] + o[2]).reshape(per, cap, 128)
        send_b[owners_here, :, :] = (o[3] + o[4] + o[5]).reshape(per, cap, 128)
    keys = 0.0
    for part in split2(jnp.broadcast_to(key, (16, ROWS))):
        keys = keys + lax.dot_general(
            part, p_mat[...], (((1,), (1,)), ((), ())), preferred_element_type=F32
        )
    for o in range(n):
        b = o // lots
        send_a[o, 0:8, :] = keys[0:8, b * 128:(b + 1) * 128]

    exchange_start(0, send_a, recv_a)

    acc[...] = jnp.zeros_like(acc)

    loads[6].wait()

    def wind(m, y, xt):
        return c_in[native_rows(m, y, xt, 64), :]

    @pl.loop(0, STEPS * LAT)
    def _(i):
        m, y = i // LAT, i % LAT
        for xt in range(2):
            one = wind(m, y, xt)
            c_t[m * 6 + y, pl.ds(HALO + xt * 128, 128), :] = jnp.concatenate([one, one], axis=0).T

    @pl.loop(0, STEPS * 2)
    def _(i):
        m, y = i // 2, i % 2
        for xt in range(2):
            both = jnp.concatenate([wind(m, y, xt), wind(m, y + 2, xt)], axis=0)
            c_t[m * 6 + 4 + y, pl.ds(HALO + xt * 128, 128), :] = both.T

    c_west = rcopy(
        c_t.at[:, pl.ds(HALO, EDGE)], c_t.at[:, pl.ds(HALO + WIDTH, EDGE)],
        h_ss.at[2], h_rs.at[2], (s, west),
    )
    c_east = rcopy(
        c_t.at[:, pl.ds(WIDTH + HALO - EDGE, EDGE)], c_t.at[:, pl.ds(HALO - EDGE, EDGE)],
        h_ss.at[3], h_rs.at[3], (s, east),
    )
    c_west.start()
    c_east.start()
    exchange_start(3, send_b, recv_b)
    loads[9].wait()

    @pl.loop(0, 8)
    def _(k):
        for xt in range(2):
            g, y = k // 4, k % 4
            df_t[k, pl.ds(xt * 128, 128), :] = (
                load_pair(f_in, g, y, xt) * load_pair(d_in, g, y, xt)
            ).T

    @pl.loop(0, 2)
    def _(y):
        for xt in range(2):
            df_t[8 + y, pl.ds(xt * 128, 128), :] = (
                load_last(f_in, y, xt) * load_last(d_in, y, xt)
            ).T

    d_halo = z_halo(df_t, rd, 1)
    d_halo.start()
    d_send = z_send(df_t, rd, 3, (prev_s, c))
    for copy in d_send:
        copy.start()

    loads[7].wait()
    loads[8].wait()

    eye = jnp.where(
        lax.broadcasted_iota(I32, (64, 64), 0) == lax.broadcasted_iota(I32, (64, 64), 1), 1.0, 0.0
    )
    nothing = jnp.zeros((64, 64), F32)
    for g, (fa, fb) in enumerate(((0, 1), (2, 3), (4, 4))):
        ma, mb = 0.6 * eye + 0.4 * vm[fa], 0.6 * eye + 0.4 * vm[fb]
        block = jnp.concatenate(
            [jnp.concatenate([ma, nothing], axis=1), jnp.concatenate([nothing, mb], axis=1)],
            axis=0,
        )
        wa[g] = pack(block)
        wf[g] = pack(block.T)
    none = jnp.zeros((64, CHANNELS), F32)
    last = jac[256:320, :]
    for g, block in enumerate(
        (
            jac[0:128, :], jac[128:256, :],
            jnp.concatenate([last, none], axis=0), jnp.concatenate([none, last], axis=0),
        )
    ):
        jf[g] = pack(block)
        jt[g] = pack(block.T)

    exchange_wait(0, send_a, recv_a)
    meta = pltpu.roll(recv_a[:, 0, :], lax.rem(128 - cap * lax.rem(c, lots), 128), 1)
    lane = lax.broadcasted_iota(I32, (n, 128), 1)
    meta = jnp.where(lane < cap, meta, 0.0)
    tiled = meta
    for i in range(1, lots):
        tiled = tiled + pltpu.roll(meta, cap * i, 1)
    tiled = jnp.concatenate([tiled] * (SLOTS // 128), axis=1)
    sender = lax.broadcasted_iota(I32, (n, SLOTS), 0)
    place = lax.broadcasted_iota(I32, (n, SLOTS), 1)
    mine = (place >= sender * cap) & (place < sender * cap + cap)
    keyrow[...] = jnp.broadcast_to(
        jnp.sum(jnp.where(mine, tiled, 0.0), axis=0, keepdims=True), (8, SLOTS)
    )

    def scatter(r, rows):
        rowsplit[...] = jnp.concatenate(split2(rows.reshape(SLOTS, 128)), axis=1)

        @pl.loop(0, STEPS * LAT)
        def _(i):
            spot = (lax.broadcasted_iota(I32, (WIDTH, SLOTS), 0) + i * WIDTH).astype(F32)
            hit = jnp.where(spot == keyrow[0:1, :], 1.0, 0.0).astype(BF16)
            o = jnp.dot(hit, rowsplit[...], preferred_element_type=F32)
            z[r, i, pl.ds(0, WIDTH), :] = halves(o)

        edge = rcopy(
            z.at[r, pl.ds(LAT, 3 * LAT), pl.ds(0, EDGE)],
            z.at[r, pl.ds(LAT, 3 * LAT), pl.ds(WIDTH, EDGE)],
            h_ss.at[4 + r], h_rs.at[4 + r], (s, west),
        )
        edge.start()
        return edge

    z_edge1 = scatter(0, recv_a[:, 8:, :])

    @pl.loop(0, SLOTS // 128)
    def _(b):
        lanes = pl.ds(pl.multiple_of(b * 128, 128), 128)
        keycol[lanes, :] = jnp.broadcast_to(keyrow[0:1, lanes], (128, 128)).T

    later = jnp.where(s < nt - 1, -1.0, 0.0).astype(F32)
    span = WIDTH + HALO

    def block(x, first, rows, count):
        return x[pl.ds(first, 2), pl.ds(rows, count), :].reshape(2 * count, 128)

    def adjoint(r, k, g, y, received, own):
        a = block(received, k, 0, span) * later
        wind_at = 4 if k is LAST else y
        for m in reversed(range(STEPS)):
            w = mm(a, wa[g])
            p = block(c_t, m * 6 + wind_at, HALO, span) * w
            if k is LAST:
                inject = mm(block(z.at[r], m * LAT, 0, span), jt[2])
                inject = inject + mm(block(z.at[r], m * LAT + 2, 0, span), jt[3])
            else:
                inject = mm(block(z.at[r], m * LAT + y, 0, span), jt[g])
            a = w - p + pltpu.roll(p, 2 * span - 1, 0) + inject
        a = a.reshape(2, span, 128)
        return [own[k + i] + a[i, 0:WIDTH, :] for i in range(2)]

    def forward(k, g, y):
        v = block(v1, k, 0, span)
        wind_at = 4 if k is LAST else y
        for m in range(STEPS):
            inner = v.reshape(2, span, 128)[:, HALO:, :].reshape(2 * WIDTH, 128)
            if k is LAST:
                yacc[pl.ds(m * LAT, 2)] += mm(inner, jf[2]).reshape(2, WIDTH, 128)
                yacc[pl.ds(m * LAT + 2, 2)] += mm(inner, jf[3]).reshape(2, WIDTH, 128)
            else:
                yacc[pl.ds(m * LAT + y, 2)] += mm(inner, jf[g]).reshape(2, WIDTH, 128)
            wind_now = block(c_t, m * 6 + wind_at, 0, span)
            v = mm(v - wind_now * (v - pltpu.roll(v, 1, 0)), wf[g])
        closing[pl.ds(k, 2)] = v.reshape(2, span, 128)[:, HALO:, :]

    def each_pair(i, run):
        if i < 2:
            @pl.loop(0, 2)
            def _(j):
                run(4 * i + 2 * j, i, 2 * j)
        else:
            run(LAST, 2, 0)

    def put_pair(ref, g, y, value):
        for xt in range(2):
            ref[native_rows(2 * g, y, xt, 128), :] = value[xt * 128:(xt + 1) * 128, :].T

    def put(ref, k, g, y, value):
        if g == 2:
            put_last(ref, y, value)
        else:
            put_pair(ref, g, y, value)

    def put_last(ref, y, value):
        for xt in range(2):
            turned = value[xt * 128:(xt + 1) * 128, :].T
            ref[native_rows(4, y, xt, 64), :] = turned[:64, :]
            ref[native_rows(4, y + 2, xt, 64), :] = turned[64:, :]

    yacc[...] = jnp.zeros_like(yacc)
    c_west.wait_recv()
    c_east.wait_recv()
    f_halo.wait_recv()
    z_edge1.wait_recv()

    def edge_v1(i):
        k0, kn = GROUPS[i]
        return rcopy(
            v1.at[pl.ds(k0, kn), pl.ds(WIDTH + HALO - EDGE, EDGE)],
            v1.at[pl.ds(k0, kn), pl.ds(HALO - EDGE, EDGE)],
            vh_ss.at[i], vh_rs.at[i], (s, east),
        )

    def send_closing(i):
        k0, kn = GROUPS[i]
        return rcopy(
            closing.at[pl.ds(k0, kn)], arr.at[pl.ds(k0, kn)],
            zz_ss.at[i], zz_rs.at[i], (next_s, c),
        )

    edges = [edge_v1(i) for i in range(3)]
    closings = [send_closing(i) for i in range(3)]

    def first_adjoint(i):
        f_send[i].wait_recv()

        def run(k, g, y):
            for j, value in enumerate(adjoint(0, k, g, y, rf, f_t)):
                v1[k + j, pl.ds(HALO, WIDTH), :] = value
                acc[1] += folded(value * value)
                put(v1n, k + j, g, y + j, value)

        each_pair(i, run)
        edges[i].start()

    def first_forward(i):
        edges[i].wait_recv()
        each_pair(i, forward)
        closings[i].start()

    first_adjoint(2)
    first_adjoint(0)
    first_forward(2)
    first_forward(0)
    exchange_wait(3, send_b, recv_b)
    z_edge2 = scatter(1, recv_b[...])
    first_adjoint(1)

    @pl.loop(0, 10)
    def _(i):
        rows = pl.ds(pl.multiple_of(i * 256, 256), 256)
        f = f_in[rows, :]
        df = f * d_in[rows, :]
        acc[0] += folded(f * df)
        acc[1] += folded(df * df)

    acc[0] += folded(wd * wrd)
    acc[1] += folded(wrd * wrd)

    first_forward(1)

    @pl.loop(0, STEPS * LAT)
    def _(i):
        ysplit[pl.ds(pl.multiple_of(i * WIDTH, WIDTH), WIDTH), :] = jnp.concatenate(
            split2(yacc[i]), axis=1
        )

    @pl.loop(0, 4)
    def _(b):
        took = keycol[pl.ds(pl.multiple_of(b * 256, 256), 256), :]
        at = jnp.concatenate([took] * (CELLS // 128), axis=1)
        total = jnp.zeros((256, 256), F32)
        for m in range(STEPS):
            spot = (lax.broadcasted_iota(I32, (256, CELLS), 1) + m * CELLS).astype(F32)
            hit = jnp.where(spot == at, 1.0, 0.0).astype(BF16)
            total = total + jnp.dot(
                hit, ysplit[m * CELLS:(m + 1) * CELLS, :], preferred_element_type=F32
            )
        obs_s[pl.ds(pl.multiple_of(b * per, per), per)] = halves(total).reshape(per, cap, 128)

    exchange_start(1, obs_s, obs_r)

    d_halo.wait_recv()
    z_edge2.wait_recv()

    def second_adjoint(i):
        d_send[i].wait_recv()

        def run(k, g, y):
            for j, value in enumerate(adjoint(1, k, g, y, rd, df_t)):
                own = v1[k + j, pl.ds(HALO, WIDTH), :]
                acc[3] += folded(own * value)
                acc[4] += folded(value * value)
                put(v2n, k + j, g, y + j, value)

        each_pair(i, run)

    has_before = jnp.where(s > 0, 1.0, 0.0).astype(F32)

    def arrive(i):
        closings[i].wait_recv()
        def run(k, g, y):
            for j in range(2):
                value = v1[k + j, pl.ds(HALO, WIDTH), :] - has_before * arr[k + j]
                put(pun, k + j, g, y + j, value)

        each_pair(i, run)

    def upper(i):
        first, count = ((0, 4), (4, 4), (8, 2))[i]

        @pl.loop(first, first + count)
        def _(b):
            rows = pl.ds(pl.multiple_of(b * 256, 256), 256)
            f, d = f_in[rows, :], d_in[rows, :]
            df = f * d
            pu = d * df + pun[rows, :]
            pun[rows, :] = pu
            acc[2] += folded(f * pu)
            acc[3] += folded(df * pu)
            acc[4] += folded(pu * pu)

    arrive(2)
    upper(2)
    second_adjoint(0)
    arrive(0)
    upper(0)
    second_adjoint(1)
    exchange_wait(1, obs_s, obs_r)
    right = jnp.concatenate(split2(obs_r[...].reshape(SLOTS, 128)), axis=1)
    seen = halves(jnp.dot(pt_mat[...], right, preferred_element_type=F32))
    pm = weight * (rvar[...] * wrd + seen)
    pm_out[...] = pm
    acc[2] += folded(wd * pm)
    acc[3] += folded(wrd * pm)
    acc[4] += folded(pm * pm)

    arrive(1)
    upper(1)
    second_adjoint(2)

    lines = [jnp.sum(acc[i], axis=0, keepdims=True) for i in range(5)]
    red[...] = jnp.concatenate(lines + [jnp.zeros((3, 128), F32)], axis=0)

    place_in, place_out = lax.rem(c, INNER), s * (n // INNER) + c // INNER
    first = c - place_in

    def share(d):
        to = lax.rem(place_in + d, INNER)
        return rcopy(red, redbuf.at[place_in], r_ss.at[d], r_rs.at[d], (s, first + to))

    for d in range(1, INNER):
        share(d).start()
    redbuf[place_in] = red[...]
    for d in range(1, INNER):
        peer = lax.rem(place_in + INNER - d, INNER)
        rcopy(red, redbuf.at[peer], r_ss.at[d], r_rs.at[d], (s, first + peer)).wait_recv()
    zred[...] = jnp.sum(redbuf[...], axis=0)
    outer = n * nt // INNER

    def share_out(d):
        to = lax.rem(place_out + d, outer)
        where = (to // (n // INNER), lax.rem(to, n // INNER) * INNER + place_in)
        return rcopy(
            zred, zbuf.at[place_out], r_ss.at[INNER + d], r_rs.at[INNER + d], where
        )

    for d in range(1, outer):
        share_out(d).start()
    zbuf[place_out] = zred[...]
    for d in range(1, outer):
        peer = lax.rem(place_out + outer - d, outer)
        where = (peer // (n // INNER), lax.rem(peer, n // INNER) * INNER + place_in)
        rcopy(zred, zbuf.at[peer], r_ss.at[INNER + d], r_rs.at[INNER + d], where).wait_recv()

    total = jnp.sum(jnp.sum(zbuf[...], axis=0), axis=1, keepdims=True)
    total = jnp.broadcast_to(total, (8, 128))
    rq, qq, rp, qp, pp = (total[i:i + 1, :] for i in range(5))
    step1 = rq / qq
    step2 = step1 * (step1 * qp - rp) / (qq - 2.0 * step1 * qp + step1 * step1 * pp)
    sc_out[...] = jnp.concatenate(
        [step1 + step2, step1 * step2, jnp.zeros((6, 128), F32)], axis=0
    )

    for i, src, dst in ((0, send_a, recv_a), (1, obs_s, obs_r), (3, send_b, recv_b)):
        exchange_sent(i, src, dst)

    for d in range(1, INNER):
        share(d).wait_send()
    for d in range(1, outer):
        share_out(d).wait_send()
    for copy in [f_halo, d_halo, c_west, c_east, z_edge1, z_edge2] + f_send + d_send:
        copy.wait_send()
    for copy in edges + closings:
        copy.wait_send()


def finish_kernel(
    sc, f_in, d_in, v1, v2, pu, wd_in, wrd_in, pm,
    ms_out, rs_out, xs_out, mr_out, rr_out, xr_out,
    ms, rs, xs, mr, rr, xr, sem,
):
    t, q = sc[0:1, :], sc[1:2, :]
    parts = 5
    size = ms.shape[0] // parts
    copies = []

    def send(i, src, dst):
        copy = pltpu.make_async_copy(src, dst, sem.at[i])
        copy.start()
        copies.append(copy)

    for i in range(parts):
        rows = pl.ds(i * size, size)
        f, v = f_in[rows, :], v1[rows, :]
        df = f * d_in[rows, :]
        ms[rows, :] = t * f - q * df
        mr[rows, :] = f - t * df + q * pu[rows, :]
        xs[rows, :] = -(q * v)
        xr[rows, :] = q * v2[rows, :] - t * v
        for j, (src, dst) in enumerate(
            ((ms, ms_out), (mr, mr_out), (xs, xs_out), (xr, xr_out))
        ):
            send(4 * i + j, src.at[rows, :], dst.at[rows, :])
    wd, wrd = wd_in[...], wrd_in[...]
    rs[...] = t * wd - q * wrd
    rr[...] = wd - t * wrd + q * pm[...]
    send(4 * parts, rs, rs_out)
    send(4 * parts + 1, rr, rr_out)
    for copy in copies:
        copy.wait()


def to_rows(x):
    a, b, y, w = x.shape
    return x.reshape(a, b, y, w // 128, 128).transpose(0, 1, 3, 2, 4).reshape(-1, 128)


def from_rows(x, shape):
    a, b, y, w = shape
    return x.reshape(a, b, w // 128, y, 128).transpose(0, 1, 3, 2, 4).reshape(shape)


def body(n, nt, forcing_state, model_error, courant, vertical_mix, radiance_jacobian,
         innovation, report_error, report_column, report_slot, report_count):
    f, d, wind = (to_rows(x[0]) for x in (forcing_state, model_error, courant))
    inn, rvar, cnt = innovation[0], report_error[0], report_count[0]
    size = f.shape[0]
    vmem = pl.BlockSpec(memory_space=pltpu.VMEM)
    hbm = pl.BlockSpec(memory_space=pltpu.HBM)
    V = pltpu.VMEM
    state = jax.ShapeDtypeStruct((size, 128), F32)
    reports = jax.ShapeDtypeStruct((ROWS, CHANNELS), F32)
    span, cap = WIDTH + HALO, SLOTS // n
    dma = pltpu.SemaphoreType.DMA
    inputs = (
        f, d, wind, vertical_mix, radiance_jacobian, inn, rvar, report_column, report_slot, cnt,
    )
    inputs = tuple(pltpu.with_memory_space_constraint(x, pltpu.HBM) for x in inputs)
    results = pl.pallas_call(
        functools.partial(system_kernel, n, nt),
        out_shape=(state,) * 5 + (reports,) * 3 + (jax.ShapeDtypeStruct((8, 128), F32),),
        in_specs=[hbm] * 10,
        out_specs=(vmem,) * 9,
        scratch_shapes=[V(x.shape, x.dtype) for x in inputs[2:]] + [
            V((10, WIDTH, 128), F32), V((10, WIDTH, 128), F32),
            V((10, span, 128), F32), V((10, span, 128), F32),
            V((6 * STEPS, span + HALO, 128), F32),
            V((10, span, 128), F32), V((10, WIDTH, 128), F32), V((10, WIDTH, 128), F32),
            V((2, STEPS * LAT, span, 128), F32), V((STEPS * LAT, WIDTH, 128), F32),
            V((STEPS * CELLS, 256), BF16), V((SLOTS, 256), BF16), V((8, SLOTS), F32), V((SLOTS, 128), F32),
            V((3, 256, 256), BF16), V((3, 256, 256), BF16),
            V((4, 256, 256), BF16), V((4, 256, 256), BF16),
            V((SLOTS, ROWS), BF16), V((ROWS, SLOTS), BF16),
            V((n, 8 + cap, 128), F32), V((n, 8 + cap, 128), F32),
            V((n, cap, 128), F32), V((n, cap, 128), F32),
            V((n, cap, 128), F32), V((n, cap, 128), F32),
            V((5, 8, 128), F32), V((8, 128), F32), V((INNER, 8, 128), F32),
            V((8, 128), F32), V((n * nt // INNER, 8, 128), F32),
            dma((10,)), dma((4, n)), dma((4, n)), dma((6,)), dma((6,)),
            dma((6,)), dma((6,)), dma((3,)), dma((3,)), dma((3,)), dma((3,)),
            dma((INNER + n * nt // INNER,)), dma((INNER + n * nt // INNER,)),
        ],
        compiler_params=pltpu.CompilerParams(
            collective_id=0, has_side_effects=True, vmem_limit_bytes=42 * 1024 * 1024
        ),
        cost_estimate=pl.CostEstimate(flops=40 * 10**9, bytes_accessed=10**7, transcendentals=0),
    )(*inputs)
    fv, dv, v1, v2, pu, wd, wrd, pm, sc = results
    outs = (state, reports, state, state, reports, state)
    ms, rs, xs, mr, rr, xr = pl.pallas_call(
        finish_kernel,
        out_shape=outs,
        in_specs=[vmem] * 9,
        out_specs=(pl.BlockSpec(memory_space=pl.ANY),) * 6,
        scratch_shapes=[V(x.shape, x.dtype) for x in outs] + [dma((22,))],
        compiler_params=pltpu.CompilerParams(vmem_limit_bytes=16 * 1024 * 1024),
    )(sc, fv, dv, v1, v2, pu, wd, wrd, pm)
    shape = forcing_state.shape[1:]
    ms, xs, mr, xr = (from_rows(x, shape)[None] for x in (ms, xs, mr, xr))
    return ms, rs[None], xs, mr, rr[None], xr


def solution(mesh):
    grid = P("tm", None, None, None, "col")
    reports = P("tm", "col", None)
    in_specs = (
        grid, grid, grid, P(), P(), reports, reports, P("tm", "col"), P("tm", "col"), reports,
    )
    out_specs = (grid, reports, grid, grid, reports, grid)
    run = functools.partial(body, mesh.shape["col"], mesh.shape["tm"])
    return jax.shard_map(run, mesh=mesh, in_specs=in_specs, out_specs=out_specs, check_vma=False)
```

```python
import functools

import jax
import jax.numpy as jnp
from jax import lax
from jax.experimental import pallas as pl
from jax.experimental.pallas import tpu as pltpu
from jax.sharding import PartitionSpec as P

F32, BF16, I32 = jnp.float32, jnp.bfloat16, jnp.int32
MESH = pl.DeviceIdType.MESH
LEVELS, LAT, WIDTH, STEPS, CHANNELS = 64, 4, 256, 4, 128
ROWS, INST = 512, 4
INST_ROWS = ROWS // INST
SLOTS = 2 * ROWS
CELLS = LAT * WIDTH
HALO, EDGE = 16, 8
INNER = 8
LAST = 8
GROUPS = ((0, 4), (4, 4), (8, 2))


def split2(x):
    hi = x.astype(BF16)
    return hi, (x - hi.astype(F32)).astype(BF16)


def pack(w):
    row = jnp.concatenate(split2(w), axis=1)
    return jnp.concatenate([row, row], axis=0)


def halves(o):
    return o[:, :128] + o[:, 128:]


def mm(u, w):
    left = jnp.concatenate(split2(u), axis=1)
    return halves(jnp.dot(left, w, preferred_element_type=F32))


def native_rows(block, y, xt, count):
    return pl.ds(block * LEVELS * 2 * LAT + xt * LAT + y, count, stride=2 * LAT)


def load_pair(ref, g, y, xt):
    return ref[native_rows(2 * g, y, xt, 128), :]


def load_last(ref, y, xt):
    top = ref[native_rows(4, y, xt, 64), :]
    low = ref[native_rows(4, y + 2, xt, 64), :]
    return jnp.concatenate([top, low], axis=0)


def folded(x):
    return jnp.sum(x.reshape(x.shape[0] // 8, 8, 128), axis=0)


def system_kernel(
    n, nt,
    f_hbm, d_hbm, c_hbm, vm_hbm, jac_hbm, inn_hbm, rvar_hbm, col_hbm, slot_hbm, cnt_hbm,
    f_in, d_in, v1n, v2n, pun, wd_out, wrd_out, pm_out, sc_out,
    c_in, vm, jac, inn, rvar, col, slot, cnt,
    f_t, df_t, rf, rd, c_t, v1, closing, arr, z, yacc, ysplit, rowsplit, keyrow, keycol,
    wa, wf, jf, jt, p_mat, pt_mat, send_a, recv_a, send_b, recv_b, obs_s, obs_r,
    acc, red, redbuf, zred, zbuf,
    in_s, a2a_ss, a2a_rs, z_ss, z_rs, h_ss, h_rs, vh_ss, vh_rs, zz_ss, zz_rs, r_ss, r_rs,
):
    cap = SLOTS // n
    s, c = lax.axis_index("tm"), lax.axis_index("col")
    prev_s, next_s = lax.rem(s + nt - 1, nt), lax.rem(s + 1, nt)
    west, east = lax.rem(c + n - 1, n), lax.rem(c + 1, n)

    def rcopy(src, dst, ss, rs, to):
        return pltpu.make_async_remote_copy(
            src_ref=src, dst_ref=dst, send_sem=ss, recv_sem=rs, device_id=to, device_id_type=MESH
        )

    def z_send(src, dst, base, to):
        rest = []
        for i, (k0, kn) in enumerate(GROUPS):
            rest.append(
                rcopy(
                    src.at[pl.ds(k0, kn)], dst.at[pl.ds(k0, kn), pl.ds(0, WIDTH)],
                    z_ss.at[base + i], z_rs.at[base + i], to,
                )
            )
        return rest

    def z_halo(src, dst, i):
        return rcopy(
            src.at[:, pl.ds(0, EDGE)], dst.at[:, pl.ds(WIDTH, EDGE)],
            h_ss.at[i], h_rs.at[i], (prev_s, west),
        )

    def exchange_start(i, src, dst):
        for d in range(1, n):
            peer = (c + d) & (n - 1)
            rcopy(src.at[peer], dst.at[c], a2a_ss.at[i], a2a_rs.at[i], (s, peer)).start()
        dst[c] = src[c]

    def exchange_all(i, src, dst):
        every = pl.ds(0, n - 1)
        return rcopy(src.at[every], dst.at[every], a2a_ss.at[i], a2a_rs.at[i], (s, east))

    def exchange_wait(i, src, dst):
        exchange_all(i, src, dst).wait_recv()

    def exchange_sent(i, src, dst):
        exchange_all(i, src, dst).wait_send()

    pairs = (
        (f_hbm, f_in), (col_hbm, col), (slot_hbm, slot), (cnt_hbm, cnt), (inn_hbm, inn),
        (rvar_hbm, rvar), (c_hbm, c_in), (vm_hbm, vm), (jac_hbm, jac), (d_hbm, d_in),
    )
    loads = [pltpu.make_async_copy(a, b, in_s.at[i]) for i, (a, b) in enumerate(pairs)]
    for load in loads:
        load.start()

    barrier = pltpu.get_barrier_semaphore()

    def greet(to):
        pl.semaphore_signal(barrier, inc=1, device_id=to, device_id_type=MESH)

    greet((prev_s, west))
    greet((next_s, east))

    @pl.loop(1, nt)
    def _(d):
        greet((lax.rem(s + d, nt), c))

        @pl.loop(1, n // INNER)
        def _(e):
            greet((lax.rem(s + d, nt), lax.rem(c + e * INNER, n)))

    @pl.loop(1, n)
    def _(d):
        greet((s, lax.rem(c + d, n)))

    loads[0].wait()

    @pl.loop(0, 8)
    def _(k):
        for xt in range(2):
            f_t[k, pl.ds(xt * 128, 128), :] = load_pair(f_in, k // 4, k % 4, xt).T

    @pl.loop(0, 2)
    def _(y):
        for xt in range(2):
            f_t[8 + y, pl.ds(xt * 128, 128), :] = load_last(f_in, y, xt).T

    pl.semaphore_wait(barrier, n + nt + (nt - 1) * (n // INNER - 1))
    f_halo = z_halo(f_t, rf, 0)
    f_halo.start()
    f_send = z_send(f_t, rf, 0, (prev_s, c))
    for i in (2, 0, 1):
        f_send[i].start()

    rows_iota = lax.broadcasted_iota(I32, (ROWS, ROWS), 0)
    lane_iota = lax.broadcasted_iota(I32, (ROWS, ROWS), 1)
    upper_ones = jnp.where(rows_iota <= lane_iota, 1.0, 0.0).astype(BF16)
    for load in loads[1:4]:
        load.wait()
    column = col[...]
    shift_w, mask_n = WIDTH.bit_length() - 1, n - 1
    owner = (column >> shift_w) & mask_n
    cell = (column >> (shift_w + n.bit_length() - 1)) * WIDTH + (column & (WIDTH - 1))
    key = (slot[...] * CELLS + cell).astype(F32)
    owners = lax.broadcasted_iota(I32, (n, ROWS), 0)
    owned = jnp.where(owners == owner, 1.0, 0.0)
    ranks = jnp.dot(owned.astype(BF16), upper_ones, preferred_element_type=F32)
    landing = jnp.sum(owned * ((owners * cap).astype(F32) + ranks - 1.0), axis=0, keepdims=True)

    def as_column(row, b):
        return jnp.broadcast_to(row[:, b * 128:(b + 1) * 128], (128, 128)).T

    for b in range(SLOTS // 128):
        spots = (lax.broadcasted_iota(I32, (128, ROWS), 0) + b * 128).astype(F32)
        p_mat[b * 128:(b + 1) * 128, :] = jnp.where(spots == landing, 1.0, 0.0).astype(BF16)
    spots = lax.broadcasted_iota(I32, (128, SLOTS), 1).astype(F32)
    for b in range(ROWS // 128):
        land_col = jnp.concatenate([as_column(landing, b)] * (SLOTS // 128), axis=1)
        pt_mat[b * 128:(b + 1) * 128, :] = jnp.where(spots == land_col, 1.0, 0.0).astype(BF16)

    def split3(x):
        hi, rest = x.astype(BF16), x - x.astype(BF16).astype(F32)
        return (hi,) + split2(rest)

    loads[4].wait()
    loads[5].wait()
    inst_iota = lax.broadcasted_iota(I32, (INST_ROWS, CHANNELS), 0)
    weight = jnp.concatenate(
        [jnp.where(inst_iota < cnt[0:1, i:i + 1], 1.0, 0.0) for i in range(INST)], axis=0
    )
    wd = weight * inn[...]
    wrd = weight * (rvar[...] * wd)
    wd_out[...] = wd
    wrd_out[...] = wrd
    right = jnp.concatenate(split3(wd) + split3(wrd), axis=1)
    per, lots = 256 // cap, 128 // cap
    for b in range(4):
        o = jnp.dot(p_mat[b * 256:(b + 1) * 256, :], right, preferred_element_type=F32)
        o = [o[:, i * 128:(i + 1) * 128] for i in range(6)]
        owners_here = slice(b * per, (b + 1) * per)
        send_a[owners_here, 8:, :] = (o[0] + o[1] + o[2]).reshape(per, cap, 128)
        send_b[owners_here, :, :] = (o[3] + o[4] + o[5]).reshape(per, cap, 128)
    keys = 0.0
    for part in split2(jnp.broadcast_to(key, (16, ROWS))):
        keys = keys + lax.dot_general(
            part, p_mat[...], (((1,), (1,)), ((), ())), preferred_element_type=F32
        )
    for o in range(n):
        b = o // lots
        send_a[o, 0:8, :] = keys[0:8, b * 128:(b + 1) * 128]

    exchange_start(0, send_a, recv_a)

    acc[...] = jnp.zeros_like(acc)

    loads[6].wait()

    def wind(m, y, xt):
        return c_in[native_rows(m, y, xt, 64), :]

    @pl.loop(0, STEPS * LAT)
    def _(i):
        m, y = i // LAT, i % LAT
        for xt in range(2):
            one = wind(m, y, xt)
            c_t[m * 6 + y, pl.ds(HALO + xt * 128, 128), :] = jnp.concatenate([one, one], axis=0).T

    @pl.loop(0, STEPS * 2)
    def _(i):
        m, y = i // 2, i % 2
        for xt in range(2):
            both = jnp.concatenate([wind(m, y, xt), wind(m, y + 2, xt)], axis=0)
            c_t[m * 6 + 4 + y, pl.ds(HALO + xt * 128, 128), :] = both.T

    c_west = rcopy(
        c_t.at[:, pl.ds(HALO, EDGE)], c_t.at[:, pl.ds(HALO + WIDTH, EDGE)],
        h_ss.at[2], h_rs.at[2], (s, west),
    )
    c_east = rcopy(
        c_t.at[:, pl.ds(WIDTH + HALO - EDGE, EDGE)], c_t.at[:, pl.ds(HALO - EDGE, EDGE)],
        h_ss.at[3], h_rs.at[3], (s, east),
    )
    c_west.start()
    c_east.start()
    exchange_start(2, send_b, recv_b)
    loads[9].wait()

    @pl.loop(0, 8)
    def _(k):
        for xt in range(2):
            g, y = k // 4, k % 4
            df_t[k, pl.ds(xt * 128, 128), :] = (
                load_pair(f_in, g, y, xt) * load_pair(d_in, g, y, xt)
            ).T

    @pl.loop(0, 2)
    def _(y):
        for xt in range(2):
            df_t[8 + y, pl.ds(xt * 128, 128), :] = (
                load_last(f_in, y, xt) * load_last(d_in, y, xt)
            ).T

    d_halo = z_halo(df_t, rd, 1)
    d_halo.start()
    d_send = z_send(df_t, rd, 3, (prev_s, c))
    for copy in d_send:
        copy.start()

    loads[7].wait()
    loads[8].wait()

    eye = jnp.where(
        lax.broadcasted_iota(I32, (64, 64), 0) == lax.broadcasted_iota(I32, (64, 64), 1), 1.0, 0.0
    )
    nothing = jnp.zeros((64, 64), F32)
    for g, (fa, fb) in enumerate(((0, 1), (2, 3), (4, 4))):
        ma, mb = 0.6 * eye + 0.4 * vm[fa], 0.6 * eye + 0.4 * vm[fb]
        block = jnp.concatenate(
            [jnp.concatenate([ma, nothing], axis=1), jnp.concatenate([nothing, mb], axis=1)],
            axis=0,
        )
        wa[g] = pack(block)
        wf[g] = pack(block.T)
    none = jnp.zeros((64, CHANNELS), F32)
    last = jac[256:320, :]
    for g, block in enumerate(
        (
            jac[0:128, :], jac[128:256, :],
            jnp.concatenate([last, none], axis=0), jnp.concatenate([none, last], axis=0),
        )
    ):
        jf[g] = pack(block)
        jt[g] = pack(block.T)

    exchange_wait(0, send_a, recv_a)
    meta = pltpu.roll(recv_a[:, 0, :], lax.rem(128 - cap * lax.rem(c, lots), 128), 1)
    lane = lax.broadcasted_iota(I32, (n, 128), 1)
    meta = jnp.where(lane < cap, meta, 0.0)
    tiled = meta
    for i in range(1, lots):
        tiled = tiled + pltpu.roll(meta, cap * i, 1)
    tiled = jnp.concatenate([tiled] * (SLOTS // 128), axis=1)
    sender = lax.broadcasted_iota(I32, (n, SLOTS), 0)
    place = lax.broadcasted_iota(I32, (n, SLOTS), 1)
    mine = (place >= sender * cap) & (place < sender * cap + cap)
    keyrow[...] = jnp.broadcast_to(
        jnp.sum(jnp.where(mine, tiled, 0.0), axis=0, keepdims=True), (8, SLOTS)
    )

    def scatter(r, rows):
        rowsplit[...] = jnp.concatenate(split2(rows.reshape(SLOTS, 128)), axis=1)

        @pl.loop(0, STEPS * LAT)
        def _(i):
            spot = (lax.broadcasted_iota(I32, (WIDTH, SLOTS), 0) + i * WIDTH).astype(F32)
            hit = jnp.where(spot == keyrow[0:1, :], 1.0, 0.0).astype(BF16)
            o = jnp.dot(hit, rowsplit[...], preferred_element_type=F32)
            z[r, i, pl.ds(0, WIDTH), :] = halves(o)

        edge = rcopy(
            z.at[r, pl.ds(LAT, 3 * LAT), pl.ds(0, EDGE)],
            z.at[r, pl.ds(LAT, 3 * LAT), pl.ds(WIDTH, EDGE)],
            h_ss.at[4 + r], h_rs.at[4 + r], (s, west),
        )
        edge.start()
        return edge

    z_edge1 = scatter(0, recv_a[:, 8:, :])

    @pl.loop(0, SLOTS // 128)
    def _(b):
        lanes = pl.ds(pl.multiple_of(b * 128, 128), 128)
        keycol[lanes, :] = jnp.broadcast_to(keyrow[0:1, lanes], (128, 128)).T

    later = jnp.where(s < nt - 1, -1.0, 0.0).astype(F32)
    span = WIDTH + HALO

    def block(x, first, rows, count):
        return x[pl.ds(first, 2), pl.ds(rows, count), :].reshape(2 * count, 128)

    def adjoint(r, k, g, y, received, own):
        a = block(received, k, 0, span) * later
        wind_at = 4 if k is LAST else y
        for m in reversed(range(STEPS)):
            w = mm(a, wa[g])
            p = block(c_t, m * 6 + wind_at, HALO, span) * w
            if k is LAST:
                inject = mm(block(z.at[r], m * LAT, 0, span), jt[2])
                inject = inject + mm(block(z.at[r], m * LAT + 2, 0, span), jt[3])
            else:
                inject = mm(block(z.at[r], m * LAT + y, 0, span), jt[g])
            a = w - p + pltpu.roll(p, 2 * span - 1, 0) + inject
        a = a.reshape(2, span, 128)
        return [own[k + i] + a[i, 0:WIDTH, :] for i in range(2)]

    def forward(k, g, y):
        v = block(v1, k, 0, span)
        wind_at = 4 if k is LAST else y
        for m in range(STEPS):
            inner = v.reshape(2, span, 128)[:, HALO:, :].reshape(2 * WIDTH, 128)
            if k is LAST:
                yacc[pl.ds(m * LAT, 2)] += mm(inner, jf[2]).reshape(2, WIDTH, 128)
                yacc[pl.ds(m * LAT + 2, 2)] += mm(inner, jf[3]).reshape(2, WIDTH, 128)
            else:
                yacc[pl.ds(m * LAT + y, 2)] += mm(inner, jf[g]).reshape(2, WIDTH, 128)
            wind_now = block(c_t, m * 6 + wind_at, 0, span)
            v = mm(v - wind_now * (v - pltpu.roll(v, 1, 0)), wf[g])
        closing[pl.ds(k, 2)] = v.reshape(2, span, 128)[:, HALO:, :]

    def each_pair(i, run):
        if i < 2:
            @pl.loop(0, 2)
            def _(j):
                run(4 * i + 2 * j, i, 2 * j)
        else:
            run(LAST, 2, 0)

    def put_pair(ref, g, y, value):
        for xt in range(2):
            ref[native_rows(2 * g, y, xt, 128), :] = value[xt * 128:(xt + 1) * 128, :].T

    def put(ref, k, g, y, value):
        if g == 2:
            put_last(ref, y, value)
        else:
            put_pair(ref, g, y, value)

    def put_last(ref, y, value):
        for xt in range(2):
            turned = value[xt * 128:(xt + 1) * 128, :].T
            ref[native_rows(4, y, xt, 64), :] = turned[:64, :]
            ref[native_rows(4, y + 2, xt, 64), :] = turned[64:, :]

    yacc[...] = jnp.zeros_like(yacc)
    c_west.wait_recv()
    c_east.wait_recv()
    f_halo.wait_recv()
    z_edge1.wait_recv()

    def edge_v1(i):
        k0, kn = GROUPS[i]
        return rcopy(
            v1.at[pl.ds(k0, kn), pl.ds(WIDTH + HALO - EDGE, EDGE)],
            v1.at[pl.ds(k0, kn), pl.ds(HALO - EDGE, EDGE)],
            vh_ss.at[i], vh_rs.at[i], (s, east),
        )

    def send_closing(i):
        k0, kn = GROUPS[i]
        return rcopy(
            closing.at[pl.ds(k0, kn)], arr.at[pl.ds(k0, kn)],
            zz_ss.at[i], zz_rs.at[i], (next_s, c),
        )

    edges = [edge_v1(i) for i in range(3)]
    closings = [send_closing(i) for i in range(3)]

    def first_adjoint(i):
        f_send[i].wait_recv()

        def run(k, g, y):
            for j, value in enumerate(adjoint(0, k, g, y, rf, f_t)):
                v1[k + j, pl.ds(HALO, WIDTH), :] = value
                acc[1] += folded(value * value)
                put(v1n, k + j, g, y + j, value)

        each_pair(i, run)
        edges[i].start()

    def first_forward(i):
        edges[i].wait_recv()
        each_pair(i, forward)
        closings[i].start()

    first_adjoint(2)
    first_adjoint(0)
    first_forward(2)
    first_forward(0)
    exchange_wait(2, send_b, recv_b)
    z_edge2 = scatter(1, recv_b[...])
    first_adjoint(1)

    @pl.loop(0, 10)
    def _(i):
        rows = pl.ds(pl.multiple_of(i * 256, 256), 256)
        f = f_in[rows, :]
        df = f * d_in[rows, :]
        acc[0] += folded(f * df)
        acc[1] += folded(df * df)

    acc[0] += folded(wd * wrd)
    acc[1] += folded(wrd * wrd)

    first_forward(1)

    @pl.loop(0, STEPS * LAT)
    def _(i):
        ysplit[pl.ds(pl.multiple_of(i * WIDTH, WIDTH), WIDTH), :] = jnp.concatenate(
            split2(yacc[i]), axis=1
        )

    @pl.loop(0, 4)
    def _(b):
        took = keycol[pl.ds(pl.multiple_of(b * 256, 256), 256), :]
        at = jnp.concatenate([took] * (CELLS // 128), axis=1)
        total = jnp.zeros((256, 256), F32)
        for m in range(STEPS):
            spot = (lax.broadcasted_iota(I32, (256, CELLS), 1) + m * CELLS).astype(F32)
            hit = jnp.where(spot == at, 1.0, 0.0).astype(BF16)
            total = total + jnp.dot(
                hit, ysplit[m * CELLS:(m + 1) * CELLS, :], preferred_element_type=F32
            )
        obs_s[pl.ds(pl.multiple_of(b * per, per), per)] = halves(total).reshape(per, cap, 128)

    exchange_start(1, obs_s, obs_r)

    d_halo.wait_recv()
    z_edge2.wait_recv()

    def second_adjoint(i):
        d_send[i].wait_recv()

        def run(k, g, y):
            for j, value in enumerate(adjoint(1, k, g, y, rd, df_t)):
                own = v1[k + j, pl.ds(HALO, WIDTH), :]
                acc[3] += folded(own * value)
                acc[4] += folded(value * value)
                put(v2n, k + j, g, y + j, value)

        each_pair(i, run)

    has_before = jnp.where(s > 0, 1.0, 0.0).astype(F32)

    def arrive(i):
        closings[i].wait_recv()
        def run(k, g, y):
            for j in range(2):
                value = v1[k + j, pl.ds(HALO, WIDTH), :] - has_before * arr[k + j]
                put(pun, k + j, g, y + j, value)

        each_pair(i, run)

    def upper(i):
        first, count = ((0, 4), (4, 4), (8, 2))[i]

        @pl.loop(first, first + count)
        def _(b):
            rows = pl.ds(pl.multiple_of(b * 256, 256), 256)
            f, d = f_in[rows, :], d_in[rows, :]
            df = f * d
            pu = d * df + pun[rows, :]
            pun[rows, :] = pu
            acc[2] += folded(f * pu)
            acc[3] += folded(df * pu)
            acc[4] += folded(pu * pu)

    arrive(2)
    upper(2)
    second_adjoint(0)
    arrive(0)
    upper(0)
    second_adjoint(1)
    exchange_wait(1, obs_s, obs_r)
    right = jnp.concatenate(split2(obs_r[...].reshape(SLOTS, 128)), axis=1)
    seen = halves(jnp.dot(pt_mat[...], right, preferred_element_type=F32))
    pm = weight * (rvar[...] * wrd + seen)
    pm_out[...] = pm
    acc[2] += folded(wd * pm)
    acc[3] += folded(wrd * pm)
    acc[4] += folded(pm * pm)

    arrive(1)
    upper(1)
    for i, src, dst in ((0, send_a, recv_a), (1, obs_s, obs_r), (2, send_b, recv_b)):
        exchange_sent(i, src, dst)
    for copy in [f_halo, d_halo, c_west, c_east, z_edge1, z_edge2] + f_send:
        copy.wait_send()
    for copy in edges + closings:
        copy.wait_send()
    second_adjoint(2)

    lines = [jnp.sum(acc[i], axis=0, keepdims=True) for i in range(5)]
    red[...] = jnp.concatenate(lines + [jnp.zeros((3, 128), F32)], axis=0)

    place_in, place_out = lax.rem(c, INNER), s * (n // INNER) + c // INNER
    first = c - place_in

    def share(d):
        to = lax.rem(place_in + d, INNER)
        return rcopy(red, redbuf.at[place_in], r_ss.at[d], r_rs.at[d], (s, first + to))

    for d in range(1, INNER):
        share(d).start()
    redbuf[place_in] = red[...]
    for d in range(1, INNER):
        peer = lax.rem(place_in + INNER - d, INNER)
        rcopy(red, redbuf.at[peer], r_ss.at[d], r_rs.at[d], (s, first + peer)).wait_recv()
    zred[...] = jnp.sum(redbuf[...], axis=0)
    outer = n * nt // INNER

    def share_out(d):
        to = lax.rem(place_out + d, outer)
        where = (to // (n // INNER), lax.rem(to, n // INNER) * INNER + place_in)
        return rcopy(
            zred, zbuf.at[place_out], r_ss.at[INNER + d], r_rs.at[INNER + d], where
        )

    for d in range(1, outer):
        share_out(d).start()
    zbuf[place_out] = zred[...]
    for d in range(1, outer):
        peer = lax.rem(place_out + outer - d, outer)
        where = (peer // (n // INNER), lax.rem(peer, n // INNER) * INNER + place_in)
        rcopy(zred, zbuf.at[peer], r_ss.at[INNER + d], r_rs.at[INNER + d], where).wait_recv()

    total = jnp.sum(jnp.sum(zbuf[...], axis=0), axis=1, keepdims=True)
    total = jnp.broadcast_to(total, (8, 128))
    rq, qq, rp, qp, pp = (total[i:i + 1, :] for i in range(5))
    step1 = rq / qq
    step2 = step1 * (step1 * qp - rp) / (qq - 2.0 * step1 * qp + step1 * step1 * pp)
    sc_out[...] = jnp.concatenate(
        [step1 + step2, step1 * step2, jnp.zeros((6, 128), F32)], axis=0
    )

    for d in range(1, INNER):
        share(d).wait_send()
    for d in range(1, outer):
        share_out(d).wait_send()
    for copy in d_send:
        copy.wait_send()


def finish_kernel(
    sc, f_in, d_in, v1, v2, pu, wd_in, wrd_in, pm,
    ms_out, rs_out, xs_out, mr_out, rr_out, xr_out,
    ms, rs, xs, mr, rr, xr, sem,
):
    t, q = sc[0:1, :], sc[1:2, :]
    parts = 5
    size = ms.shape[0] // parts
    copies = []

    def send(i, src, dst):
        copy = pltpu.make_async_copy(src, dst, sem.at[i])
        copy.start()
        copies.append(copy)

    for i in range(parts):
        rows = pl.ds(i * size, size)
        f, v = f_in[rows, :], v1[rows, :]
        df = f * d_in[rows, :]
        ms[rows, :] = t * f - q * df
        mr[rows, :] = f - t * df + q * pu[rows, :]
        xs[rows, :] = -(q * v)
        xr[rows, :] = q * v2[rows, :] - t * v
        for j, (src, dst) in enumerate(
            ((ms, ms_out), (mr, mr_out), (xs, xs_out), (xr, xr_out))
        ):
            send(4 * i + j, src.at[rows, :], dst.at[rows, :])
    wd, wrd = wd_in[...], wrd_in[...]
    rs[...] = t * wd - q * wrd
    rr[...] = wd - t * wrd + q * pm[...]
    send(4 * parts, rs, rs_out)
    send(4 * parts + 1, rr, rr_out)
    for copy in copies:
        copy.wait()


def to_rows(x):
    a, b, y, w = x.shape
    return x.reshape(a, b, y, w // 128, 128).transpose(0, 1, 3, 2, 4).reshape(-1, 128)


def from_rows(x, shape):
    a, b, y, w = shape
    return x.reshape(a, b, w // 128, y, 128).transpose(0, 1, 3, 2, 4).reshape(shape)


def body(n, nt, forcing_state, model_error, courant, vertical_mix, radiance_jacobian,
         innovation, report_error, report_column, report_slot, report_count):
    f, d, wind = (to_rows(x[0]) for x in (forcing_state, model_error, courant))
    inn, rvar, cnt = innovation[0], report_error[0], report_count[0]
    size = f.shape[0]
    vmem = pl.BlockSpec(memory_space=pltpu.VMEM)
    hbm = pl.BlockSpec(memory_space=pltpu.HBM)
    V = pltpu.VMEM
    state = jax.ShapeDtypeStruct((size, 128), F32)
    reports = jax.ShapeDtypeStruct((ROWS, CHANNELS), F32)
    span, cap = WIDTH + HALO, SLOTS // n
    dma = pltpu.SemaphoreType.DMA
    inputs = (
        f, d, wind, vertical_mix, radiance_jacobian, inn, rvar, report_column, report_slot, cnt,
    )
    inputs = tuple(pltpu.with_memory_space_constraint(x, pltpu.HBM) for x in inputs)
    results = pl.pallas_call(
        functools.partial(system_kernel, n, nt),
        out_shape=(state,) * 5 + (reports,) * 3 + (jax.ShapeDtypeStruct((8, 128), F32),),
        in_specs=[hbm] * 10,
        out_specs=(vmem,) * 9,
        scratch_shapes=[V(x.shape, x.dtype) for x in inputs[2:]] + [
            V((10, WIDTH, 128), F32), V((10, WIDTH, 128), F32),
            V((10, span, 128), F32), V((10, span, 128), F32),
            V((6 * STEPS, span + HALO, 128), F32),
            V((10, span, 128), F32), V((10, WIDTH, 128), F32), V((10, WIDTH, 128), F32),
            V((2, STEPS * LAT, span, 128), F32), V((STEPS * LAT, WIDTH, 128), F32),
            V((STEPS * CELLS, 256), BF16), V((SLOTS, 256), BF16), V((8, SLOTS), F32), V((SLOTS, 128), F32),
            V((3, 256, 256), BF16), V((3, 256, 256), BF16),
            V((4, 256, 256), BF16), V((4, 256, 256), BF16),
            V((SLOTS, ROWS), BF16), V((ROWS, SLOTS), BF16),
            V((n, 8 + cap, 128), F32), V((n, 8 + cap, 128), F32),
            V((n, cap, 128), F32), V((n, cap, 128), F32),
            V((n, cap, 128), F32), V((n, cap, 128), F32),
            V((5, 8, 128), F32), V((8, 128), F32), V((INNER, 8, 128), F32),
            V((8, 128), F32), V((n * nt // INNER, 8, 128), F32),
            dma((10,)), dma((3,)), dma((3,)), dma((6,)), dma((6,)),
            dma((6,)), dma((6,)), dma((3,)), dma((3,)), dma((3,)), dma((3,)),
            dma((INNER + n * nt // INNER,)), dma((INNER + n * nt // INNER,)),
        ],
        compiler_params=pltpu.CompilerParams(
            collective_id=0, has_side_effects=True, vmem_limit_bytes=42 * 1024 * 1024
        ),
        cost_estimate=pl.CostEstimate(flops=40 * 10**9, bytes_accessed=10**7, transcendentals=0),
    )(*inputs)
    fv, dv, v1, v2, pu, wd, wrd, pm, sc = results
    outs = (state, reports, state, state, reports, state)
    ms, rs, xs, mr, rr, xr = pl.pallas_call(
        finish_kernel,
        out_shape=outs,
        in_specs=[vmem] * 9,
        out_specs=(pl.BlockSpec(memory_space=pl.ANY),) * 6,
        scratch_shapes=[V(x.shape, x.dtype) for x in outs] + [dma((22,))],
        compiler_params=pltpu.CompilerParams(vmem_limit_bytes=16 * 1024 * 1024),
    )(sc, fv, dv, v1, v2, pu, wd, wrd, pm)
    shape = forcing_state.shape[1:]
    ms, xs, mr, xr = (from_rows(x, shape)[None] for x in (ms, xs, mr, xr))
    return ms, rs[None], xs, mr, rr[None], xr


def solution(mesh):
    grid = P("tm", None, None, None, "col")
    reports = P("tm", "col", None)
    in_specs = (
        grid, grid, grid, P(), P(), reports, reports, P("tm", "col"), P("tm", "col"), reports,
    )
    out_specs = (grid, reports, grid, grid, reports, grid)
    run = functools.partial(body, mesh.shape["col"], mesh.shape["tm"])
    return jax.shard_map(run, mesh=mesh, in_specs=in_specs, out_specs=out_specs, check_vma=False)
```

```python
import functools

import jax
import jax.numpy as jnp
from jax import lax
from jax.experimental import pallas as pl
from jax.experimental.pallas import tpu as pltpu
from jax.sharding import PartitionSpec as P

F32, BF16, I32 = jnp.float32, jnp.bfloat16, jnp.int32
MESH = pl.DeviceIdType.MESH
LEVELS, LAT, WIDTH, STEPS, CHANNELS = 64, 4, 256, 4, 128
ROWS, INST = 512, 4
INST_ROWS = ROWS // INST
SLOTS = 2 * ROWS
CELLS = LAT * WIDTH
HALO, EDGE = 16, 8
INNER = 8
LAST = 8
GROUPS = ((0, 4), (4, 4), (8, 2))


def split2(x):
    hi = x.astype(BF16)
    return hi, (x - hi.astype(F32)).astype(BF16)


def pack(w):
    row = jnp.concatenate(split2(w), axis=1)
    return jnp.concatenate([row, row], axis=0)


def halves(o):
    return o[:, :128] + o[:, 128:]


def mm(u, w):
    left = jnp.concatenate(split2(u), axis=1)
    return halves(jnp.dot(left, w, preferred_element_type=F32))


def native_rows(block, y, xt, count):
    return pl.ds(block * LEVELS * 2 * LAT + xt * LAT + y, count, stride=2 * LAT)


def load_pair(ref, g, y, xt):
    return ref[native_rows(2 * g, y, xt, 128), :]


def load_last(ref, y, xt):
    top = ref[native_rows(4, y, xt, 64), :]
    low = ref[native_rows(4, y + 2, xt, 64), :]
    return jnp.concatenate([top, low], axis=0)


def folded(x):
    return jnp.sum(x.reshape(x.shape[0] // 8, 8, 128), axis=0)


def system_kernel(
    n, nt,
    f_hbm, d_hbm, c_hbm, vm_hbm, jac_hbm, inn_hbm, rvar_hbm, col_hbm, slot_hbm, cnt_hbm,
    f_in, d_in, v1n, v2n, pun, wd_out, wrd_out, pm_out, sc_out,
    c_in, vm, jac, inn, rvar, col, slot, cnt,
    f_t, df_t, f_raw, rf, rd, c_t, v1, closing, arr, z, yacc, ysplit, rowsplit, keyrow, keycol,
    wa, wf, jf, jt, p_mat, pt_mat, send_a, recv_a, send_b, recv_b, obs_s, obs_r,
    acc, red, redbuf, zred, zbuf,
    in_s, a2a_ss, a2a_rs, z_ss, z_rs, h_ss, h_rs, vh_ss, vh_rs, zz_ss, zz_rs, r_ss, r_rs,
):
    cap = SLOTS // n
    s, c = lax.axis_index("tm"), lax.axis_index("col")
    prev_s, next_s = lax.rem(s + nt - 1, nt), lax.rem(s + 1, nt)
    west, east = lax.rem(c + n - 1, n), lax.rem(c + 1, n)

    def rcopy(src, dst, ss, rs, to):
        return pltpu.make_async_remote_copy(
            src_ref=src, dst_ref=dst, send_sem=ss, recv_sem=rs, device_id=to, device_id_type=MESH
        )

    def z_send(src, dst, base, to):
        rest = []
        for i, (k0, kn) in enumerate(GROUPS):
            rest.append(
                rcopy(
                    src.at[pl.ds(k0, kn)], dst.at[pl.ds(k0, kn), pl.ds(0, WIDTH)],
                    z_ss.at[base + i], z_rs.at[base + i], to,
                )
            )
        return rest

    def z_halo(src, dst, i):
        return rcopy(
            src.at[:, pl.ds(0, EDGE)], dst.at[:, pl.ds(WIDTH, EDGE)],
            h_ss.at[i], h_rs.at[i], (prev_s, west),
        )

    def exchange_start(i, src, dst):
        for d in range(1, n):
            peer = (c + d) & (n - 1)
            rcopy(src.at[peer], dst.at[c], a2a_ss.at[i], a2a_rs.at[i], (s, peer)).start()
        dst[c] = src[c]

    def exchange_all(i, src, dst):
        every = pl.ds(0, n - 1)
        return rcopy(src.at[every], dst.at[every], a2a_ss.at[i], a2a_rs.at[i], (s, east))

    def exchange_wait(i, src, dst):
        exchange_all(i, src, dst).wait_recv()

    def exchange_sent(i, src, dst):
        exchange_all(i, src, dst).wait_send()

    pairs = (
        (f_hbm, f_in), (col_hbm, col), (slot_hbm, slot), (cnt_hbm, cnt), (inn_hbm, inn),
        (rvar_hbm, rvar), (c_hbm, c_in), (vm_hbm, vm), (jac_hbm, jac), (d_hbm, d_in),
    )
    loads = [pltpu.make_async_copy(a, b, in_s.at[i]) for i, (a, b) in enumerate(pairs)]
    for load in loads:
        load.start()

    barrier = pltpu.get_barrier_semaphore()

    def greet(to):
        pl.semaphore_signal(barrier, inc=1, device_id=to, device_id_type=MESH)

    greet((prev_s, west))
    greet((next_s, east))

    @pl.loop(1, nt)
    def _(d):
        greet((lax.rem(s + d, nt), c))

        @pl.loop(1, n // INNER)
        def _(e):
            greet((lax.rem(s + d, nt), lax.rem(c + e * INNER, n)))

    @pl.loop(1, n)
    def _(d):
        greet((s, lax.rem(c + d, n)))

    pl.semaphore_wait(barrier, n + nt + (nt - 1) * (n // INNER - 1))

    f_send = []
    for i, (k0, kn) in enumerate(GROUPS):
        rows = pl.ds(k0 * WIDTH, kn * WIDTH)
        f_send.append(
            rcopy(f_hbm.at[rows], f_raw.at[rows], z_ss.at[i], z_rs.at[i], (prev_s, c))
        )
    for i in (2, 0, 1):
        f_send[i].start()
    loads[0].wait()

    @pl.loop(0, 8)
    def _(k):
        for xt in range(2):
            f_t[k, pl.ds(xt * 128, 128), :] = load_pair(f_in, k // 4, k % 4, xt).T

    @pl.loop(0, 2)
    def _(y):
        for xt in range(2):
            f_t[8 + y, pl.ds(xt * 128, 128), :] = load_last(f_in, y, xt).T

    f_halo = z_halo(f_t, rf, 0)
    f_halo.start()

    rows_iota = lax.broadcasted_iota(I32, (ROWS, ROWS), 0)
    lane_iota = lax.broadcasted_iota(I32, (ROWS, ROWS), 1)
    upper_ones = jnp.where(rows_iota <= lane_iota, 1.0, 0.0).astype(BF16)
    for load in loads[1:4]:
        load.wait()
    column = col[...]
    shift_w, mask_n = WIDTH.bit_length() - 1, n - 1
    owner = (column >> shift_w) & mask_n
    cell = (column >> (shift_w + n.bit_length() - 1)) * WIDTH + (column & (WIDTH - 1))
    key = (slot[...] * CELLS + cell).astype(F32)
    owners = lax.broadcasted_iota(I32, (n, ROWS), 0)
    owned = jnp.where(owners == owner, 1.0, 0.0)
    ranks = jnp.dot(owned.astype(BF16), upper_ones, preferred_element_type=F32)
    landing = jnp.sum(owned * ((owners * cap).astype(F32) + ranks - 1.0), axis=0, keepdims=True)

    def as_column(row, b):
        return jnp.broadcast_to(row[:, b * 128:(b + 1) * 128], (128, 128)).T

    for b in range(SLOTS // 128):
        spots = (lax.broadcasted_iota(I32, (128, ROWS), 0) + b * 128).astype(F32)
        p_mat[b * 128:(b + 1) * 128, :] = jnp.where(spots == landing, 1.0, 0.0).astype(BF16)
    spots = lax.broadcasted_iota(I32, (128, SLOTS), 1).astype(F32)
    for b in range(ROWS // 128):
        land_col = jnp.concatenate([as_column(landing, b)] * (SLOTS // 128), axis=1)
        pt_mat[b * 128:(b + 1) * 128, :] = jnp.where(spots == land_col, 1.0, 0.0).astype(BF16)

    def split3(x):
        hi, rest = x.astype(BF16), x - x.astype(BF16).astype(F32)
        return (hi,) + split2(rest)

    loads[4].wait()
    loads[5].wait()
    inst_iota = lax.broadcasted_iota(I32, (INST_ROWS, CHANNELS), 0)
    weight = jnp.concatenate(
        [jnp.where(inst_iota < cnt[0:1, i:i + 1], 1.0, 0.0) for i in range(INST)], axis=0
    )
    wd = weight * inn[...]
    wrd = weight * (rvar[...] * wd)
    wd_out[...] = wd
    wrd_out[...] = wrd
    right = jnp.concatenate(split3(wd) + split3(wrd), axis=1)
    per, lots = 256 // cap, 128 // cap
    for b in range(4):
        o = jnp.dot(p_mat[b * 256:(b + 1) * 256, :], right, preferred_element_type=F32)
        o = [o[:, i * 128:(i + 1) * 128] for i in range(6)]
        owners_here = slice(b * per, (b + 1) * per)
        send_a[owners_here, 8:, :] = (o[0] + o[1] + o[2]).reshape(per, cap, 128)
        send_b[owners_here, :, :] = (o[3] + o[4] + o[5]).reshape(per, cap, 128)
    keys = 0.0
    for part in split2(jnp.broadcast_to(key, (16, ROWS))):
        keys = keys + lax.dot_general(
            part, p_mat[...], (((1,), (1,)), ((), ())), preferred_element_type=F32
        )
    for o in range(n):
        b = o // lots
        send_a[o, 0:8, :] = keys[0:8, b * 128:(b + 1) * 128]

    exchange_start(0, send_a, recv_a)

    acc[...] = jnp.zeros_like(acc)

    loads[6].wait()

    def wind(m, y, xt):
        return c_in[native_rows(m, y, xt, 64), :]

    @pl.loop(0, STEPS * LAT)
    def _(i):
        m, y = i // LAT, i % LAT
        for xt in range(2):
            one = wind(m, y, xt)
            c_t[m * 6 + y, pl.ds(HALO + xt * 128, 128), :] = jnp.concatenate([one, one], axis=0).T

    @pl.loop(0, STEPS * 2)
    def _(i):
        m, y = i // 2, i % 2
        for xt in range(2):
            both = jnp.concatenate([wind(m, y, xt), wind(m, y + 2, xt)], axis=0)
            c_t[m * 6 + 4 + y, pl.ds(HALO + xt * 128, 128), :] = both.T

    c_west = rcopy(
        c_t.at[:, pl.ds(HALO, EDGE)], c_t.at[:, pl.ds(HALO + WIDTH, EDGE)],
        h_ss.at[2], h_rs.at[2], (s, west),
    )
    c_east = rcopy(
        c_t.at[:, pl.ds(WIDTH + HALO - EDGE, EDGE)], c_t.at[:, pl.ds(HALO - EDGE, EDGE)],
        h_ss.at[3], h_rs.at[3], (s, east),
    )
    c_west.start()
    c_east.start()
    exchange_start(2, send_b, recv_b)
    loads[9].wait()

    @pl.loop(0, 8)
    def _(k):
        for xt in range(2):
            g, y = k // 4, k % 4
            df_t[k, pl.ds(xt * 128, 128), :] = (
                load_pair(f_in, g, y, xt) * load_pair(d_in, g, y, xt)
            ).T

    @pl.loop(0, 2)
    def _(y):
        for xt in range(2):
            df_t[8 + y, pl.ds(xt * 128, 128), :] = (
                load_last(f_in, y, xt) * load_last(d_in, y, xt)
            ).T

    d_halo = z_halo(df_t, rd, 1)
    d_halo.start()
    d_send = z_send(df_t, rd, 3, (prev_s, c))
    for copy in d_send:
        copy.start()

    loads[7].wait()
    loads[8].wait()

    eye = jnp.where(
        lax.broadcasted_iota(I32, (64, 64), 0) == lax.broadcasted_iota(I32, (64, 64), 1), 1.0, 0.0
    )
    nothing = jnp.zeros((64, 64), F32)
    for g, (fa, fb) in enumerate(((0, 1), (2, 3), (4, 4))):
        ma, mb = 0.6 * eye + 0.4 * vm[fa], 0.6 * eye + 0.4 * vm[fb]
        block = jnp.concatenate(
            [jnp.concatenate([ma, nothing], axis=1), jnp.concatenate([nothing, mb], axis=1)],
            axis=0,
        )
        wa[g] = pack(block)
        wf[g] = pack(block.T)
    none = jnp.zeros((64, CHANNELS), F32)
    last = jac[256:320, :]
    for g, block in enumerate(
        (
            jac[0:128, :], jac[128:256, :],
            jnp.concatenate([last, none], axis=0), jnp.concatenate([none, last], axis=0),
        )
    ):
        jf[g] = pack(block)
        jt[g] = pack(block.T)

    exchange_wait(0, send_a, recv_a)
    meta = pltpu.roll(recv_a[:, 0, :], lax.rem(128 - cap * lax.rem(c, lots), 128), 1)
    lane = lax.broadcasted_iota(I32, (n, 128), 1)
    meta = jnp.where(lane < cap, meta, 0.0)
    tiled = meta
    for i in range(1, lots):
        tiled = tiled + pltpu.roll(meta, cap * i, 1)
    tiled = jnp.concatenate([tiled] * (SLOTS // 128), axis=1)
    sender = lax.broadcasted_iota(I32, (n, SLOTS), 0)
    place = lax.broadcasted_iota(I32, (n, SLOTS), 1)
    mine = (place >= sender * cap) & (place < sender * cap + cap)
    keyrow[...] = jnp.broadcast_to(
        jnp.sum(jnp.where(mine, tiled, 0.0), axis=0, keepdims=True), (8, SLOTS)
    )

    def scatter(r, rows):
        rowsplit[...] = jnp.concatenate(split2(rows.reshape(SLOTS, 128)), axis=1)

        @pl.loop(0, STEPS * LAT)
        def _(i):
            spot = (lax.broadcasted_iota(I32, (WIDTH, SLOTS), 0) + i * WIDTH).astype(F32)
            hit = jnp.where(spot == keyrow[0:1, :], 1.0, 0.0).astype(BF16)
            o = jnp.dot(hit, rowsplit[...], preferred_element_type=F32)
            z[r, i, pl.ds(0, WIDTH), :] = halves(o)

        edge = rcopy(
            z.at[r, pl.ds(LAT, 3 * LAT), pl.ds(0, EDGE)],
            z.at[r, pl.ds(LAT, 3 * LAT), pl.ds(WIDTH, EDGE)],
            h_ss.at[4 + r], h_rs.at[4 + r], (s, west),
        )
        edge.start()
        return edge

    z_edge1 = scatter(0, recv_a[:, 8:, :])

    @pl.loop(0, SLOTS // 128)
    def _(b):
        lanes = pl.ds(pl.multiple_of(b * 128, 128), 128)
        keycol[lanes, :] = jnp.broadcast_to(keyrow[0:1, lanes], (128, 128)).T

    later = jnp.where(s < nt - 1, -1.0, 0.0).astype(F32)
    span = WIDTH + HALO

    def block(x, first, rows, count):
        return x[pl.ds(first, 2), pl.ds(rows, count), :].reshape(2 * count, 128)

    def adjoint(r, k, g, y, received, own):
        a = block(received, k, 0, span) * later
        wind_at = 4 if k is LAST else y
        for m in reversed(range(STEPS)):
            w = mm(a, wa[g])
            p = block(c_t, m * 6 + wind_at, HALO, span) * w
            if k is LAST:
                inject = mm(block(z.at[r], m * LAT, 0, span), jt[2])
                inject = inject + mm(block(z.at[r], m * LAT + 2, 0, span), jt[3])
            else:
                inject = mm(block(z.at[r], m * LAT + y, 0, span), jt[g])
            a = w - p + pltpu.roll(p, 2 * span - 1, 0) + inject
        a = a.reshape(2, span, 128)
        return [own[k + i] + a[i, 0:WIDTH, :] for i in range(2)]

    def forward(k, g, y):
        v = block(v1, k, 0, span)
        wind_at = 4 if k is LAST else y
        for m in range(STEPS):
            inner = v.reshape(2, span, 128)[:, HALO:, :].reshape(2 * WIDTH, 128)
            if k is LAST:
                yacc[pl.ds(m * LAT, 2)] += mm(inner, jf[2]).reshape(2, WIDTH, 128)
                yacc[pl.ds(m * LAT + 2, 2)] += mm(inner, jf[3]).reshape(2, WIDTH, 128)
            else:
                yacc[pl.ds(m * LAT + y, 2)] += mm(inner, jf[g]).reshape(2, WIDTH, 128)
            wind_now = block(c_t, m * 6 + wind_at, 0, span)
            v = mm(v - wind_now * (v - pltpu.roll(v, 1, 0)), wf[g])
        closing[pl.ds(k, 2)] = v.reshape(2, span, 128)[:, HALO:, :]

    def each_pair(i, run):
        if i < 2:
            @pl.loop(0, 2)
            def _(j):
                run(4 * i + 2 * j, i, 2 * j)
        else:
            run(LAST, 2, 0)

    def put_pair(ref, g, y, value):
        for xt in range(2):
            ref[native_rows(2 * g, y, xt, 128), :] = value[xt * 128:(xt + 1) * 128, :].T

    def put(ref, k, g, y, value):
        if g == 2:
            put_last(ref, y, value)
        else:
            put_pair(ref, g, y, value)

    def put_last(ref, y, value):
        for xt in range(2):
            turned = value[xt * 128:(xt + 1) * 128, :].T
            ref[native_rows(4, y, xt, 64), :] = turned[:64, :]
            ref[native_rows(4, y + 2, xt, 64), :] = turned[64:, :]

    yacc[...] = jnp.zeros_like(yacc)
    c_west.wait_recv()
    c_east.wait_recv()
    f_halo.wait_recv()
    z_edge1.wait_recv()

    def edge_v1(i):
        k0, kn = GROUPS[i]
        return rcopy(
            v1.at[pl.ds(k0, kn), pl.ds(WIDTH + HALO - EDGE, EDGE)],
            v1.at[pl.ds(k0, kn), pl.ds(HALO - EDGE, EDGE)],
            vh_ss.at[i], vh_rs.at[i], (s, east),
        )

    def send_closing(i):
        k0, kn = GROUPS[i]
        return rcopy(
            closing.at[pl.ds(k0, kn)], arr.at[pl.ds(k0, kn)],
            zz_ss.at[i], zz_rs.at[i], (next_s, c),
        )

    edges = [edge_v1(i) for i in range(3)]
    closings = [send_closing(i) for i in range(3)]

    def first_adjoint(i):
        f_send[i].wait_recv()

        def run(k, g, y):
            for j in range(2):
                for xt in range(2):
                    half = pl.ds(xt * 128, 128)
                    if g == 2:
                        rf[k + j, half, :] = load_last(f_raw, y + j, xt).T
                    else:
                        rf[k + j, half, :] = load_pair(f_raw, g, y + j, xt).T
            for j, value in enumerate(adjoint(0, k, g, y, rf, f_t)):
                v1[k + j, pl.ds(HALO, WIDTH), :] = value
                acc[1] += folded(value * value)
                put(v1n, k + j, g, y + j, value)

        each_pair(i, run)
        edges[i].start()

    def first_forward(i):
        edges[i].wait_recv()
        each_pair(i, forward)
        closings[i].start()

    first_adjoint(2)
    first_adjoint(0)
    first_forward(2)
    first_forward(0)
    exchange_wait(2, send_b, recv_b)
    z_edge2 = scatter(1, recv_b[...])
    first_adjoint(1)

    @pl.loop(0, 10)
    def _(i):
        rows = pl.ds(pl.multiple_of(i * 256, 256), 256)
        f = f_in[rows, :]
        df = f * d_in[rows, :]
        acc[0] += folded(f * df)
        acc[1] += folded(df * df)

    acc[0] += folded(wd * wrd)
    acc[1] += folded(wrd * wrd)

    first_forward(1)

    @pl.loop(0, STEPS * LAT)
    def _(i):
        ysplit[pl.ds(pl.multiple_of(i * WIDTH, WIDTH), WIDTH), :] = jnp.concatenate(
            split2(yacc[i]), axis=1
        )

    @pl.loop(0, 4)
    def _(b):
        took = keycol[pl.ds(pl.multiple_of(b * 256, 256), 256), :]
        at = jnp.concatenate([took] * (CELLS // 128), axis=1)
        total = jnp.zeros((256, 256), F32)
        for m in range(STEPS):
            spot = (lax.broadcasted_iota(I32, (256, CELLS), 1) + m * CELLS).astype(F32)
            hit = jnp.where(spot == at, 1.0, 0.0).astype(BF16)
            total = total + jnp.dot(
                hit, ysplit[m * CELLS:(m + 1) * CELLS, :], preferred_element_type=F32
            )
        obs_s[pl.ds(pl.multiple_of(b * per, per), per)] = halves(total).reshape(per, cap, 128)

    exchange_start(1, obs_s, obs_r)

    d_halo.wait_recv()
    z_edge2.wait_recv()

    def second_adjoint(i):
        d_send[i].wait_recv()

        def run(k, g, y):
            for j, value in enumerate(adjoint(1, k, g, y, rd, df_t)):
                own = v1[k + j, pl.ds(HALO, WIDTH), :]
                acc[3] += folded(own * value)
                acc[4] += folded(value * value)
                if g == 2:
                    closing[k + j] = value
                else:
                    put(v2n, k + j, g, y + j, value)

        each_pair(i, run)

    has_before = jnp.where(s > 0, 1.0, 0.0).astype(F32)

    def arrive(i):
        closings[i].wait_recv()
        def run(k, g, y):
            for j in range(2):
                value = v1[k + j, pl.ds(HALO, WIDTH), :] - has_before * arr[k + j]
                put(pun, k + j, g, y + j, value)

        each_pair(i, run)

    def upper(i):
        first, count = ((0, 4), (4, 4), (8, 2))[i]

        @pl.loop(first, first + count)
        def _(b):
            rows = pl.ds(pl.multiple_of(b * 256, 256), 256)
            f, d = f_in[rows, :], d_in[rows, :]
            df = f * d
            pu = d * df + pun[rows, :]
            pun[rows, :] = pu
            acc[2] += folded(f * pu)
            acc[3] += folded(df * pu)
            acc[4] += folded(pu * pu)

    arrive(2)
    upper(2)
    second_adjoint(0)
    arrive(0)
    upper(0)
    second_adjoint(1)
    exchange_wait(1, obs_s, obs_r)
    right = jnp.concatenate(split2(obs_r[...].reshape(SLOTS, 128)), axis=1)
    seen = halves(jnp.dot(pt_mat[...], right, preferred_element_type=F32))
    pm = weight * (rvar[...] * wrd + seen)
    pm_out[...] = pm
    acc[2] += folded(wd * pm)
    acc[3] += folded(wrd * pm)
    acc[4] += folded(pm * pm)

    arrive(1)
    upper(1)
    for i, src, dst in ((0, send_a, recv_a), (1, obs_s, obs_r), (2, send_b, recv_b)):
        exchange_sent(i, src, dst)
    for copy in [f_halo, d_halo, c_west, c_east, z_edge1, z_edge2] + f_send:
        copy.wait_send()
    for copy in edges + closings:
        copy.wait_send()
    second_adjoint(2)

    lines = [jnp.sum(acc[i], axis=0, keepdims=True) for i in range(5)]
    red[...] = jnp.concatenate(lines + [jnp.zeros((3, 128), F32)], axis=0)

    place_in, place_out = lax.rem(c, INNER), s * (n // INNER) + c // INNER
    first = c - place_in

    def share(d):
        to = lax.rem(place_in + d, INNER)
        return rcopy(red, redbuf.at[place_in], r_ss.at[d], r_rs.at[d], (s, first + to))

    for d in range(1, INNER):
        share(d).start()
    redbuf[place_in] = red[...]
    for y in range(2):
        put_last(v2n, y, closing[LAST + y])
    for d in range(1, INNER):
        peer = lax.rem(place_in + INNER - d, INNER)
        rcopy(red, redbuf.at[peer], r_ss.at[d], r_rs.at[d], (s, first + peer)).wait_recv()
    zred[...] = jnp.sum(redbuf[...], axis=0)
    outer = n * nt // INNER

    def share_out(d):
        to = lax.rem(place_out + d, outer)
        where = (to // (n // INNER), lax.rem(to, n // INNER) * INNER + place_in)
        return rcopy(
            zred, zbuf.at[place_out], r_ss.at[INNER + d], r_rs.at[INNER + d], where
        )

    for d in range(1, outer):
        share_out(d).start()
    zbuf[place_out] = zred[...]
    for d in range(1, outer):
        peer = lax.rem(place_out + outer - d, outer)
        where = (peer // (n // INNER), lax.rem(peer, n // INNER) * INNER + place_in)
        rcopy(zred, zbuf.at[peer], r_ss.at[INNER + d], r_rs.at[INNER + d], where).wait_recv()

    total = jnp.sum(jnp.sum(zbuf[...], axis=0), axis=1, keepdims=True)
    total = jnp.broadcast_to(total, (8, 128))
    rq, qq, rp, qp, pp = (total[i:i + 1, :] for i in range(5))
    step1 = rq / qq
    step2 = step1 * (step1 * qp - rp) / (qq - 2.0 * step1 * qp + step1 * step1 * pp)
    sc_out[...] = jnp.concatenate(
        [step1 + step2, step1 * step2, jnp.zeros((6, 128), F32)], axis=0
    )

    for d in range(1, INNER):
        share(d).wait_send()
    for d in range(1, outer):
        share_out(d).wait_send()
    for copy in d_send:
        copy.wait_send()


def finish_kernel(
    sc, f_in, d_in, v1, v2, pu, wd_in, wrd_in, pm,
    ms_out, rs_out, xs_out, mr_out, rr_out, xr_out,
    ms, rs, xs, mr, rr, xr, sem,
):
    t, q = sc[0:1, :], sc[1:2, :]
    parts = 5
    size = ms.shape[0] // parts
    copies = []

    def send(i, src, dst):
        copy = pltpu.make_async_copy(src, dst, sem.at[i])
        copy.start()
        copies.append(copy)

    for i in range(parts):
        rows = pl.ds(i * size, size)
        f, v = f_in[rows, :], v1[rows, :]
        df = f * d_in[rows, :]
        ms[rows, :] = t * f - q * df
        mr[rows, :] = f - t * df + q * pu[rows, :]
        xs[rows, :] = -(q * v)
        xr[rows, :] = q * v2[rows, :] - t * v
        for j, (src, dst) in enumerate(
            ((ms, ms_out), (mr, mr_out), (xs, xs_out), (xr, xr_out))
        ):
            send(4 * i + j, src.at[rows, :], dst.at[rows, :])
    wd, wrd = wd_in[...], wrd_in[...]
    rs[...] = t * wd - q * wrd
    rr[...] = wd - t * wrd + q * pm[...]
    send(4 * parts, rs, rs_out)
    send(4 * parts + 1, rr, rr_out)
    for copy in copies:
        copy.wait()


def to_rows(x):
    a, b, y, w = x.shape
    return x.reshape(a, b, y, w // 128, 128).transpose(0, 1, 3, 2, 4).reshape(-1, 128)


def from_rows(x, shape):
    a, b, y, w = shape
    return x.reshape(a, b, w // 128, y, 128).transpose(0, 1, 3, 2, 4).reshape(shape)


def body(n, nt, forcing_state, model_error, courant, vertical_mix, radiance_jacobian,
         innovation, report_error, report_column, report_slot, report_count):
    f, d, wind = (to_rows(x[0]) for x in (forcing_state, model_error, courant))
    inn, rvar, cnt = innovation[0], report_error[0], report_count[0]
    size = f.shape[0]
    vmem = pl.BlockSpec(memory_space=pltpu.VMEM)
    hbm = pl.BlockSpec(memory_space=pltpu.HBM)
    V = pltpu.VMEM
    state = jax.ShapeDtypeStruct((size, 128), F32)
    reports = jax.ShapeDtypeStruct((ROWS, CHANNELS), F32)
    span, cap = WIDTH + HALO, SLOTS // n
    dma = pltpu.SemaphoreType.DMA
    inputs = (
        f, d, wind, vertical_mix, radiance_jacobian, inn, rvar, report_column, report_slot, cnt,
    )
    inputs = tuple(pltpu.with_memory_space_constraint(x, pltpu.HBM) for x in inputs)
    results = pl.pallas_call(
        functools.partial(system_kernel, n, nt),
        out_shape=(state,) * 5 + (reports,) * 3 + (jax.ShapeDtypeStruct((8, 128), F32),),
        in_specs=[hbm] * 10,
        out_specs=(vmem,) * 9,
        scratch_shapes=[V(x.shape, x.dtype) for x in inputs[2:]] + [
            V((10, WIDTH, 128), F32), V((10, WIDTH, 128), F32), V((size, 128), F32),
            V((10, span, 128), F32), V((10, span, 128), F32),
            V((6 * STEPS, span + HALO, 128), F32),
            V((10, span, 128), F32), V((10, WIDTH, 128), F32), V((10, WIDTH, 128), F32),
            V((2, STEPS * LAT, span, 128), F32), V((STEPS * LAT, WIDTH, 128), F32),
            V((STEPS * CELLS, 256), BF16), V((SLOTS, 256), BF16), V((8, SLOTS), F32), V((SLOTS, 128), F32),
            V((3, 256, 256), BF16), V((3, 256, 256), BF16),
            V((4, 256, 256), BF16), V((4, 256, 256), BF16),
            V((SLOTS, ROWS), BF16), V((ROWS, SLOTS), BF16),
            V((n, 8 + cap, 128), F32), V((n, 8 + cap, 128), F32),
            V((n, cap, 128), F32), V((n, cap, 128), F32),
            V((n, cap, 128), F32), V((n, cap, 128), F32),
            V((5, 8, 128), F32), V((8, 128), F32), V((INNER, 8, 128), F32),
            V((8, 128), F32), V((n * nt // INNER, 8, 128), F32),
            dma((10,)), dma((3,)), dma((3,)), dma((6,)), dma((6,)),
            dma((6,)), dma((6,)), dma((3,)), dma((3,)), dma((3,)), dma((3,)),
            dma((INNER + n * nt // INNER,)), dma((INNER + n * nt // INNER,)),
        ],
        compiler_params=pltpu.CompilerParams(
            collective_id=0, has_side_effects=True, vmem_limit_bytes=42 * 1024 * 1024
        ),
        cost_estimate=pl.CostEstimate(flops=40 * 10**9, bytes_accessed=10**7, transcendentals=0),
    )(*inputs)
    fv, dv, v1, v2, pu, wd, wrd, pm, sc = results
    outs = (state, reports, state, state, reports, state)
    ms, rs, xs, mr, rr, xr = pl.pallas_call(
        finish_kernel,
        out_shape=outs,
        in_specs=[vmem] * 9,
        out_specs=(pl.BlockSpec(memory_space=pl.ANY),) * 6,
        scratch_shapes=[V(x.shape, x.dtype) for x in outs] + [dma((22,))],
        compiler_params=pltpu.CompilerParams(vmem_limit_bytes=16 * 1024 * 1024),
    )(sc, fv, dv, v1, v2, pu, wd, wrd, pm)
    shape = forcing_state.shape[1:]
    ms, xs, mr, xr = (from_rows(x, shape)[None] for x in (ms, xs, mr, xr))
    return ms, rs[None], xs, mr, rr[None], xr


def solution(mesh):
    grid = P("tm", None, None, None, "col")
    reports = P("tm", "col", None)
    in_specs = (
        grid, grid, grid, P(), P(), reports, reports, P("tm", "col"), P("tm", "col"), reports,
    )
    out_specs = (grid, reports, grid, grid, reports, grid)
    run = functools.partial(body, mesh.shape["col"], mesh.shape["tm"])
    return jax.shard_map(run, mesh=mesh, in_specs=in_specs, out_specs=out_specs, check_vma=False)
```

```python
import functools

import jax
import jax.numpy as jnp
from jax import lax
from jax.experimental import pallas as pl
from jax.experimental.pallas import tpu as pltpu
from jax.sharding import PartitionSpec as P

F32, BF16, I32 = jnp.float32, jnp.bfloat16, jnp.int32
MESH = pl.DeviceIdType.MESH
LEVELS, LAT, WIDTH, STEPS, CHANNELS = 64, 4, 256, 4, 128
ROWS, INST = 512, 4
INST_ROWS = ROWS // INST
SLOTS = 2 * ROWS
CELLS = LAT * WIDTH
HALO, EDGE = 16, 8
INNER = 8
LAST = 8
GROUPS = ((0, 4), (4, 4), (8, 2))


def split2(x):
    hi = x.astype(BF16)
    return hi, (x - hi.astype(F32)).astype(BF16)


def pack(w):
    row = jnp.concatenate(split2(w), axis=1)
    return jnp.concatenate([row, row], axis=0)


def halves(o):
    return o[:, :128] + o[:, 128:]


def mm(u, w):
    left = jnp.concatenate(split2(u), axis=1)
    return halves(jnp.dot(left, w, preferred_element_type=F32))


def native_rows(block, y, xt, count):
    return pl.ds(block * LEVELS * 2 * LAT + xt * LAT + y, count, stride=2 * LAT)


def load_pair(ref, g, y, xt):
    return ref[native_rows(2 * g, y, xt, 128), :]


def load_last(ref, y, xt):
    top = ref[native_rows(4, y, xt, 64), :]
    low = ref[native_rows(4, y + 2, xt, 64), :]
    return jnp.concatenate([top, low], axis=0)


def folded(x):
    return jnp.sum(x.reshape(x.shape[0] // 8, 8, 128), axis=0)


def system_kernel(
    n, nt,
    f_hbm, d_hbm, c_hbm, vm_hbm, jac_hbm, inn_hbm, rvar_hbm, col_hbm, slot_hbm, cnt_hbm,
    f_in, d_in, v1n, v2n, pun, wd_out, wrd_out, pm_out, sc_out,
    c_in, vm, jac, inn, rvar, col, slot, cnt,
    f_t, df_t, rf, rd, c_t, v1, closing, arr, z, yacc, ysplit, rowsplit, keyrow, keycol,
    wa, wf, jf, jt, p_mat, pt_mat, send_a, recv_a, send_b, recv_b, obs_s, obs_r,
    acc, red, redbuf, zred, zbuf,
    in_s, a2a_ss, a2a_rs, z_ss, z_rs, h_ss, h_rs, vh_ss, vh_rs, zz_ss, zz_rs, r_ss, r_rs,
):
    cap = SLOTS // n
    s, c = lax.axis_index("tm"), lax.axis_index("col")
    prev_s, next_s = lax.rem(s + nt - 1, nt), lax.rem(s + 1, nt)
    west, east = lax.rem(c + n - 1, n), lax.rem(c + 1, n)

    def rcopy(src, dst, ss, rs, to):
        return pltpu.make_async_remote_copy(
            src_ref=src, dst_ref=dst, send_sem=ss, recv_sem=rs, device_id=to, device_id_type=MESH
        )

    def z_send(src, dst, base, to):
        rest = []
        for i, (k0, kn) in enumerate(GROUPS):
            rest.append(
                rcopy(
                    src.at[pl.ds(k0, kn)], dst.at[pl.ds(k0, kn), pl.ds(0, WIDTH)],
                    z_ss.at[base + i], z_rs.at[base + i], to,
                )
            )
        return rest

    def z_halo(src, dst, i):
        return rcopy(
            src.at[:, pl.ds(0, EDGE)], dst.at[:, pl.ds(WIDTH, EDGE)],
            h_ss.at[i], h_rs.at[i], (prev_s, west),
        )

    def exchange_start(i, src, dst):
        for d in range(1, n):
            peer = (c + d) & (n - 1)
            rcopy(src.at[peer], dst.at[c], a2a_ss.at[i], a2a_rs.at[i], (s, peer)).start()
        dst[c] = src[c]

    def exchange_all(i, src, dst):
        every = pl.ds(0, n - 1)
        return rcopy(src.at[every], dst.at[every], a2a_ss.at[i], a2a_rs.at[i], (s, east))

    def exchange_wait(i, src, dst):
        exchange_all(i, src, dst).wait_recv()

    def exchange_sent(i, src, dst):
        exchange_all(i, src, dst).wait_send()

    pairs = (
        (f_hbm, f_in), (col_hbm, col), (slot_hbm, slot), (cnt_hbm, cnt), (inn_hbm, inn),
        (rvar_hbm, rvar), (c_hbm, c_in), (vm_hbm, vm), (jac_hbm, jac), (d_hbm, d_in),
    )
    loads = [pltpu.make_async_copy(a, b, in_s.at[i]) for i, (a, b) in enumerate(pairs)]
    for load in loads:
        load.start()

    barrier = pltpu.get_barrier_semaphore()

    def greet(to):
        pl.semaphore_signal(barrier, inc=1, device_id=to, device_id_type=MESH)

    greet((prev_s, west))
    greet((next_s, east))

    @pl.loop(1, nt)
    def _(d):
        greet((lax.rem(s + d, nt), c))

        @pl.loop(1, n // INNER)
        def _(e):
            greet((lax.rem(s + d, nt), lax.rem(c + e * INNER, n)))

    @pl.loop(1, n)
    def _(d):
        greet((s, lax.rem(c + d, n)))

    loads[0].wait()

    @pl.loop(0, 8)
    def _(k):
        for xt in range(2):
            f_t[k, pl.ds(xt * 128, 128), :] = load_pair(f_in, k // 4, k % 4, xt).T

    @pl.loop(0, 2)
    def _(y):
        for xt in range(2):
            f_t[8 + y, pl.ds(xt * 128, 128), :] = load_last(f_in, y, xt).T

    rows_iota = lax.broadcasted_iota(I32, (ROWS, ROWS), 0)
    lane_iota = lax.broadcasted_iota(I32, (ROWS, ROWS), 1)
    upper_ones = jnp.where(rows_iota <= lane_iota, 1.0, 0.0).astype(BF16)
    for load in loads[1:4]:
        load.wait()
    column = col[...]
    shift_w, mask_n = WIDTH.bit_length() - 1, n - 1
    owner = (column >> shift_w) & mask_n
    cell = (column >> (shift_w + n.bit_length() - 1)) * WIDTH + (column & (WIDTH - 1))
    key = (slot[...] * CELLS + cell).astype(F32)
    owners = lax.broadcasted_iota(I32, (n, ROWS), 0)
    owned = jnp.where(owners == owner, 1.0, 0.0)
    ranks = jnp.dot(owned.astype(BF16), upper_ones, preferred_element_type=F32)
    landing = jnp.sum(owned * ((owners * cap).astype(F32) + ranks - 1.0), axis=0, keepdims=True)

    def as_column(row, b):
        return jnp.broadcast_to(row[:, b * 128:(b + 1) * 128], (128, 128)).T

    for b in range(SLOTS // 128):
        spots = (lax.broadcasted_iota(I32, (128, ROWS), 0) + b * 128).astype(F32)
        p_mat[b * 128:(b + 1) * 128, :] = jnp.where(spots == landing, 1.0, 0.0).astype(BF16)
    spots = lax.broadcasted_iota(I32, (128, SLOTS), 1).astype(F32)
    for b in range(ROWS // 128):
        land_col = jnp.concatenate([as_column(landing, b)] * (SLOTS // 128), axis=1)
        pt_mat[b * 128:(b + 1) * 128, :] = jnp.where(spots == land_col, 1.0, 0.0).astype(BF16)

    def split3(x):
        hi, rest = x.astype(BF16), x - x.astype(BF16).astype(F32)
        return (hi,) + split2(rest)

    loads[4].wait()
    loads[5].wait()
    inst_iota = lax.broadcasted_iota(I32, (INST_ROWS, CHANNELS), 0)
    weight = jnp.concatenate(
        [jnp.where(inst_iota < cnt[0:1, i:i + 1], 1.0, 0.0) for i in range(INST)], axis=0
    )
    wd = weight * inn[...]
    wrd = weight * (rvar[...] * wd)
    wd_out[...] = wd
    wrd_out[...] = wrd
    right = jnp.concatenate(split3(wd) + split3(wrd), axis=1)
    per, lots = 256 // cap, 128 // cap
    for b in range(4):
        o = jnp.dot(p_mat[b * 256:(b + 1) * 256, :], right, preferred_element_type=F32)
        o = [o[:, i * 128:(i + 1) * 128] for i in range(6)]
        owners_here = slice(b * per, (b + 1) * per)
        send_a[owners_here, 8:, :] = (o[0] + o[1] + o[2]).reshape(per, cap, 128)
        send_b[owners_here, :, :] = (o[3] + o[4] + o[5]).reshape(per, cap, 128)
    keys = 0.0
    for part in split2(jnp.broadcast_to(key, (16, ROWS))):
        keys = keys + lax.dot_general(
            part, p_mat[...], (((1,), (1,)), ((), ())), preferred_element_type=F32
        )
    for o in range(n):
        b = o // lots
        send_a[o, 0:8, :] = keys[0:8, b * 128:(b + 1) * 128]

    pl.semaphore_wait(barrier, n + nt + (nt - 1) * (n // INNER - 1))
    f_halo = z_halo(f_t, rf, 0)
    f_halo.start()
    f_send = z_send(f_t, rf, 0, (prev_s, c))
    for i in (2, 0, 1):
        f_send[i].start()
    exchange_start(0, send_a, recv_a)

    acc[...] = jnp.zeros_like(acc)

    loads[6].wait()

    def wind(m, y, xt):
        return c_in[native_rows(m, y, xt, 64), :]

    @pl.loop(0, STEPS * LAT)
    def _(i):
        m, y = i // LAT, i % LAT
        for xt in range(2):
            one = wind(m, y, xt)
            c_t[m * 6 + y, pl.ds(HALO + xt * 128, 128), :] = jnp.concatenate([one, one], axis=0).T

    @pl.loop(0, STEPS * 2)
    def _(i):
        m, y = i // 2, i % 2
        for xt in range(2):
            both = jnp.concatenate([wind(m, y, xt), wind(m, y + 2, xt)], axis=0)
            c_t[m * 6 + 4 + y, pl.ds(HALO + xt * 128, 128), :] = both.T

    c_west = rcopy(
        c_t.at[:, pl.ds(HALO, EDGE)], c_t.at[:, pl.ds(HALO + WIDTH, EDGE)],
        h_ss.at[2], h_rs.at[2], (s, west),
    )
    c_east = rcopy(
        c_t.at[:, pl.ds(WIDTH + HALO - EDGE, EDGE)], c_t.at[:, pl.ds(HALO - EDGE, EDGE)],
        h_ss.at[3], h_rs.at[3], (s, east),
    )
    c_west.start()
    c_east.start()
    exchange_start(2, send_b, recv_b)
    loads[9].wait()

    @pl.loop(0, 8)
    def _(k):
        for xt in range(2):
            g, y = k // 4, k % 4
            df_t[k, pl.ds(xt * 128, 128), :] = (
                load_pair(f_in, g, y, xt) * load_pair(d_in, g, y, xt)
            ).T

    @pl.loop(0, 2)
    def _(y):
        for xt in range(2):
            df_t[8 + y, pl.ds(xt * 128, 128), :] = (
                load_last(f_in, y, xt) * load_last(d_in, y, xt)
            ).T

    d_halo = z_halo(df_t, rd, 1)
    d_halo.start()
    d_send = z_send(df_t, rd, 3, (prev_s, c))
    for copy in d_send:
        copy.start()

    loads[7].wait()
    loads[8].wait()

    eye = jnp.where(
        lax.broadcasted_iota(I32, (64, 64), 0) == lax.broadcasted_iota(I32, (64, 64), 1), 1.0, 0.0
    )
    nothing = jnp.zeros((64, 64), F32)
    for g, (fa, fb) in enumerate(((0, 1), (2, 3), (4, 4))):
        ma, mb = 0.6 * eye + 0.4 * vm[fa], 0.6 * eye + 0.4 * vm[fb]
        block = jnp.concatenate(
            [jnp.concatenate([ma, nothing], axis=1), jnp.concatenate([nothing, mb], axis=1)],
            axis=0,
        )
        wa[g] = pack(block)
        wf[g] = pack(block.T)
    none = jnp.zeros((64, CHANNELS), F32)
    last = jac[256:320, :]
    for g, block in enumerate(
        (
            jac[0:128, :], jac[128:256, :],
            jnp.concatenate([last, none], axis=0), jnp.concatenate([none, last], axis=0),
        )
    ):
        jf[g] = pack(block)
        jt[g] = pack(block.T)

    exchange_wait(0, send_a, recv_a)
    meta = pltpu.roll(recv_a[:, 0, :], lax.rem(128 - cap * lax.rem(c, lots), 128), 1)
    lane = lax.broadcasted_iota(I32, (n, 128), 1)
    meta = jnp.where(lane < cap, meta, 0.0)
    tiled = meta
    for i in range(1, lots):
        tiled = tiled + pltpu.roll(meta, cap * i, 1)
    tiled = jnp.concatenate([tiled] * (SLOTS // 128), axis=1)
    sender = lax.broadcasted_iota(I32, (n, SLOTS), 0)
    place = lax.broadcasted_iota(I32, (n, SLOTS), 1)
    mine = (place >= sender * cap) & (place < sender * cap + cap)
    keyrow[...] = jnp.broadcast_to(
        jnp.sum(jnp.where(mine, tiled, 0.0), axis=0, keepdims=True), (8, SLOTS)
    )

    def scatter(r, rows):
        rowsplit[...] = jnp.concatenate(split2(rows.reshape(SLOTS, 128)), axis=1)

        @pl.loop(0, STEPS * LAT)
        def _(i):
            spot = (lax.broadcasted_iota(I32, (WIDTH, SLOTS), 0) + i * WIDTH).astype(F32)
            hit = jnp.where(spot == keyrow[0:1, :], 1.0, 0.0).astype(BF16)
            o = jnp.dot(hit, rowsplit[...], preferred_element_type=F32)
            z[r, i, pl.ds(0, WIDTH), :] = halves(o)

        edge = rcopy(
            z.at[r, pl.ds(LAT, 3 * LAT), pl.ds(0, EDGE)],
            z.at[r, pl.ds(LAT, 3 * LAT), pl.ds(WIDTH, EDGE)],
            h_ss.at[4 + r], h_rs.at[4 + r], (s, west),
        )
        edge.start()
        return edge

    z_edge1 = scatter(0, recv_a[:, 8:, :])

    @pl.loop(0, SLOTS // 128)
    def _(b):
        lanes = pl.ds(pl.multiple_of(b * 128, 128), 128)
        keycol[lanes, :] = jnp.broadcast_to(keyrow[0:1, lanes], (128, 128)).T

    later = jnp.where(s < nt - 1, -1.0, 0.0).astype(F32)
    span = WIDTH + HALO

    def block(x, first, rows, count):
        return x[pl.ds(first, 2), pl.ds(rows, count), :].reshape(2 * count, 128)

    def adjoint(r, k, g, y, received, own):
        a = block(received, k, 0, span) * later
        wind_at = 4 if k is LAST else y
        for m in reversed(range(STEPS)):
            w = mm(a, wa[g])
            p = block(c_t, m * 6 + wind_at, HALO, span) * w
            if k is LAST:
                inject = mm(block(z.at[r], m * LAT, 0, span), jt[2])
                inject = inject + mm(block(z.at[r], m * LAT + 2, 0, span), jt[3])
            else:
                inject = mm(block(z.at[r], m * LAT + y, 0, span), jt[g])
            a = w - p + pltpu.roll(p, 2 * span - 1, 0) + inject
        a = a.reshape(2, span, 128)
        return [own[k + i] + a[i, 0:WIDTH, :] for i in range(2)]

    def forward(k, g, y):
        v = block(v1, k, 0, span)
        wind_at = 4 if k is LAST else y
        for m in range(STEPS):
            inner = v.reshape(2, span, 128)[:, HALO:, :].reshape(2 * WIDTH, 128)
            if k is LAST:
                yacc[pl.ds(m * LAT, 2)] += mm(inner, jf[2]).reshape(2, WIDTH, 128)
                yacc[pl.ds(m * LAT + 2, 2)] += mm(inner, jf[3]).reshape(2, WIDTH, 128)
            else:
                yacc[pl.ds(m * LAT + y, 2)] += mm(inner, jf[g]).reshape(2, WIDTH, 128)
            wind_now = block(c_t, m * 6 + wind_at, 0, span)
            v = mm(v - wind_now * (v - pltpu.roll(v, 1, 0)), wf[g])
        closing[pl.ds(k, 2)] = v.reshape(2, span, 128)[:, HALO:, :]

    def each_pair(i, run):
        if i < 2:
            @pl.loop(0, 2)
            def _(j):
                run(4 * i + 2 * j, i, 2 * j)
        else:
            run(LAST, 2, 0)

    def put_pair(ref, g, y, value):
        for xt in range(2):
            ref[native_rows(2 * g, y, xt, 128), :] = value[xt * 128:(xt + 1) * 128, :].T

    def put(ref, k, g, y, value):
        if g == 2:
            put_last(ref, y, value)
        else:
            put_pair(ref, g, y, value)

    def put_last(ref, y, value):
        for xt in range(2):
            turned = value[xt * 128:(xt + 1) * 128, :].T
            ref[native_rows(4, y, xt, 64), :] = turned[:64, :]
            ref[native_rows(4, y + 2, xt, 64), :] = turned[64:, :]

    yacc[...] = jnp.zeros_like(yacc)
    c_west.wait_recv()
    c_east.wait_recv()
    f_halo.wait_recv()
    z_edge1.wait_recv()

    def edge_v1(i):
        k0, kn = GROUPS[i]
        return rcopy(
            v1.at[pl.ds(k0, kn), pl.ds(WIDTH + HALO - EDGE, EDGE)],
            v1.at[pl.ds(k0, kn), pl.ds(HALO - EDGE, EDGE)],
            vh_ss.at[i], vh_rs.at[i], (s, east),
        )

    def send_closing(i):
        k0, kn = GROUPS[i]
        return rcopy(
            closing.at[pl.ds(k0, kn)], arr.at[pl.ds(k0, kn)],
            zz_ss.at[i], zz_rs.at[i], (next_s, c),
        )

    edges = [edge_v1(i) for i in range(3)]
    closings = [send_closing(i) for i in range(3)]

    def first_adjoint(i):
        f_send[i].wait_recv()

        def run(k, g, y):
            for j, value in enumerate(adjoint(0, k, g, y, rf, f_t)):
                v1[k + j, pl.ds(HALO, WIDTH), :] = value
                acc[1] += folded(value * value)
                put(v1n, k + j, g, y + j, value)

        each_pair(i, run)
        edges[i].start()

    def first_forward(i):
        edges[i].wait_recv()
        each_pair(i, forward)
        closings[i].start()

    first_adjoint(2)
    first_adjoint(0)
    first_forward(2)
    first_forward(0)
    exchange_wait(2, send_b, recv_b)
    z_edge2 = scatter(1, recv_b[...])
    first_adjoint(1)

    @pl.loop(0, 10)
    def _(i):
        rows = pl.ds(pl.multiple_of(i * 256, 256), 256)
        f = f_in[rows, :]
        df = f * d_in[rows, :]
        acc[0] += folded(f * df)
        acc[1] += folded(df * df)

    acc[0] += folded(wd * wrd)
    acc[1] += folded(wrd * wrd)

    first_forward(1)

    @pl.loop(0, STEPS * LAT)
    def _(i):
        ysplit[pl.ds(pl.multiple_of(i * WIDTH, WIDTH), WIDTH), :] = jnp.concatenate(
            split2(yacc[i]), axis=1
        )

    @pl.loop(0, 4)
    def _(b):
        took = keycol[pl.ds(pl.multiple_of(b * 256, 256), 256), :]
        at = jnp.concatenate([took] * (CELLS // 128), axis=1)
        total = jnp.zeros((256, 256), F32)
        for m in range(STEPS):
            spot = (lax.broadcasted_iota(I32, (256, CELLS), 1) + m * CELLS).astype(F32)
            hit = jnp.where(spot == at, 1.0, 0.0).astype(BF16)
            total = total + jnp.dot(
                hit, ysplit[m * CELLS:(m + 1) * CELLS, :], preferred_element_type=F32
            )
        obs_s[pl.ds(pl.multiple_of(b * per, per), per)] = halves(total).reshape(per, cap, 128)

    exchange_start(1, obs_s, obs_r)

    d_halo.wait_recv()
    z_edge2.wait_recv()

    def second_adjoint(i):
        d_send[i].wait_recv()

        def run(k, g, y):
            for j, value in enumerate(adjoint(1, k, g, y, rd, df_t)):
                own = v1[k + j, pl.ds(HALO, WIDTH), :]
                acc[3] += folded(own * value)
                acc[4] += folded(value * value)
                if g == 2:
                    closing[k + j] = value
                else:
                    put(v2n, k + j, g, y + j, value)

        each_pair(i, run)

    has_before = jnp.where(s > 0, 1.0, 0.0).astype(F32)

    def arrive(i):
        closings[i].wait_recv()
        def run(k, g, y):
            for j in range(2):
                value = v1[k + j, pl.ds(HALO, WIDTH), :] - has_before * arr[k + j]
                put(pun, k + j, g, y + j, value)

        each_pair(i, run)

    def upper(i):
        first, count = ((0, 4), (4, 4), (8, 2))[i]

        @pl.loop(first, first + count)
        def _(b):
            rows = pl.ds(pl.multiple_of(b * 256, 256), 256)
            f, d = f_in[rows, :], d_in[rows, :]
            df = f * d
            pu = d * df + pun[rows, :]
            pun[rows, :] = pu
            acc[2] += folded(f * pu)
            acc[3] += folded(df * pu)
            acc[4] += folded(pu * pu)

    arrive(2)
    upper(2)
    second_adjoint(0)
    arrive(0)
    upper(0)
    second_adjoint(1)
    exchange_wait(1, obs_s, obs_r)
    right = jnp.concatenate(split2(obs_r[...].reshape(SLOTS, 128)), axis=1)
    seen = halves(jnp.dot(pt_mat[...], right, preferred_element_type=F32))
    pm = weight * (rvar[...] * wrd + seen)
    pm_out[...] = pm
    acc[2] += folded(wd * pm)
    acc[3] += folded(wrd * pm)
    acc[4] += folded(pm * pm)

    arrive(1)
    upper(1)
    for i, src, dst in ((0, send_a, recv_a), (1, obs_s, obs_r), (2, send_b, recv_b)):
        exchange_sent(i, src, dst)
    for copy in [f_halo, d_halo, c_west, c_east, z_edge1, z_edge2] + f_send:
        copy.wait_send()
    for copy in edges + closings:
        copy.wait_send()
    second_adjoint(2)

    lines = [jnp.sum(acc[i], axis=0, keepdims=True) for i in range(5)]
    red[...] = jnp.concatenate(lines + [jnp.zeros((3, 128), F32)], axis=0)

    place_in, place_out = lax.rem(c, INNER), s * (n // INNER) + c // INNER
    first = c - place_in

    def share(d):
        to = lax.rem(place_in + d, INNER)
        return rcopy(red, redbuf.at[place_in], r_ss.at[d], r_rs.at[d], (s, first + to))

    for d in range(1, INNER):
        share(d).start()
    redbuf[place_in] = red[...]
    for y in range(2):
        put_last(v2n, y, closing[LAST + y])
    for d in range(1, INNER):
        peer = lax.rem(place_in + INNER - d, INNER)
        rcopy(red, redbuf.at[peer], r_ss.at[d], r_rs.at[d], (s, first + peer)).wait_recv()
    zred[...] = jnp.sum(redbuf[...], axis=0)
    outer = n * nt // INNER

    def share_out(d):
        to = lax.rem(place_out + d, outer)
        where = (to // (n // INNER), lax.rem(to, n // INNER) * INNER + place_in)
        return rcopy(
            zred, zbuf.at[place_out], r_ss.at[INNER + d], r_rs.at[INNER + d], where
        )

    for d in range(1, outer):
        share_out(d).start()
    zbuf[place_out] = zred[...]
    for d in range(1, outer):
        peer = lax.rem(place_out + outer - d, outer)
        where = (peer // (n // INNER), lax.rem(peer, n // INNER) * INNER + place_in)
        rcopy(zred, zbuf.at[peer], r_ss.at[INNER + d], r_rs.at[INNER + d], where).wait_recv()

    total = jnp.sum(jnp.sum(zbuf[...], axis=0), axis=1, keepdims=True)
    total = jnp.broadcast_to(total, (8, 128))
    rq, qq, rp, qp, pp = (total[i:i + 1, :] for i in range(5))
    step1 = rq / qq
    step2 = step1 * (step1 * qp - rp) / (qq - 2.0 * step1 * qp + step1 * step1 * pp)
    sc_out[...] = jnp.concatenate(
        [step1 + step2, step1 * step2, jnp.zeros((6, 128), F32)], axis=0
    )

    for d in range(1, INNER):
        share(d).wait_send()
    for d in range(1, outer):
        share_out(d).wait_send()
    for copy in d_send:
        copy.wait_send()


def finish_kernel(
    sc, f_in, d_in, v1, v2, pu, wd_in, wrd_in, pm,
    ms_out, rs_out, xs_out, mr_out, rr_out, xr_out,
    ms, rs, xs, mr, rr, xr, sem,
):
    t, q = sc[0:1, :], sc[1:2, :]
    parts = 5
    size = ms.shape[0] // parts
    copies = []

    def send(i, src, dst):
        copy = pltpu.make_async_copy(src, dst, sem.at[i])
        copy.start()
        copies.append(copy)

    for i in range(parts):
        rows = pl.ds(i * size, size)
        f, v = f_in[rows, :], v1[rows, :]
        df = f * d_in[rows, :]
        ms[rows, :] = t * f - q * df
        mr[rows, :] = f - t * df + q * pu[rows, :]
        xs[rows, :] = -(q * v)
        xr[rows, :] = q * v2[rows, :] - t * v
        for j, (src, dst) in enumerate(
            ((ms, ms_out), (mr, mr_out), (xs, xs_out), (xr, xr_out))
        ):
            send(4 * i + j, src.at[rows, :], dst.at[rows, :])
    wd, wrd = wd_in[...], wrd_in[...]
    rs[...] = t * wd - q * wrd
    rr[...] = wd - t * wrd + q * pm[...]
    send(4 * parts, rs, rs_out)
    send(4 * parts + 1, rr, rr_out)
    for copy in copies:
        copy.wait()


def to_rows(x):
    a, b, y, w = x.shape
    return x.reshape(a, b, y, w // 128, 128).transpose(0, 1, 3, 2, 4).reshape(-1, 128)


def from_rows(x, shape):
    a, b, y, w = shape
    return x.reshape(a, b, w // 128, y, 128).transpose(0, 1, 3, 2, 4).reshape(shape)


def body(n, nt, forcing_state, model_error, courant, vertical_mix, radiance_jacobian,
         innovation, report_error, report_column, report_slot, report_count):
    f, d, wind = (to_rows(x[0]) for x in (forcing_state, model_error, courant))
    inn, rvar, cnt = innovation[0], report_error[0], report_count[0]
    size = f.shape[0]
    vmem = pl.BlockSpec(memory_space=pltpu.VMEM)
    hbm = pl.BlockSpec(memory_space=pltpu.HBM)
    V = pltpu.VMEM
    state = jax.ShapeDtypeStruct((size, 128), F32)
    reports = jax.ShapeDtypeStruct((ROWS, CHANNELS), F32)
    span, cap = WIDTH + HALO, SLOTS // n
    dma = pltpu.SemaphoreType.DMA
    inputs = (
        f, d, wind, vertical_mix, radiance_jacobian, inn, rvar, report_column, report_slot, cnt,
    )
    inputs = tuple(pltpu.with_memory_space_constraint(x, pltpu.HBM) for x in inputs)
    results = pl.pallas_call(
        functools.partial(system_kernel, n, nt),
        out_shape=(state,) * 5 + (reports,) * 3 + (jax.ShapeDtypeStruct((8, 128), F32),),
        in_specs=[hbm] * 10,
        out_specs=(vmem,) * 9,
        scratch_shapes=[V(x.shape, x.dtype) for x in inputs[2:]] + [
            V((10, WIDTH, 128), F32), V((10, WIDTH, 128), F32),
            V((10, span, 128), F32), V((10, span, 128), F32),
            V((6 * STEPS, span + HALO, 128), F32),
            V((10, span, 128), F32), V((10, WIDTH, 128), F32), V((10, WIDTH, 128), F32),
            V((2, STEPS * LAT, span, 128), F32), V((STEPS * LAT, WIDTH, 128), F32),
            V((STEPS * CELLS, 256), BF16), V((SLOTS, 256), BF16), V((8, SLOTS), F32), V((SLOTS, 128), F32),
            V((3, 256, 256), BF16), V((3, 256, 256), BF16),
            V((4, 256, 256), BF16), V((4, 256, 256), BF16),
            V((SLOTS, ROWS), BF16), V((ROWS, SLOTS), BF16),
            V((n, 8 + cap, 128), F32), V((n, 8 + cap, 128), F32),
            V((n, cap, 128), F32), V((n, cap, 128), F32),
            V((n, cap, 128), F32), V((n, cap, 128), F32),
            V((5, 8, 128), F32), V((8, 128), F32), V((INNER, 8, 128), F32),
            V((8, 128), F32), V((n * nt // INNER, 8, 128), F32),
            dma((10,)), dma((3,)), dma((3,)), dma((6,)), dma((6,)),
            dma((6,)), dma((6,)), dma((3,)), dma((3,)), dma((3,)), dma((3,)),
            dma((INNER + n * nt // INNER,)), dma((INNER + n * nt // INNER,)),
        ],
        compiler_params=pltpu.CompilerParams(
            collective_id=0, has_side_effects=True, vmem_limit_bytes=42 * 1024 * 1024
        ),
        cost_estimate=pl.CostEstimate(flops=40 * 10**9, bytes_accessed=10**7, transcendentals=0),
    )(*inputs)
    fv, dv, v1, v2, pu, wd, wrd, pm, sc = results
    outs = (state, reports, state, state, reports, state)
    ms, rs, xs, mr, rr, xr = pl.pallas_call(
        finish_kernel,
        out_shape=outs,
        in_specs=[vmem] * 9,
        out_specs=(pl.BlockSpec(memory_space=pl.ANY),) * 6,
        scratch_shapes=[V(x.shape, x.dtype) for x in outs] + [dma((22,))],
        compiler_params=pltpu.CompilerParams(vmem_limit_bytes=16 * 1024 * 1024),
    )(sc, fv, dv, v1, v2, pu, wd, wrd, pm)
    shape = forcing_state.shape[1:]
    ms, xs, mr, xr = (from_rows(x, shape)[None] for x in (ms, xs, mr, xr))
    return ms, rs[None], xs, mr, rr[None], xr


def solution(mesh):
    grid = P("tm", None, None, None, "col")
    reports = P("tm", "col", None)
    in_specs = (
        grid, grid, grid, P(), P(), reports, reports, P("tm", "col"), P("tm", "col"), reports,
    )
    out_specs = (grid, reports, grid, grid, reports, grid)
    run = functools.partial(body, mesh.shape["col"], mesh.shape["tm"])
    return jax.shard_map(run, mesh=mesh, in_specs=in_specs, out_specs=out_specs, check_vma=False)
```
